32 devices in a mesh: gx: 4 (over z), gy: 8 (over y, x, core).
Axes of the slice: x: 2, y: 2, z: 4, core: 2. Of those that a mesh axis runs over, the one named last changes fastest.
Arguments:
- source: float32 [32, 64, 512], P('gx', 'gy'), may hold values from -60 to 60
- conductivity: float32 [32, 64, 512], P('gx', 'gy'), may hold values from 0.5 to 5
- robin_flags: int32 [4, 8, 64], P('gx', 'gy'), may hold values from 0 to 63
- htc_class: int32 [4, 8, 64], P('gx', 'gy'), may hold values from 0 to 3
- htc_table: float32 [4], replicated, may hold values from 0.5 to 8
Outputs:
- adjoint: float32 [32, 64, 512], P('gx', 'gy')
- residual: float32 [32, 64, 512], P('gx', 'gy')
The draws below stay inside these ranges and needn't reach their ends.
Inputs may be any that keep to these rules, and one draw needn't show every extreme that they name: `robin_flags`: bit f (value 2^f) flags face f of the element, in the order x-min, x-max, y-min, y-max, z-min, z-max.
All inputs are finite; a program needn't handle non-finite values.
Results may differ from the reference program's by a relative error of at most 0.0003.
Values sent between devices are 32-bit elements; how exact they have to be, the bound alone decides.
No kernel may reach another device: no remote copies, remote signals or barrier semaphores. Data moves between devices by JAX's collectives and lax.ppermute only.
A program may use at most 64 MiB of HBM per device.

```python
import math
import jax
import jax.numpy as jnp
import numpy as np
from jax import lax

CLASSES = 4
ITERS = 3
EZ = 64
NEX = 4
NEY = 8


def draw_source(key, part):
    shape_all = (8 * NEX, 8 * NEY, 8 * EZ)
    noise = jax.random.normal(jax.random.fold_in(key, 11), shape_all, jnp.float32)
    rough_part = 10.0 * noise
    return jnp.clip(rough_part, -60.0, 60.0)


def plant(values, stream_key, smallest, high):
    dims = values.shape
    index_at = [jax.random.randint(jax.random.fold_in(stream_key, axis), (), 0, dims[axis]) for axis in range(len(dims))]
    values = values.at[tuple(index_at)].set(smallest)
    longest = dims.index(max(dims))
    index_at[longest] = (index_at[longest] + 1) % dims[longest]
    return values.at[tuple(index_at)].set(high)


def level_of(stream_key, dims, split, least, top_value):
    def one(dim, shards_of):
        steps = jax.random.uniform(jax.random.fold_in(jax.random.fold_in(stream_key, 6), dim), (shards_of,), jnp.float32, least / len(split), top_value / len(split))
        return jnp.repeat(jnp.exp(steps), dims[dim] // shards_of).reshape((-1,) + (1,) * (len(dims) - dim - 1))

    factor_of = one(*split[0])
    for cut in split[1:]:
        factor_of = factor_of * one(*cut)
    return factor_of


def setup_inputs(seed: int = 0) -> dict:
    key_of = jax.random.split(jax.random.key(seed), 6)
    source = draw_source(jax.random.fold_in(key_of[5], 71), 0)
    conductivity = jnp.clip(jnp.exp(math.log(5.0) - 2.3025851 * jax.random.uniform(key_of[1], (8 * NEX, 8 * NEY, 8 * EZ), jnp.float32) ** level_of(key_of[1], (8 * NEX, 8 * NEY, 8 * EZ), ((0, 4), (1, 8)), -0.2, 0.2)), 0.5, 5.0)
    robin_flags = plant(jax.random.randint(key_of[2], (NEX, NEY, EZ), 0, 64), jax.random.fold_in(key_of[2], 1), 0, 63).astype(jnp.int32)
    htc_class = plant(jax.random.randint(key_of[3], (NEX, NEY, EZ), 0, CLASSES), jax.random.fold_in(key_of[3], 1), 0, CLASSES - 1).astype(jnp.int32)
    htc_table = jnp.clip(jnp.exp(jax.random.uniform(key_of[4], (CLASSES,), jnp.float32, math.log(0.5), math.log(8.0))), 0.5, 8.0)
    return dict(source=source, conductivity=conductivity, robin_flags=robin_flags, htc_class=htc_class, htc_table=htc_table)


gll_points = (-1.0, -0.8717401485096066, -0.5917001814331423, -0.2092992179024789, 0.2092992179024789, 0.5917001814331423, 0.8717401485096066, 1.0)
gll_weights = (0.03571428571428571, 0.21070422714350603, 0.3411226924835044, 0.4124587946587038, 0.4124587946587038, 0.3411226924835044, 0.21070422714350603, 0.03571428571428571)
mass_coef = 0.2
scan_speed = 2.0
highest = lax.Precision.HIGHEST


def lagrange_derivative():
    points = np.array(gll_points)
    barycentric = np.array([1.0 / np.prod([points[j] - points[m] for m in range(8) if m != j]) for j in range(8)])
    derivative = np.zeros((8, 8))
    for a in range(8):
        for b in range(8):
            if a != b:
                derivative[a, b] = barycentric[b] / barycentric[a] / (points[a] - points[b])
        derivative[a, a] = -np.sum(derivative[a])
    return jnp.asarray(derivative, jnp.float32)


def edge_weights(elements):
    return jnp.tile(jnp.asarray(np.array(gll_weights), jnp.float32), elements)


def copies_along(elements, first_element, total_elements):
    node_index = jnp.arange(8 * elements) % 8
    element_index = first_element + jnp.arange(8 * elements) // 8
    shared = ((node_index == 7) & (element_index < total_elements - 1)) | ((node_index == 0) & (element_index > 0))
    return jnp.where(shared, 2.0, 1.0).astype(jnp.float32)


def fold_inside(values, which_axis):
    moved_field = jnp.moveaxis(values, which_axis, 0)
    extent = moved_field.shape
    blocks = moved_field.reshape((extent[0] // 8, 8) + extent[1:])
    shared = blocks[:-1, 7] + blocks[1:, 0]
    blocks = blocks.at[:-1, 7].set(shared).at[1:, 0].set(shared)
    return jnp.moveaxis(blocks.reshape(extent), 0, which_axis)


def assemble(values):
    return fold_inside(fold_inside(fold_inside(values, 0), 1), 2)


def slab_operator(pieces, derivative, weight_y, weight_z):
    values, conduct_slab, robin_slab = pieces
    weight_x = edge_weights(1)
    weights = weight_x[:, None, None] * weight_y[None, :, None] * weight_z[None, None, :]
    size_y = values.shape[1]
    size_z = values.shape[2]
    grad_x = jnp.einsum("ij,jbc->ibc", derivative, values, precision=highest)
    grad_y = jnp.einsum("ij,anjc->anic", derivative, values.reshape(8, size_y // 8, 8, size_z), precision=highest).reshape(values.shape)
    grad_z = jnp.einsum("abkj,ij->abki", values.reshape(8, size_y, size_z // 8, 8), derivative, precision=highest).reshape(values.shape)
    flux_x = weights * (conduct_slab * grad_x - scan_speed * values)
    flux_y = weights * conduct_slab * grad_y
    flux_z = weights * conduct_slab * grad_z
    back_x = jnp.einsum("ij,ibc->jbc", derivative, flux_x, precision=highest)
    back_y = jnp.einsum("ij,anic->anjc", derivative, flux_y.reshape(8, size_y // 8, 8, size_z), precision=highest).reshape(values.shape)
    back_z = jnp.einsum("abki,ij->abkj", flux_z.reshape(8, size_y, size_z // 8, 8), derivative, precision=highest).reshape(values.shape)
    return mass_coef * weights * values + robin_slab * values + back_x + back_y + back_z


def reference_robin(robin_flags, htc_class, htc_table):
    class_hits = (htc_class[..., None] == jnp.arange(CLASSES)).astype(jnp.float32)
    coefficient = jnp.sum(class_hits * htc_table, axis=-1)
    index_x = jnp.arange(NEX)[:, None, None]
    index_y = jnp.arange(NEY)[None, :, None]
    index_z = jnp.arange(EZ)[None, None, :]
    boundary = [index_x == 0, index_x == NEX - 1, index_y == 0, index_y == NEY - 1, index_z == 0, index_z == EZ - 1]
    weight_x = edge_weights(NEX)
    weight_y = edge_weights(NEY)
    weight_z = edge_weights(EZ)
    node_x = (jnp.arange(8 * NEX) % 8)[:, None, None]
    node_y = (jnp.arange(8 * NEY) % 8)[None, :, None]
    node_z = (jnp.arange(8 * EZ) % 8)[None, None, :]
    cross_x = weight_y[None, :, None] * weight_z[None, None, :]
    cross_y = weight_x[:, None, None] * weight_z[None, None, :]
    cross_z = weight_x[:, None, None] * weight_y[None, :, None]
    patterns = [(node_x == 0) * cross_x, (node_x == 7) * cross_x, (node_y == 0) * cross_y, (node_y == 7) * cross_y, (node_z == 0) * cross_z, (node_z == 7) * cross_z]
    robin_sum = jnp.zeros((8 * NEX, 8 * NEY, 8 * EZ), jnp.float32)
    for face_bit in range(6):
        flag_bit = ((robin_flags // (1 << face_bit)) % 2).astype(jnp.float32)
        coef_face = coefficient * flag_bit * boundary[face_bit].astype(jnp.float32)
        spread = jnp.repeat(jnp.repeat(jnp.repeat(coef_face, 8, axis=0), 8, axis=1), 8, axis=2)
        robin_sum = robin_sum + spread * patterns[face_bit].astype(jnp.float32)
    return robin_sum


def reference(source, conductivity, robin_flags, htc_class, htc_table):
    derivative = lagrange_derivative()
    weight_x = edge_weights(NEX)
    weight_y = edge_weights(NEY)
    weight_z = edge_weights(EZ)
    copies_x = copies_along(NEX, 0, NEX)
    copies_y = copies_along(NEY, 0, NEY)
    copies_z = copies_along(EZ, 0, EZ)
    inv_copies = 1.0 / (copies_x[:, None, None] * copies_y[None, :, None] * copies_z[None, None, :])
    robin_diag = reference_robin(robin_flags, htc_class, htc_table)
    slab_shape = (NEX, 8, 8 * NEY, 8 * EZ)

    def operate(values):
        stacked = (values.reshape(slab_shape), conductivity.reshape(slab_shape), robin_diag.reshape(slab_shape))
        local_terms = lax.map(lambda pieces: slab_operator(pieces, derivative, weight_y, weight_z), stacked)
        return assemble(local_terms.reshape(values.shape))

    def inner(left, right):
        return jnp.sum(left * right * inv_copies)

    weights = weight_x[:, None, None] * weight_y[None, :, None] * weight_z[None, None, :]
    assembled = assemble(weights * source)
    adjoint = jnp.zeros_like(assembled)
    residual = assembled
    direction = assembled
    rho_now = inner(assembled, assembled)
    for iteration in range(ITERS):
        applied = operate(direction)
        alpha_step = rho_now / inner(assembled, applied)
        half_resid = residual - alpha_step * applied
        applied_half = operate(half_resid)
        omega_step = inner(applied_half, half_resid) / inner(applied_half, applied_half)
        adjoint = adjoint + alpha_step * direction + omega_step * half_resid
        residual = half_resid - omega_step * applied_half
        rho_next = inner(assembled, residual)
        beta_step = (rho_next / rho_now) * (alpha_step / omega_step)
        direction = residual + beta_step * (direction - omega_step * applied)
        rho_now = rho_next
    return adjoint, residual
```

```python
import functools

import jax
import jax.numpy as jnp
import numpy as np
from jax import lax
from jax.experimental import pallas as pl
from jax.experimental.pallas import tpu as pltpu
from jax.sharding import PartitionSpec as P

ITERS = 3
N = 8

gll_points = (
    -1.0,
    -0.8717401485096066,
    -0.5917001814331423,
    -0.2092992179024789,
    0.2092992179024789,
    0.5917001814331423,
    0.8717401485096066,
    1.0,
)
gll_weights = (
    0.03571428571428571,
    0.21070422714350603,
    0.3411226924835044,
    0.4124587946587038,
    0.4124587946587038,
    0.3411226924835044,
    0.21070422714350603,
    0.03571428571428571,
)
mass_coef = 0.2
scan_speed = 2.0
f32 = jnp.float32
VMEM = pl.BlockSpec(memory_space=pltpu.VMEM)
SMEM = pl.BlockSpec(memory_space=pltpu.SMEM)
dot = functools.partial(jnp.dot, precision=lax.Precision.HIGHEST, preferred_element_type=f32)


def lagrange_derivative():
    points = np.array(gll_points)
    barycentric = np.array(
        [1.0 / np.prod([points[j] - points[m] for m in range(N) if m != j]) for j in range(N)]
    )
    derivative = np.zeros((N, N))
    for a in range(N):
        for b in range(N):
            if a != b:
                derivative[a, b] = barycentric[b] / barycentric[a] / (points[a] - points[b])
        derivative[a, a] = -np.sum(derivative[a])
    return derivative.astype(np.float32)


def constants(elems_z):
    d = lagrange_derivative()
    w = np.array(gll_weights).astype(np.float32)
    eye = np.eye(N, dtype=np.float32)
    ends = d.T[[0, N - 1]]
    zero = np.zeros((2 * N, N * N), np.float32)
    forward = np.concatenate([np.kron(d, eye), np.kron(eye, d)], 0)
    y_ends = np.concatenate([np.kron(eye, ends[:1]), np.kron(eye, ends[1:])], 0)
    back = np.concatenate(
        [
            np.concatenate([np.kron(d.T, eye), np.kron(eye, d.T)], 1),
            np.concatenate([np.kron(ends, eye), zero], 1),
            np.concatenate([zero, y_ends], 1),
        ],
        0,
    )
    group = min(elems_z, 32)
    z_back = np.kron(np.eye(group, dtype=np.float32), d)
    z_forward = np.ascontiguousarray(z_back.T)
    lane = np.arange(N * elems_z)
    low = (lane % N == 0) & (lane > 0)
    high = (lane % N == N - 1) & (lane < N * elems_z - 1)
    w_z = np.tile(w, elems_z)
    lanes = np.stack([low, high, w_z, 1.0 + low + high] + [0 * lane] * 4).astype(np.float32)
    weights = (w[:, None, None] * w[None, :, None] * w_z).reshape(N * N, N * elems_z)
    w_a = np.repeat(w, N)
    w_b = np.tile(w, N)
    a = np.arange(N * N) // N
    b = np.arange(N * N) % N
    one = np.ones(N * N)
    faces = np.stack(
        [(a == 0) * w_b, (a == 7) * w_b, (b == 0) * w_a, (b == 7) * w_a, w_a * w_b, w_a * w_b, 0 * one, 0 * one],
        1,
    ).astype(np.float32)
    spread = np.kron(np.eye(elems_z), np.ones((1, N))).astype(np.float32)
    return dict(
        forward=forward,
        back=back.astype(np.float32),
        z_forward=z_forward,
        z_back=z_back,
        lanes=lanes,
        weights=weights.astype(np.float32),
        faces=faces,
        spread=spread,
    )


def fold_z(v, lanes_ref):
    size = v.shape[1]
    return (
        v
        + pltpu.roll(v, 1, axis=1) * lanes_ref[0:1, :]
        + pltpu.roll(v, size - 1, axis=1) * lanes_ref[1:2, :]
    )


def y_rows(ref, b):
    return jnp.concatenate([ref[N * a + b : N * a + b + 1, :] for a in range(N)], 0)


def add_y_rows(out, b, values):
    for a in range(N):
        out[N * a + b : N * a + b + 1, :] += values[a : a + 1]


def pick(pos_ref, axis, even, odd):
    return jnp.where(pos_ref[axis] % 2 == 0, even, odd)


def send(pos_ref, axis, low, high, even_ref, odd_ref):
    even_ref[...] = pick(pos_ref, axis, high, low)
    odd_ref[...] = pick(pos_ref, axis, low, high)


def received(pos_ref, axis, count, even, odd):
    low = jnp.where(pos_ref[axis] > 0, pick(pos_ref, axis, odd, even), 0.0)
    high = jnp.where(pos_ref[axis] < count - 1, pick(pos_ref, axis, even, odd), 0.0)
    return low, high


def field_kernel(sizes, pos, table, source, k, flags, classes, weights, faces, lanes, spread,
                 ws_out, wk_out, robin_out, even_out, odd_out):
    elems_z = flags.shape[1]
    ws_out[...] = weights[...] * source[...]
    wk_out[...] = weights[...] * k[...]
    coefficient = jnp.zeros(flags.shape, f32)
    for c in range(table.shape[0]):
        coefficient = jnp.where(classes[...] == c, table[c], coefficient)
    element = lax.broadcasted_iota(jnp.int32, flags.shape, 1)
    sides = [
        pos[0] == 0, pos[0] == sizes[0] - 1, pos[1] == 0, pos[1] == sizes[1] - 1,
        element == 0, element == elems_z - 1,
    ]
    rows = []
    for bit, side in enumerate(sides):
        flagged = (flags[...] >> bit) % 2 == 1
        rows.append(jnp.where(flagged & side, coefficient, 0.0))
    rows += [jnp.zeros(flags.shape, f32)] * 2
    wide = dot(jnp.concatenate(rows, 0), spread[...])
    row = lax.broadcasted_iota(jnp.int32, wide.shape, 0)
    lane = lax.broadcasted_iota(jnp.int32, wide.shape, 1) % N
    along = jnp.where(
        row < 4,
        lanes[2:3, :],
        jnp.where(row == 4, jnp.where(lane == 0, 1.0, 0.0), jnp.where(lane == N - 1, 1.0, 0.0)),
    )
    robin_out[...] = dot(faces[...], wide * along)
    low = jnp.concatenate([y_rows(r, 0) for r in (ws_out, wk_out, robin_out)], 0)
    high = jnp.concatenate([y_rows(r, N - 1) for r in (ws_out, wk_out, robin_out)], 0)
    send(pos, 1, low, high, even_out, odd_out)


def fold_y_kernel(sizes, pos, ws, wk, robin, even, odd, ws_out, wk_out, robin_out, even_out, odd_out):
    low, high = received(pos, 1, sizes[1], even[...], odd[...])
    for i, (field, out) in enumerate(((ws, ws_out), (wk, wk_out), (robin, robin_out))):
        out[...] = field[...]
        add_y_rows(out, 0, low[N * i : N * i + N])
        add_y_rows(out, N - 1, high[N * i : N * i + N])
    fields = (ws_out, wk_out, robin_out, wk)
    last = N * (N - 1)
    send(
        pos, 0,
        jnp.concatenate([r[0:N, :] for r in fields], 0),
        jnp.concatenate([r[last : last + N, :] for r in fields], 0),
        even_out, odd_out,
    )


def copies(sizes, pos, lanes, shape):
    row = lax.broadcasted_iota(jnp.int32, (shape[0], 1), 0)
    a, b = row // N, row % N
    shared_x = ((a == 0) & (pos[0] > 0)) | ((a == N - 1) & (pos[0] < sizes[0] - 1))
    shared_y = ((b == 0) & (pos[1] > 0)) | ((b == N - 1) & (pos[1] < sizes[1] - 1))
    return jnp.where(shared_x, 2.0, 1.0), jnp.where(shared_y, 2.0, 1.0), lanes[3:4, :]


def operate(pos, v, coefs, mats, q_out, sends):
    kx, ky, kz, advect, diagonal = coefs
    forward, back, z_forward, z_back, lanes = mats
    rows, size = v.shape
    group = z_forward.shape[0]
    grad = dot(forward[...], v)
    tiles = [v[:, i : i + group] for i in range(0, size, group)]
    grad_z = dot(jnp.concatenate(tiles, 0), z_forward[...])
    flux_x = kx[...] * grad[:rows] - advect[...] * v
    flux_y = ky[...] * grad[rows:]
    flux = jnp.concatenate([flux_x, flux_y], 0)
    both = dot(back[...], flux)
    send(pos, 0, both[rows : rows + N], both[rows + N : rows + 2 * N], sends[0], sends[1])
    send(pos, 1, both[rows + 2 * N : rows + 3 * N], both[rows + 3 * N :], sends[2], sends[3])
    flux_z = [
        kz[:, i * group : (i + 1) * group] * grad_z[i * rows : (i + 1) * rows]
        for i in range(len(tiles))
    ]
    back_z = dot(jnp.concatenate(flux_z, 0), z_back[...])
    back_z = jnp.concatenate([back_z[i * rows : (i + 1) * rows] for i in range(len(tiles))], 1)
    q_out[...] = both[:rows] + fold_z(back_z, lanes) + diagonal[...] * v


def assemble(sizes, pos, q, recv, out):
    x_even, x_odd, y_even, y_odd = recv
    last = N * (N - 1)
    x_low, x_high = received(pos, 0, sizes[0], x_even[...], x_odd[...])
    y_low, y_high = received(pos, 1, sizes[1], y_even[...], y_odd[...])
    out[...] = q[...]
    out[0:N, :] += x_low
    out[last : last + N, :] += x_high
    add_y_rows(out, 0, y_low)
    add_y_rows(out, N - 1, y_high)


def first_kernel(sizes, pos, ws, wk_y, robin, wk, even, odd, weights, *refs):
    mats, outs = refs[:5], refs[5:]
    b, kx, ky, kz, advect, diagonal, inverse, q = outs[:8]
    sends = outs[8:12]
    lanes = mats[4]
    last = N * (N - 1)
    low, high = received(pos, 0, sizes[0], even[...], odd[...])
    for i, (field, out) in enumerate(((ws, b), (wk_y, kz), (robin, diagonal), (wk, ky))):
        out[...] = field[...]
        out[0:N, :] += low[N * i : N * i + N]
        out[last : last + N, :] += high[N * i : N * i + N]
    copies_x, copies_y, copies_z = copies(sizes, pos, lanes, ws.shape)
    b[...] = fold_z(b[...], lanes)
    kx[...] = fold_z(wk_y[...], lanes)
    ky[...] = fold_z(ky[...], lanes)
    weights_yz = weights[...] * (copies_y * copies_z)
    advect[...] = scan_speed * weights_yz
    diagonal[...] = fold_z(diagonal[...], lanes) + mass_coef * (weights_yz * copies_x)
    inverse[...] = 1.0 / (copies_x * copies_y * copies_z)
    operate(pos, b[...], (kx, ky, kz, advect, diagonal), mats, q, sends)


def dots_row(pairs, inverse, out):
    lane = lax.broadcasted_iota(jnp.int32, (1, out.shape[-1]), 1)
    row = jnp.zeros(lane.shape, f32)
    scaled = {}
    for i, (u, v) in enumerate(pairs):
        if id(u) not in scaled:
            scaled[id(u)] = u * inverse
        product = scaled[id(u)] * v
        total = jnp.sum(jnp.sum(product, axis=0, keepdims=True), axis=1, keepdims=True)
        row = jnp.where(lane == i, total, row)
    for i in range(out.shape[0]):
        out[i] = row


def totals(gathered, count):
    row = jnp.sum(gathered[...], axis=0)
    lane = lax.broadcasted_iota(jnp.int32, row.shape, 1)
    return [jnp.sum(jnp.where(lane == i, row, 0.0), axis=1, keepdims=True) for i in range(count)]


def apply_kernel(sizes, pos, q, *refs):
    recv, coefs, mats, outs = refs[:4], refs[4:9], refs[9:14], refs[14:]
    v, q_next = outs[:2]
    assemble(sizes, pos, q, recv, v)
    operate(pos, v[...], coefs, mats, q_next, outs[2:6])


def inner_pairs(b, r, s, w, z):
    return [(b, r), (b, s), (b, w), (b, z), (w, r), (w, s), (r, z), (s, z), (w, w), (w, z), (z, z)]


def steps(g):
    br, bs, bw, bz, wr, ws, rz, sz, ww, wz, zz = g
    alpha = br / bs
    omega = (wr - alpha * (ws + rz) + alpha * alpha * sz) / (
        ww - 2.0 * alpha * wz + alpha * alpha * zz
    )
    rho_next = (br - alpha * bs) - omega * (bw - alpha * bz)
    beta = rho_next / br * (alpha / omega)
    return alpha, omega, beta


def first_dots_kernel(sizes, pos, b, s, inverse, q, *refs):
    recv, coefs, mats, outs = refs[:4], refs[4:9], refs[9:14], refs[14:]
    z, row, q_next = outs[:3]
    assemble(sizes, pos, q, recv, z)
    b_, s_, z_ = b[...], s[...], z[...]
    dots_row([(b_, b_), (b_, s_), (b_, z_), (s_, s_), (s_, z_), (z_, z_)], inverse[...], row)
    operate(pos, z_, coefs, mats, q_next, outs[3:7])


def update(alpha, omega, r, s, w, z, aw, az):
    half = r - alpha * s
    applied_half = w - alpha * z
    w_next = applied_half - omega * (aw - alpha * az)
    return half, applied_half, w_next


def update_kernel(sizes, first, pos, gathered, q, *refs):
    recv, refs = refs[:4], refs[4:]
    if first:
        b, s, z = refs[:3]
        refs = refs[3:]
        bb, bs, bz, ss, sz, zz = totals(gathered, 6)
        g = (bb, bs, bs, bz, bs, ss, bz, sz, ss, sz, zz)
        r, p, w, aw, x = b, b, s, z, None
    else:
        r, p, s, w, z, aw, x = refs[:7]
        refs = refs[7:]
        g = totals(gathered, 11)
    coefs, mats, outs = refs[:5], refs[5:10], refs[10:]
    x_out, r_out, p_out, s_out, w_out, zpart_out, q_next = outs[:7]
    alpha, omega, beta = steps(g)
    assemble(sizes, pos, q, recv, zpart_out)
    az = zpart_out[...]
    half, applied_half, w_next = update(alpha, omega, r[...], s[...], w[...], z[...], aw[...], az)
    w_out[...] = w_next
    operate(pos, w_next, coefs, mats, q_next, outs[7:11])
    step = alpha * p[...] + omega * half
    x_out[...] = step if x is None else x[...] + step
    r_next = half - omega * applied_half
    r_out[...] = r_next
    p_out[...] = r_next + beta * (p[...] - omega * s[...])
    s_out[...] = w_next + beta * (s[...] - omega * z[...])
    zpart_out[...] = beta * (z[...] - omega * az)


def dots_kernel(sizes, last, pos, b, r, s, w, zpart, inverse, q, *refs):
    recv, refs = refs[:4], refs[4:]
    if last:
        aw, z, row = refs
    else:
        coefs, mats, outs = refs[:5], refs[5:10], refs[10:]
        aw, z, row, q_next = outs[:4]
    assemble(sizes, pos, q, recv, aw)
    z[...] = aw[...] + zpart[...]
    pairs = inner_pairs(b[...], r[...], s[...], w[...], z[...])
    dots_row(pairs, inverse[...], row)
    if not last:
        operate(pos, z[...], coefs, mats, q_next, outs[4:8])


def last_kernel(sizes, gathered, r, p, s, w, z, x, x_out, r_out):
    alpha, omega, _ = steps(totals(gathered, 11))
    half = r[...] - alpha * s[...]
    x_out[...] = x[...] + alpha * p[...] + omega * half
    r_out[...] = half - omega * (w[...] - alpha * z[...])


def pairings(count):
    even = [(i, i ^ 1) for i in range(count)]
    odd = [(i, (i - 1 if i % 2 == 0 else i + 1) % count) for i in range(count)]
    return even, odd


def per_device(sizes, source, conductivity, robin_flags, htc_class, htc_table):
    shape = source.shape
    elems_z = robin_flags.shape[2]
    rows, size = shape[0] * shape[1], shape[2]
    assert robin_flags.shape[:2] == (1, 1) and sizes[0] % 2 == 0 and sizes[1] % 2 == 0
    devices = sizes[0] * sizes[1]
    pos = jnp.stack([lax.axis_index("gx"), lax.axis_index("gy")]).astype(jnp.int32)
    c = {name: jnp.asarray(value) for name, value in constants(elems_z).items()}
    mats = [c[name] for name in ("forward", "back", "z_forward", "z_back", "lanes")]
    x_pairs, y_pairs = pairings(sizes[0]), pairings(sizes[1])

    def struct(n=rows):
        return jax.ShapeDtypeStruct((n, size), f32)

    field = struct()
    faces = [struct(N)] * 4
    row = jax.ShapeDtypeStruct((devices, 1, 128), f32)

    def call(kernel, outs, smem, *operands):
        specs = [SMEM] * smem + [VMEM] * (len(operands) - smem)
        return pl.pallas_call(
            kernel,
            out_shape=outs,
            in_specs=specs,
            out_specs=[VMEM] * len(outs),
            compiler_params=pltpu.CompilerParams(vmem_limit_bytes=32 * 1024 * 1024),
        )(*operands)

    def exchange(axis, pairs, even, odd):
        return lax.ppermute(even, axis, pairs[0]), lax.ppermute(odd, axis, pairs[1])

    def swap(parts):
        return exchange("gx", x_pairs, *parts[:2]) + exchange("gy", y_pairs, *parts[2:])

    def spread(values):
        return lax.all_to_all(values, ("gx", "gy"), 0, 0)

    flat = lambda v: v.reshape(rows, size)
    ws, wk, robin, *parts = call(
        functools.partial(field_kernel, sizes),
        [field] * 3 + [struct(3 * N)] * 2,
        2,
        pos, htc_table, flat(source), flat(conductivity),
        robin_flags.reshape(1, elems_z), htc_class.reshape(1, elems_z),
        c["weights"], c["faces"], c["lanes"], c["spread"],
    )
    parts = exchange("gy", y_pairs, *parts)
    ws, wk_y, robin, *parts = call(
        functools.partial(fold_y_kernel, sizes),
        [field] * 3 + [struct(4 * N)] * 2,
        1,
        pos, ws, wk, robin, *parts,
    )
    parts = exchange("gx", x_pairs, *parts)
    b, *coefs, inverse, q, s0, s1, s2, s3 = call(
        functools.partial(first_kernel, sizes),
        [field] * 8 + faces,
        1,
        pos, ws, wk_y, robin, wk, *parts, c["weights"], *mats,
    )
    recv = swap((s0, s1, s2, s3))
    s, q, *parts = call(
        functools.partial(apply_kernel, sizes), [field] * 2 + faces, 1,
        pos, q, *recv, *coefs, *mats,
    )
    recv = swap(parts)
    z, products, q, *parts = call(
        functools.partial(first_dots_kernel, sizes), [field, row, field] + faces, 1,
        pos, b, s, inverse, q, *recv, *coefs, *mats,
    )
    state = (b, s, z)
    for iteration in range(ITERS - 1):
        recv = swap(parts)
        gathered = spread(products)
        x, r, p, s, w, zpart, q, *parts = call(
            functools.partial(update_kernel, sizes, iteration == 0),
            [field] * 7 + faces,
            1,
            pos, gathered, q, *recv, *state, *coefs, *mats,
        )
        recv = swap(parts)
        last = iteration == ITERS - 2
        aw, z, products, *rest = call(
            functools.partial(dots_kernel, sizes, last),
            [field] * 2 + [row] + ([] if last else [field] + faces),
            1,
            pos, b, r, s, w, zpart, inverse, q, *recv, *(() if last else (*coefs, *mats)),
        )
        if not last:
            q, *parts = rest
            state = (r, p, s, w, z, aw, x)
    gathered = spread(products)
    x, r = call(functools.partial(last_kernel, sizes), [field] * 2, 0, gathered, r, p, s, w, z, x)
    return x.reshape(shape), r.reshape(shape)


def solution(mesh):
    sizes = (mesh.shape["gx"], mesh.shape["gy"])
    field = P("gx", "gy", None)
    return jax.shard_map(
        functools.partial(per_device, sizes),
        mesh=mesh,
        in_specs=(field, field, field, field, P()),
        out_specs=(field, field),
        check_vma=False,
    )
```

```python
import functools

import jax
import jax.numpy as jnp
import numpy as np
from jax import lax
from jax.experimental import pallas as pl
from jax.experimental.pallas import tpu as pltpu
from jax.sharding import PartitionSpec as P

ITERS = 3
N = 8

gll_points = (
    -1.0,
    -0.8717401485096066,
    -0.5917001814331423,
    -0.2092992179024789,
    0.2092992179024789,
    0.5917001814331423,
    0.8717401485096066,
    1.0,
)
gll_weights = (
    0.03571428571428571,
    0.21070422714350603,
    0.3411226924835044,
    0.4124587946587038,
    0.4124587946587038,
    0.3411226924835044,
    0.21070422714350603,
    0.03571428571428571,
)
mass_coef = 0.2
scan_speed = 2.0
f32 = jnp.float32
VMEM = pl.BlockSpec(memory_space=pltpu.VMEM)
SMEM = pl.BlockSpec(memory_space=pltpu.SMEM)
dot = functools.partial(jnp.dot, precision=lax.Precision.HIGHEST, preferred_element_type=f32)


def lagrange_derivative():
    points = np.array(gll_points)
    barycentric = np.array(
        [1.0 / np.prod([points[j] - points[m] for m in range(N) if m != j]) for j in range(N)]
    )
    derivative = np.zeros((N, N))
    for a in range(N):
        for b in range(N):
            if a != b:
                derivative[a, b] = barycentric[b] / barycentric[a] / (points[a] - points[b])
        derivative[a, a] = -np.sum(derivative[a])
    return derivative.astype(np.float32)


def constants(elems_z):
    d = lagrange_derivative()
    w = np.array(gll_weights).astype(np.float32)
    eye = np.eye(N, dtype=np.float32)
    ends = d.T[[0, N - 1]]
    zero = np.zeros((2 * N, N * N), np.float32)
    forward = np.concatenate([np.kron(d, eye), np.kron(eye, d)], 0)
    y_ends = np.concatenate([np.kron(eye, ends[:1]), np.kron(eye, ends[1:])], 0)
    back = np.concatenate(
        [
            np.concatenate([np.kron(d.T, eye), np.kron(eye, d.T)], 1),
            np.concatenate([np.kron(ends, eye), zero], 1),
            np.concatenate([zero, y_ends], 1),
        ],
        0,
    )
    group = min(elems_z, 32)
    z_back = np.kron(np.eye(group, dtype=np.float32), d)
    z_forward = np.ascontiguousarray(z_back.T)
    lane = np.arange(N * elems_z)
    low = (lane % N == 0) & (lane > 0)
    high = (lane % N == N - 1) & (lane < N * elems_z - 1)
    w_z = np.tile(w, elems_z)
    lanes = np.stack([low, high, w_z, 1.0 + low + high] + [0 * lane] * 4).astype(np.float32)
    weights = (w[:, None, None] * w[None, :, None] * w_z).reshape(N * N, N * elems_z)
    w_a = np.repeat(w, N)
    w_b = np.tile(w, N)
    a = np.arange(N * N) // N
    b = np.arange(N * N) % N
    one = np.ones(N * N)
    faces = np.stack(
        [(a == 0) * w_b, (a == 7) * w_b, (b == 0) * w_a, (b == 7) * w_a, w_a * w_b, w_a * w_b, 0 * one, 0 * one],
        1,
    ).astype(np.float32)
    spread = np.kron(np.eye(elems_z), np.ones((1, N))).astype(np.float32)
    return dict(
        forward=forward,
        back=back.astype(np.float32),
        z_forward=z_forward,
        z_back=z_back,
        lanes=lanes,
        weights=weights.astype(np.float32),
        faces=faces,
        spread=spread,
    )


def fold_z(v, lanes_ref):
    size = v.shape[1]
    return (
        v
        + pltpu.roll(v, 1, axis=1) * lanes_ref[0:1, :]
        + pltpu.roll(v, size - 1, axis=1) * lanes_ref[1:2, :]
    )


def y_rows(ref, b):
    return jnp.concatenate([ref[N * a + b : N * a + b + 1, :] for a in range(N)], 0)


def add_y_rows(out, b, values):
    for a in range(N):
        out[N * a + b : N * a + b + 1, :] += values[a : a + 1]


def pick(pos_ref, axis, even, odd):
    return jnp.where(pos_ref[axis] % 2 == 0, even, odd)


def send(pos_ref, axis, low, high, even_ref, odd_ref):
    even_ref[...] = pick(pos_ref, axis, high, low)
    odd_ref[...] = pick(pos_ref, axis, low, high)


def received(pos_ref, axis, count, even, odd):
    low = jnp.where(pos_ref[axis] > 0, pick(pos_ref, axis, odd, even), 0.0)
    high = jnp.where(pos_ref[axis] < count - 1, pick(pos_ref, axis, even, odd), 0.0)
    return low, high


def field_kernel(sizes, pos, table, source, k, flags, classes, weights, faces, lanes, spread,
                 ws_out, wk_out, robin_out, even_out, odd_out):
    elems_z = flags.shape[1]
    ws_out[...] = weights[...] * source[...]
    wk_out[...] = weights[...] * k[...]
    coefficient = jnp.zeros(flags.shape, f32)
    for c in range(table.shape[0]):
        coefficient = jnp.where(classes[...] == c, table[c], coefficient)
    element = lax.broadcasted_iota(jnp.int32, flags.shape, 1)
    sides = [
        pos[0] == 0, pos[0] == sizes[0] - 1, pos[1] == 0, pos[1] == sizes[1] - 1,
        element == 0, element == elems_z - 1,
    ]
    rows = []
    for bit, side in enumerate(sides):
        flagged = (flags[...] >> bit) % 2 == 1
        rows.append(jnp.where(flagged & side, coefficient, 0.0))
    rows += [jnp.zeros(flags.shape, f32)] * 2
    wide = dot(jnp.concatenate(rows, 0), spread[...])
    row = lax.broadcasted_iota(jnp.int32, wide.shape, 0)
    lane = lax.broadcasted_iota(jnp.int32, wide.shape, 1) % N
    along = jnp.where(
        row < 4,
        lanes[2:3, :],
        jnp.where(row == 4, jnp.where(lane == 0, 1.0, 0.0), jnp.where(lane == N - 1, 1.0, 0.0)),
    )
    robin_out[...] = dot(faces[...], wide * along)
    low = jnp.concatenate([y_rows(r, 0) for r in (ws_out, wk_out, robin_out)], 0)
    high = jnp.concatenate([y_rows(r, N - 1) for r in (ws_out, wk_out, robin_out)], 0)
    send(pos, 1, low, high, even_out, odd_out)


def fold_y_kernel(sizes, pos, ws, wk, robin, even, odd, ws_out, wk_out, robin_out, even_out, odd_out):
    low, high = received(pos, 1, sizes[1], even[...], odd[...])
    for i, (field, out) in enumerate(((ws, ws_out), (wk, wk_out), (robin, robin_out))):
        out[...] = field[...]
        add_y_rows(out, 0, low[N * i : N * i + N])
        add_y_rows(out, N - 1, high[N * i : N * i + N])
    fields = (ws_out, wk_out, robin_out, wk)
    last = N * (N - 1)
    send(
        pos, 0,
        jnp.concatenate([r[0:N, :] for r in fields], 0),
        jnp.concatenate([r[last : last + N, :] for r in fields], 0),
        even_out, odd_out,
    )


def copies(sizes, pos, lanes, shape):
    row = lax.broadcasted_iota(jnp.int32, (shape[0], 1), 0)
    a, b = row // N, row % N
    shared_x = ((a == 0) & (pos[0] > 0)) | ((a == N - 1) & (pos[0] < sizes[0] - 1))
    shared_y = ((b == 0) & (pos[1] > 0)) | ((b == N - 1) & (pos[1] < sizes[1] - 1))
    return jnp.where(shared_x, 2.0, 1.0), jnp.where(shared_y, 2.0, 1.0), lanes[3:4, :]


def operate(pos, v, coefs, mats, q_out, sends):
    kx, ky, kz, advect, diagonal = coefs
    forward, back, z_forward, z_back, lanes = mats
    rows, size = v.shape
    group = z_forward.shape[0]
    grad = dot(forward[...], v)
    tiles = [v[:, i : i + group] for i in range(0, size, group)]
    grad_z = dot(jnp.concatenate(tiles, 0), z_forward[...])
    flux_x = kx[...] * grad[:rows] - advect[...] * v
    flux_y = ky[...] * grad[rows:]
    flux = jnp.concatenate([flux_x, flux_y], 0)
    both = dot(back[...], flux)
    send(pos, 0, both[rows : rows + N], both[rows + N : rows + 2 * N], sends[0], sends[1])
    send(pos, 1, both[rows + 2 * N : rows + 3 * N], both[rows + 3 * N :], sends[2], sends[3])
    flux_z = [
        kz[:, i * group : (i + 1) * group] * grad_z[i * rows : (i + 1) * rows]
        for i in range(len(tiles))
    ]
    back_z = dot(jnp.concatenate(flux_z, 0), z_back[...])
    back_z = jnp.concatenate([back_z[i * rows : (i + 1) * rows] for i in range(len(tiles))], 1)
    q_out[...] = both[:rows] + fold_z(back_z, lanes) + diagonal[...] * v


def assemble(sizes, pos, q, recv, out):
    x_even, x_odd, y_even, y_odd = recv
    last = N * (N - 1)
    x_low, x_high = received(pos, 0, sizes[0], x_even[...], x_odd[...])
    y_low, y_high = received(pos, 1, sizes[1], y_even[...], y_odd[...])
    out[...] = q[...]
    out[0:N, :] += x_low
    out[last : last + N, :] += x_high
    add_y_rows(out, 0, y_low)
    add_y_rows(out, N - 1, y_high)


def first_kernel(sizes, pos, ws, wk_y, robin, wk, even, odd, weights, *refs):
    mats, outs = refs[:5], refs[5:]
    b, kx, ky, kz, advect, diagonal, inverse, q = outs[:8]
    sends = outs[8:12]
    lanes = mats[4]
    last = N * (N - 1)
    low, high = received(pos, 0, sizes[0], even[...], odd[...])
    for i, (field, out) in enumerate(((ws, b), (wk_y, kz), (robin, diagonal), (wk, ky))):
        out[...] = field[...]
        out[0:N, :] += low[N * i : N * i + N]
        out[last : last + N, :] += high[N * i : N * i + N]
    copies_x, copies_y, copies_z = copies(sizes, pos, lanes, ws.shape)
    b[...] = fold_z(b[...], lanes)
    kx[...] = fold_z(wk_y[...], lanes)
    ky[...] = fold_z(ky[...], lanes)
    weights_yz = weights[...] * (copies_y * copies_z)
    advect[...] = scan_speed * weights_yz
    diagonal[...] = fold_z(diagonal[...], lanes) + mass_coef * (weights_yz * copies_x)
    inverse[...] = 1.0 / (copies_x * copies_y * copies_z)
    operate(pos, b[...], (kx, ky, kz, advect, diagonal), mats, q, sends)


def dots_row(pairs, inverse, out):
    lane = lax.broadcasted_iota(jnp.int32, (1, out.shape[-1]), 1)
    row = jnp.zeros(lane.shape, f32)
    scaled = {}
    for i, (u, v) in enumerate(pairs):
        if id(u) not in scaled:
            scaled[id(u)] = u * inverse
        product = scaled[id(u)] * v
        total = jnp.sum(jnp.sum(product, axis=0, keepdims=True), axis=1, keepdims=True)
        row = jnp.where(lane == i, total, row)
    for i in range(out.shape[0]):
        out[i] = row


def totals(gathered, count):
    row = jnp.sum(gathered[...], axis=0)
    lane = lax.broadcasted_iota(jnp.int32, row.shape, 1)
    return [jnp.sum(jnp.where(lane == i, row, 0.0), axis=1, keepdims=True) for i in range(count)]


def apply_kernel(sizes, pos, q, *refs):
    recv, coefs, mats, outs = refs[:4], refs[4:9], refs[9:14], refs[14:]
    v, q_next = outs[:2]
    assemble(sizes, pos, q, recv, v)
    operate(pos, v[...], coefs, mats, q_next, outs[2:6])


def inner_pairs(b, r, s, w, z):
    return [(b, r), (b, s), (b, w), (b, z), (w, r), (w, s), (r, z), (s, z), (w, w), (w, z), (z, z)]


def steps(g):
    br, bs, bw, bz, wr, ws, rz, sz, ww, wz, zz = g
    alpha = br / bs
    omega = (wr - alpha * (ws + rz) + alpha * alpha * sz) / (
        ww - 2.0 * alpha * wz + alpha * alpha * zz
    )
    rho_next = (br - alpha * bs) - omega * (bw - alpha * bz)
    beta = rho_next / br * (alpha / omega)
    return alpha, omega, beta


def first_dots_kernel(sizes, pos, b, s, inverse, q, *refs):
    recv, coefs, mats, outs = refs[:4], refs[4:9], refs[9:14], refs[14:]
    z, row, q_next = outs[:3]
    assemble(sizes, pos, q, recv, z)
    b_, s_, z_ = b[...], s[...], z[...]
    dots_row([(b_, b_), (b_, s_), (b_, z_), (s_, s_), (s_, z_), (z_, z_)], inverse[...], row)
    operate(pos, z_, coefs, mats, q_next, outs[3:7])


def update(alpha, omega, r, s, w, z, aw, az):
    half = r - alpha * s
    applied_half = w - alpha * z
    w_next = applied_half - omega * (aw - alpha * az)
    return half, applied_half, w_next


def update_kernel(sizes, first, pos, gathered, q, *refs):
    recv, refs = refs[:4], refs[4:]
    if first:
        b, s, z = refs[:3]
        refs = refs[3:]
        bb, bs, bz, ss, sz, zz = totals(gathered, 6)
        g = (bb, bs, bs, bz, bs, ss, bz, sz, ss, sz, zz)
        r, p, w, aw, x = b, b, s, z, None
    else:
        r, p, s, w, z, aw, x = refs[:7]
        refs = refs[7:]
        g = totals(gathered, 11)
    coefs, mats, outs = refs[:5], refs[5:10], refs[10:]
    x_out, r_out, p_out, s_out, w_out, zpart_out, q_next = outs[:7]
    alpha, omega, beta = steps(g)
    assemble(sizes, pos, q, recv, zpart_out)
    az = zpart_out[...]
    half, applied_half, w_next = update(alpha, omega, r[...], s[...], w[...], z[...], aw[...], az)
    w_out[...] = w_next
    operate(pos, w_next, coefs, mats, q_next, outs[7:11])
    step = alpha * p[...] + omega * half
    x_out[...] = step if x is None else x[...] + step
    r_next = half - omega * applied_half
    r_out[...] = r_next
    p_out[...] = r_next + beta * (p[...] - omega * s[...])
    s_out[...] = w_next + beta * (s[...] - omega * z[...])
    zpart_out[...] = beta * (z[...] - omega * az)


def dots_kernel(sizes, last, pos, b, r, s, w, zpart, inverse, q, *refs):
    recv, refs = refs[:4], refs[4:]
    if last:
        aw, z, row = refs
    else:
        coefs, mats, outs = refs[:5], refs[5:10], refs[10:]
        aw, z, row, q_next = outs[:4]
    assemble(sizes, pos, q, recv, aw)
    z[...] = aw[...] + zpart[...]
    pairs = inner_pairs(b[...], r[...], s[...], w[...], z[...])
    dots_row(pairs, inverse[...], row)
    if not last:
        operate(pos, z[...], coefs, mats, q_next, outs[4:8])


def last_kernel(sizes, gathered, r, p, s, w, z, x, x_out, r_out):
    alpha, omega, _ = steps(totals(gathered, 11))
    half = r[...] - alpha * s[...]
    x_out[...] = x[...] + alpha * p[...] + omega * half
    r_out[...] = half - omega * (w[...] - alpha * z[...])


def pairings(sizes):
    count_x, count_y = sizes
    grid = [(i, j) for i in range(count_x) for j in range(count_y)]
    number = lambda i, j: i * count_y + j
    step = lambda i: i + 1 if i % 2 else i - 1
    x_even = [(number(i, j), number(i ^ 1, j)) for i, j in grid]
    x_odd = [
        (number(i, j), number(step(i), j) if 0 < i < count_x - 1 else number(i, j ^ 1)) for i, j in grid
    ]
    y_even = [(number(i, j), number(i, j ^ 1)) for i, j in grid]
    y_odd = [(number(i, j), number(i, step(j) % count_y)) for i, j in grid]
    return (x_even, x_odd), (y_even, y_odd)


def per_device(sizes, source, conductivity, robin_flags, htc_class, htc_table):
    shape = source.shape
    elems_z = robin_flags.shape[2]
    rows, size = shape[0] * shape[1], shape[2]
    assert robin_flags.shape[:2] == (1, 1) and sizes[0] % 2 == 0 and sizes[1] % 2 == 0
    devices = sizes[0] * sizes[1]
    pos = jnp.stack([lax.axis_index("gx"), lax.axis_index("gy")]).astype(jnp.int32)
    c = {name: jnp.asarray(value) for name, value in constants(elems_z).items()}
    mats = [c[name] for name in ("forward", "back", "z_forward", "z_back", "lanes")]
    x_pairs, y_pairs = pairings(sizes)

    def struct(n=rows):
        return jax.ShapeDtypeStruct((n, size), f32)

    field = struct()
    faces = [struct(N)] * 4
    row = jax.ShapeDtypeStruct((devices, 1, 128), f32)

    def call(kernel, outs, smem, *operands):
        specs = [SMEM] * smem + [VMEM] * (len(operands) - smem)
        return pl.pallas_call(
            kernel,
            out_shape=outs,
            in_specs=specs,
            out_specs=[VMEM] * len(outs),
            compiler_params=pltpu.CompilerParams(vmem_limit_bytes=32 * 1024 * 1024),
        )(*operands)

    def permute(values, pairs):
        return lax.ppermute(values, ("gx", "gy"), pairs)

    def exchange(pairs, even, odd):
        odd = permute(odd, pairs[1])
        return permute(even, pairs[0]), odd

    def swap(parts):
        x_odd = permute(parts[1], x_pairs[1])
        y_odd = permute(parts[3], y_pairs[1])
        x_even = permute(parts[0], x_pairs[0])
        return x_even, x_odd, permute(parts[2], y_pairs[0]), y_odd

    def spread(values):
        return lax.all_to_all(values, ("gx", "gy"), 0, 0)

    flat = lambda v: v.reshape(rows, size)
    ws, wk, robin, *parts = call(
        functools.partial(field_kernel, sizes),
        [field] * 3 + [struct(3 * N)] * 2,
        2,
        pos, htc_table, flat(source), flat(conductivity),
        robin_flags.reshape(1, elems_z), htc_class.reshape(1, elems_z),
        c["weights"], c["faces"], c["lanes"], c["spread"],
    )
    parts = exchange(y_pairs, *parts)
    ws, wk_y, robin, *parts = call(
        functools.partial(fold_y_kernel, sizes),
        [field] * 3 + [struct(4 * N)] * 2,
        1,
        pos, ws, wk, robin, *parts,
    )
    parts = exchange(x_pairs, *parts)
    b, *coefs, inverse, q, s0, s1, s2, s3 = call(
        functools.partial(first_kernel, sizes),
        [field] * 8 + faces,
        1,
        pos, ws, wk_y, robin, wk, *parts, c["weights"], *mats,
    )
    recv = swap((s0, s1, s2, s3))
    s, q, *parts = call(
        functools.partial(apply_kernel, sizes), [field] * 2 + faces, 1,
        pos, q, *recv, *coefs, *mats,
    )
    recv = swap(parts)
    z, products, q, *parts = call(
        functools.partial(first_dots_kernel, sizes), [field, row, field] + faces, 1,
        pos, b, s, inverse, q, *recv, *coefs, *mats,
    )
    state = (b, s, z)
    for iteration in range(ITERS - 1):
        recv = swap(parts)
        gathered = spread(products)
        x, r, p, s, w, zpart, q, *parts = call(
            functools.partial(update_kernel, sizes, iteration == 0),
            [field] * 7 + faces,
            1,
            pos, gathered, q, *recv, *state, *coefs, *mats,
        )
        recv = swap(parts)
        last = iteration == ITERS - 2
        aw, z, products, *rest = call(
            functools.partial(dots_kernel, sizes, last),
            [field] * 2 + [row] + ([] if last else [field] + faces),
            1,
            pos, b, r, s, w, zpart, inverse, q, *recv, *(() if last else (*coefs, *mats)),
        )
        if not last:
            q, *parts = rest
            state = (r, p, s, w, z, aw, x)
    gathered = spread(products)
    x, r = call(functools.partial(last_kernel, sizes), [field] * 2, 0, gathered, r, p, s, w, z, x)
    return x.reshape(shape), r.reshape(shape)


def solution(mesh):
    sizes = (mesh.shape["gx"], mesh.shape["gy"])
    field = P("gx", "gy", None)
    return jax.shard_map(
        functools.partial(per_device, sizes),
        mesh=mesh,
        in_specs=(field, field, field, field, P()),
        out_specs=(field, field),
        check_vma=False,
    )
```

```python
import functools

import jax
import jax.numpy as jnp
import numpy as np
from jax import lax
from jax.experimental import pallas as pl
from jax.experimental.pallas import tpu as pltpu
from jax.sharding import PartitionSpec as P

ITERS = 3
N = 8

gll_points = (
    -1.0,
    -0.8717401485096066,
    -0.5917001814331423,
    -0.2092992179024789,
    0.2092992179024789,
    0.5917001814331423,
    0.8717401485096066,
    1.0,
)
gll_weights = (
    0.03571428571428571,
    0.21070422714350603,
    0.3411226924835044,
    0.4124587946587038,
    0.4124587946587038,
    0.3411226924835044,
    0.21070422714350603,
    0.03571428571428571,
)
mass_coef = 0.2
scan_speed = 2.0
f32 = jnp.float32
VMEM = pl.BlockSpec(memory_space=pltpu.VMEM)
HBM = pl.BlockSpec(memory_space=pl.ANY)
COST = 1 << 20
dot = functools.partial(jnp.dot, precision=lax.Precision.HIGHEST, preferred_element_type=f32)


def lagrange_derivative():
    points = np.array(gll_points)
    barycentric = np.array(
        [1.0 / np.prod([points[j] - points[m] for m in range(N) if m != j]) for j in range(N)]
    )
    derivative = np.zeros((N, N))
    for a in range(N):
        for b in range(N):
            if a != b:
                derivative[a, b] = barycentric[b] / barycentric[a] / (points[a] - points[b])
        derivative[a, a] = -np.sum(derivative[a])
    return derivative.astype(np.float32)


def constants(elems_z):
    group = min(elems_z, 32)
    z_back = np.kron(np.eye(group, dtype=np.float32), lagrange_derivative())
    lane = np.arange(N * elems_z)
    low = (lane % N == 0) & (lane > 0)
    high = (lane % N == N - 1) & (lane < N * elems_z - 1)
    lanes = np.stack([low, high] + [0 * lane] * 6).astype(np.float32)
    return np.ascontiguousarray(z_back.T), z_back, lanes


def weights_1d():
    return [float(np.float32(x)) for x in gll_weights]


def position():
    return lax.axis_index("gx"), lax.axis_index("gy")


def tiles(ref):
    return [ref[N * a : N * a + N, :] for a in range(N)]


def store(ref, values):
    for a in range(N):
        ref[N * a : N * a + N, :] = values[a]


def row_index(shape):
    return lax.broadcasted_iota(jnp.int32, shape, 0)


def along(shape, values, index):
    out = jnp.full(shape, values[0], f32)
    for i in range(1, len(values)):
        out = jnp.where(index == i, values[i], out)
    return out


def fold_z(v, lanes):
    size = v.shape[1]
    return (
        v
        + pltpu.roll(v, 1, axis=1) * lanes[0:1, :]
        + pltpu.roll(v, size - 1, axis=1) * lanes[1:2, :]
    )


def pick(pos, axis, even, odd):
    return jnp.where(pos[axis] % 2 == 0, even, odd)


def send(pos, axis, low, high, even_ref, odd_ref):
    even_ref[...] = pick(pos, axis, high, low)
    odd_ref[...] = pick(pos, axis, low, high)


def received(sizes, pos, axis, even, odd):
    low = jnp.where(pos[axis] > 0, pick(pos, axis, odd, even), 0.0)
    high = jnp.where(pos[axis] < sizes[axis] - 1, pick(pos, axis, even, odd), 0.0)
    return low, high


def place(low, high, a, row):
    return jnp.where(row == 0, low[a : a + 1], jnp.where(row == N - 1, high[a : a + 1], 0.0))


def robin_tiles(sizes, pos, table, flags, classes, size):
    elems_z = flags.shape[1]
    coefficient = jnp.zeros(flags.shape, f32)
    for c in range(table.shape[1]):
        coefficient = jnp.where(classes[...] == c, table[:, c : c + 1], coefficient)
    element = lax.broadcasted_iota(jnp.int32, flags.shape, 1)
    sides = [
        pos[0] == 0, pos[0] == sizes[0] - 1, pos[1] == 0, pos[1] == sizes[1] - 1,
        element == 0, element == elems_z - 1,
    ]
    rows = []
    for bit, side in enumerate(sides):
        flagged = (flags[...] >> bit) % 2 == 1
        rows.append(jnp.where(flagged & side, coefficient, 0.0))
    rows += [jnp.zeros(flags.shape, f32)] * 2
    spread = lax.broadcasted_iota(jnp.int32, (elems_z, size), 1) // N == row_index((elems_z, size))
    faces = dot(jnp.concatenate(rows, 0), spread.astype(f32))
    node = lax.broadcasted_iota(jnp.int32, (1, size), 1) % N
    w = weights_1d()
    w_z = along((1, size), w, node)
    row = row_index((N, size))
    w_b = along((N, size), w, row)
    w_bz = w_b * w_z
    ends_z = jnp.where(node == 0, faces[4:5], 0.0) + jnp.where(node == N - 1, faces[5:6], 0.0)
    common = place(faces[2:3] * w_z, faces[3:4] * w_z, 0, row) + w_b * ends_z
    robin = [w[a] * common for a in range(N)]
    robin[0] += w_bz * faces[0:1]
    robin[N - 1] += w_bz * faces[1:2]
    return robin, w_bz


def field_kernel(sizes, source, k, flags, classes, table, even_out, odd_out,
                 v_ref, k_ref, flags_ref, classes_ref, table_ref, low, high, sems):
    pairs = (
        (flags, flags_ref), (classes, classes_ref), (table, table_ref), (source, v_ref), (k, k_ref),
    )
    copies = [pltpu.make_async_copy(*pair, sems.at[i]) for i, pair in enumerate(pairs)]
    for copy in copies:
        copy.start()
    for copy in copies[:3]:
        copy.wait()
    pos = position()
    robin, w_bz = robin_tiles(sizes, pos, table_ref, flags_ref, classes_ref, source.shape[1])
    for copy in copies[3:]:
        copy.wait()
    w = weights_1d()
    ws = [w[a] * w_bz * v for a, v in enumerate(tiles(v_ref))]
    wk = [w[a] * w_bz * v for a, v in enumerate(tiles(k_ref))]
    for i, field in enumerate((ws, wk, robin)):
        for a in range(N):
            low[N * i + a : N * i + a + 1, :] = field[a][0:1]
            high[N * i + a : N * i + a + 1, :] = field[a][N - 1 : N]
    send(pos, 1, low[...], high[...], even_out, odd_out)


def whole_field_kernel(sizes, source, k, flags, classes, table, ws_out, wk_out, robin_out):
    robin, w_bz = robin_tiles(sizes, position(), table, flags, classes, source.shape[1])
    w = weights_1d()
    store(robin_out, robin)
    store(ws_out, [w[a] * w_bz * v for a, v in enumerate(tiles(source))])
    store(wk_out, [w[a] * w_bz * v for a, v in enumerate(tiles(k))])


def fold_y_kernel(sizes, ws, wk, robin, even, odd, even_out, odd_out):
    pos = position()
    low, high = received(sizes, pos, 1, even[...], odd[...])
    row = row_index((N, ws.shape[1]))
    sides = []
    for a in (0, N - 1):
        part = [
            field[N * a : N * a + N, :] + place(low, high, N * i + a, row)
            for i, field in enumerate((ws, wk, robin))
        ]
        sides.append(jnp.concatenate(part + [wk[N * a : N * a + N, :]], 0))
    send(pos, 0, sides[0], sides[1], even_out, odd_out)


def prepare_kernel(sizes, ws, wk, robin, even, odd, lanes,
                   b_out, kx_out, ky_out, kz_out, advect_out, diagonal_out, inverse_out):
    pos = position()
    low, high = received(sizes, pos, 1, even[...], odd[...])
    shape = (N, ws.shape[1])
    row = row_index(shape)
    w = weights_1d()
    node = lax.broadcasted_iota(jnp.int32, (1, shape[1]), 1) % N
    copies_z = 1.0 + lanes[0:1, :] + lanes[1:2, :]
    shared_y = ((row == 0) & (pos[1] > 0)) | ((row == N - 1) & (pos[1] < sizes[1] - 1))
    copies_yz = jnp.where(shared_y, 2.0, 1.0) * copies_z
    weights_yz = along(shape, w, row) * along((1, shape[1]), w, node) * copies_yz
    inverse_yz = 1.0 / copies_yz
    for a in range(N):
        at = slice(N * a, N * a + N)
        summed = [
            field[at, :] + place(low, high, N * i + a, row) for i, field in enumerate((ws, wk, robin))
        ]
        b_out[at, :] = fold_z(summed[0], lanes)
        kz_out[at, :] = summed[1]
        kx_out[at, :] = fold_z(summed[1], lanes)
        ky_out[at, :] = fold_z(wk[at, :], lanes)
        copies_x = 1.0
        if a == 0:
            copies_x = jnp.where(pos[0] > 0, 2.0, 1.0)
        if a == N - 1:
            copies_x = jnp.where(pos[0] < sizes[0] - 1, 2.0, 1.0)
        weights_a = w[a] * weights_yz
        advect_out[at, :] = scan_speed * weights_a
        diagonal_out[at, :] = fold_z(summed[2], lanes) + mass_coef * copies_x * weights_a
        inverse_out[at, :] = inverse_yz * (1.0 / copies_x)


def contract(m, values):
    half = N // 2
    total = [values[b] + values[N - 1 - b] for b in range(half)]
    apart = [values[b] - values[N - 1 - b] for b in range(half)]
    out = [None] * N
    for a in range(half):
        even = sum(float((m[a][b] + m[a][N - 1 - b]) / 2) * total[b] for b in range(half))
        odd = sum(float((m[a][b] - m[a][N - 1 - b]) / 2) * apart[b] for b in range(half))
        out[a] = even + odd
        out[N - 1 - a] = odd - even
    return out


def rotations(m, row):
    return [along(row.shape, [float(m[b][(b + s) % N]) for b in range(N)], row) for s in range(N)]


def contract_rows(coefs, v):
    out = coefs[0] * v
    for s in range(1, N):
        out += coefs[s] * pltpu.roll(v, N - s, axis=0)
    return out


def operate(pos, v, kx, ky, advect, xy_out, sends, low, high):
    d = lagrange_derivative()
    k, speed = tiles(kx), tiles(advect)
    flux = [k[a] * g - speed[a] * v[a] for a, g in enumerate(contract(d, v))]
    x = contract(d.T, flux)
    send(pos, 0, x[0], x[N - 1], sends[0], sends[1])
    row = row_index(v[0].shape)
    forward, back = rotations(d, row), rotations(d.T, row)
    for a in range(N):
        at = slice(N * a, N * a + N)
        y = contract_rows(back, ky[at, :] * contract_rows(forward, v[a]))
        low[a : a + 1, :] = y[0:1]
        high[a : a + 1, :] = y[N - 1 : N]
        xy_out[at, :] = x[a] + y
    send(pos, 1, low[...], high[...], sends[2], sends[3])


def along_z(v, xy, kz, diagonal, z_forward, z_back, lanes, q_out):
    group = z_forward.shape[0]
    rows, size = v.shape
    columns = [slice(i, i + group) for i in range(0, size, group)]
    grad = dot(jnp.concatenate([v[:, c] for c in columns], 0), z_forward[...])
    flux = [kz[:, c] * grad[i * rows : (i + 1) * rows] for i, c in enumerate(columns)]
    back = dot(jnp.concatenate(flux, 0), z_back[...])
    back = jnp.concatenate([back[i * rows : (i + 1) * rows] for i in range(len(columns))], 1)
    q_out[...] = fold_z(back, lanes) + (xy[...] + diagonal[...] * v[...])


def assemble(sizes, pos, q, recv):
    x_even, x_odd, y_even, y_odd = recv
    x_low, x_high = received(sizes, pos, 0, x_even[...], x_odd[...])
    y_low, y_high = received(sizes, pos, 1, y_even[...], y_odd[...])
    row = row_index(y_low.shape)
    out = [q[N * a : N * a + N, :] + place(y_low, y_high, a, row) for a in range(N)]
    out[0] += x_low
    out[N - 1] += x_high
    return out


def first_kernel(sizes, b_in, kx, ky_in, advect, even, odd, lanes,
                 b_out, ky_out, xy_out, *refs):
    pos = position()
    low, high = received(sizes, pos, 0, even[...], odd[...])
    b, ky = tiles(b_in), tiles(ky_in)
    for a, side in ((0, low), (N - 1, high)):
        b[a] += fold_z(side[0:N], lanes)
        ky[a] += fold_z(side[3 * N : 4 * N], lanes)
    store(b_out, b)
    store(ky_out, ky)
    operate(pos, b, kx, ky_out, advect, xy_out, refs[:4], *refs[4:])


def first_z_kernel(sizes, b, xy, kz_in, diagonal_in, even, odd, z_forward, z_back, lanes,
                   kz_out, diagonal_out, q_out):
    pos = position()
    low, high = received(sizes, pos, 0, even[...], odd[...])
    kz_out[...] = kz_in[...]
    diagonal_out[...] = diagonal_in[...]
    for a, side in ((0, low), (N - 1, high)):
        at = slice(N * a, N * a + N)
        kz_out[at, :] += side[N : 2 * N]
        diagonal_out[at, :] += fold_z(side[2 * N : 3 * N], lanes)
    along_z(b, xy, kz_out, diagonal_out, z_forward, z_back, lanes, q_out)


def dots_row(pairs, inverse, out):
    width = out.shape[-1]
    rows = []
    for u, v in pairs:
        product = sum(x * (y * m) for x, y, m in zip(u, v, inverse))
        product = sum(product[:, i : i + width] for i in range(0, product.shape[1], width))
        rows.append(jnp.sum(product, axis=0, keepdims=True))
    rows += [jnp.zeros_like(rows[0])] * (-len(rows) % N)
    sums = jnp.sum(jnp.concatenate(rows, 0), axis=1, keepdims=True)
    shape = (len(rows), width)
    lane = lax.broadcasted_iota(jnp.int32, shape, 1)
    row = jnp.sum(jnp.where(lane == row_index(shape), sums, 0.0), axis=0, keepdims=True)
    for i in range(out.shape[0]):
        out[i] = row


def totals(gathered, count):
    row = jnp.sum(gathered[...], axis=0)
    return [jnp.broadcast_to(row[:, i : i + 1], row.shape) for i in range(count)]


def wide(scalar, like):
    return jnp.concatenate([scalar] * (like.shape[1] // scalar.shape[1]), 1)


def inner_pairs(b, r, s, w, z):
    return [(b, r), (b, s), (b, w), (b, z), (w, r), (w, s), (r, z), (s, z), (w, w), (w, z), (z, z)]


def steps(g):
    br, bs, bw, bz, wr, ws, rz, sz, ww, wz, zz = g
    alpha = br / bs
    omega = (wr - alpha * (ws + rz) + alpha * alpha * sz) / (
        ww - 2.0 * alpha * wz + alpha * alpha * zz
    )
    rho_next = (br - alpha * bs) - omega * (bw - alpha * bz)
    beta = rho_next / br * (alpha / omega)
    return alpha, omega, beta


def apply_kernel(sizes, q, x0, x1, y0, y1, kx, ky, advect, s_out, xy_out, *refs):
    pos = position()
    s = assemble(sizes, pos, q, (x0, x1, y0, y1))
    store(s_out, s)
    operate(pos, s, kx, ky, advect, xy_out, refs[:4], *refs[4:])


def z_kernel(v, xy, kz, diagonal, z_forward, z_back, lanes, q_out):
    along_z(v, xy, kz, diagonal, z_forward, z_back, lanes, q_out)


def first_dots_kernel(sizes, b, s, inverse, q, x0, x1, y0, y1, kx, ky, advect,
                      z_out, row, xy_out, *refs):
    pos = position()
    z = assemble(sizes, pos, q, (x0, x1, y0, y1))
    store(z_out, z)
    b, s = tiles(b), tiles(s)
    dots_row([(b, b), (b, s), (b, z), (s, s), (s, z), (z, z)], tiles(inverse), row)
    operate(pos, z, kx, ky, advect, xy_out, refs[:4], *refs[4:])


def update_kernel(sizes, first, gathered, s, w, z, aw, q, x0, x1, y0, y1, kx, ky, advect,
                  w_out, az_out, scalars, xy_out, *refs):
    pos = position()
    if first:
        bb, bs, bz, ss, sz, zz = totals(gathered, 6)
        g = (bb, bs, bs, bz, bs, ss, bz, sz, ss, sz, zz)
    else:
        g = totals(gathered, 11)
    values = steps(g)
    for i, value in enumerate(values):
        scalars[i : i + 1, :] = value
    alpha, omega, _ = (wide(value, s) for value in values)
    az = assemble(sizes, pos, q, (x0, x1, y0, y1))
    store(az_out, az)
    w_next = [
        (w_ - alpha * z_) - omega * (aw_ - alpha * az_)
        for w_, z_, aw_, az_ in zip(tiles(w), tiles(z), tiles(aw), az)
    ]
    store(w_out, w_next)
    operate(pos, w_next, kx, ky, advect, xy_out, refs[:4], *refs[4:])


def update_rest_kernel(first, scalars, r, p, s, w, z, az, w_next, xy, kz, diagonal, z_forward, z_back,
                       lanes, *refs):
    x, outs = (None, refs) if first else (refs[0], refs[1:])
    x_out, r_out, p_out, s_out, zpart_out, q_out = outs
    along_z(w_next, xy, kz, diagonal, z_forward, z_back, lanes, q_out)
    alpha, omega, beta = (wide(scalars[i : i + 1, :], s) for i in range(3))
    half = r[...] - alpha * s[...]
    step = alpha * p[...] + omega * half
    x_out[...] = step if first else x[...] + step
    r_next = half - omega * (w[...] - alpha * z[...])
    r_out[...] = r_next
    p_out[...] = r_next + beta * (p[...] - omega * s[...])
    s_out[...] = w_next[...] + beta * (s[...] - omega * z[...])
    zpart_out[...] = beta * (z[...] - omega * az[...])


def dots_kernel(sizes, last, b, r, s, w, zpart, inverse, q, x0, x1, y0, y1, *refs):
    pos = position()
    aw = assemble(sizes, pos, q, (x0, x1, y0, y1))
    z = [u + v for u, v in zip(aw, tiles(zpart))]
    if last:
        z_out, row = refs
    else:
        kx, ky, advect, z_out, row, aw_out, xy_out, *refs = refs
        store(aw_out, aw)
    store(z_out, z)
    pairs = inner_pairs(tiles(b), tiles(r), tiles(s), tiles(w), z)
    dots_row(pairs, tiles(inverse), row)
    if not last:
        operate(pos, z, kx, ky, advect, xy_out, refs[:4], *refs[4:])


def last_kernel(gathered, r, p, s, w, z, x, x_out, r_out):
    alpha, omega, _ = steps(totals(gathered, 11))
    alpha, omega = wide(alpha, s), wide(omega, s)
    half = r[...] - alpha * s[...]
    x_out[...] = x[...] + alpha * p[...] + omega * half
    r_out[...] = half - omega * (w[...] - alpha * z[...])


def pairings(sizes):
    count_x, count_y = sizes
    grid = [(i, j) for i in range(count_x) for j in range(count_y)]
    number = lambda i, j: i * count_y + j
    step = lambda i: i + 1 if i % 2 else i - 1
    x_even = [(number(i, j), number(i ^ 1, j)) for i, j in grid]
    x_odd = [
        (number(i, j), number(step(i), j) if 0 < i < count_x - 1 else number(i, j ^ 1)) for i, j in grid
    ]
    y_even = [(number(i, j), number(i, j ^ 1)) for i, j in grid]
    y_odd = [(number(i, j), number(i, step(j) % count_y)) for i, j in grid]
    return (x_even, x_odd), (y_even, y_odd)


def per_device(sizes, source, conductivity, robin_flags, htc_class, htc_table):
    shape = source.shape
    elems_z = robin_flags.shape[2]
    rows, size = shape[0] * shape[1], shape[2]
    assert robin_flags.shape[:2] == (1, 1) and sizes[0] % 2 == 0 and sizes[1] % 2 == 0
    devices = sizes[0] * sizes[1]
    z_forward, z_back, lanes = (jnp.asarray(value) for value in constants(elems_z))
    x_pairs, y_pairs = pairings(sizes)

    def struct(n=rows):
        return jax.ShapeDtypeStruct((n, size), f32)

    field = struct()
    faces = [struct(N)] * 4
    row = jax.ShapeDtypeStruct((devices, 1, 128), f32)
    scalars = jax.ShapeDtypeStruct((N, 128), f32)
    side = [pltpu.VMEM((N, size), f32)] * 2

    def call(kernel, outs, *operands, scratch=(), hbm=0, limit=32, cost=0):
        specs = [HBM] * hbm + [VMEM] * (len(operands) - hbm)
        return pl.pallas_call(
            kernel,
            out_shape=outs,
            in_specs=specs,
            out_specs=[VMEM] * len(outs),
            scratch_shapes=list(scratch),
            compiler_params=pltpu.CompilerParams(vmem_limit_bytes=limit * 1024 * 1024),
            cost_estimate=pl.CostEstimate(flops=cost, bytes_accessed=cost, transcendentals=0)
            if cost
            else None,
        )(*operands)

    def permute(values, pairs):
        return lax.ppermute(values, ("gx", "gy"), pairs)

    def exchange(pairs, even, odd):
        odd = permute(odd, pairs[1])
        return permute(even, pairs[0]), odd

    def swap(parts):
        x_odd = permute(parts[1], x_pairs[1])
        y_odd = permute(parts[3], y_pairs[1])
        x_even = permute(parts[0], x_pairs[0])
        return x_even, x_odd, permute(parts[2], y_pairs[0]), y_odd

    def spread(values):
        return lax.all_to_all(values, ("gx", "gy"), 0, 0)

    given = (
        source.reshape(rows, size), conductivity.reshape(rows, size),
        robin_flags.reshape(1, elems_z), htc_class.reshape(1, elems_z), htc_table.reshape(1, -1),
    )
    parts = call(
        functools.partial(field_kernel, sizes), [struct(3 * N)] * 2, *given,
        hbm=5,
        limit=60,
        scratch=[pltpu.VMEM(v.shape, v.dtype) for v in given]
        + [pltpu.VMEM((3 * N, size), f32)] * 2
        + [pltpu.SemaphoreType.DMA((5,))],
    )
    recv = exchange(y_pairs, *parts)
    ws, wk, robin = call(functools.partial(whole_field_kernel, sizes), [field] * 3, *given, cost=COST)
    parts = call(
        functools.partial(fold_y_kernel, sizes), [struct(4 * N)] * 2, ws, wk, robin, *recv
    )
    b, kx, ky, kz, advect, diagonal, inverse = call(
        functools.partial(prepare_kernel, sizes), [field] * 7, ws, wk, robin, *recv, lanes,
        cost=COST,
    )
    recv = exchange(x_pairs, *parts)
    b, ky, xy, *parts = call(
        functools.partial(first_kernel, sizes), [field] * 3 + faces,
        b, kx, ky, advect, *recv, lanes, scratch=side,
    )
    kz, diagonal, q = call(
        functools.partial(first_z_kernel, sizes), [field] * 3,
        b, xy, kz, diagonal, *recv, z_forward, z_back, lanes, cost=COST,
    )
    coefs = (kx, ky, advect)
    z_args = (kz, diagonal, z_forward, z_back, lanes)
    recv = swap(parts)
    s, xy, *parts = call(
        functools.partial(apply_kernel, sizes), [field] * 2 + faces,
        q, *recv, *coefs, scratch=side,
    )
    (q,) = call(z_kernel, [field], s, xy, *z_args, cost=COST)
    recv = swap(parts)
    z, products, xy, *parts = call(
        functools.partial(first_dots_kernel, sizes), [field, row, field] + faces,
        b, s, inverse, q, *recv, *coefs, scratch=side,
    )
    (q,) = call(z_kernel, [field], z, xy, *z_args, cost=COST)
    r, p, w, aw, x = b, b, s, z, ()
    for iteration in range(ITERS - 1):
        gathered = spread(products)
        recv = swap(parts)
        first, last = iteration == 0, iteration == ITERS - 2
        w_next, az, values, xy, *parts = call(
            functools.partial(update_kernel, sizes, first),
            [field] * 2 + [scalars, field] + faces,
            gathered, s, w, z, aw, q, *recv, *coefs, scratch=side,
        )
        x, r, p, s, zpart, q = call(
            functools.partial(update_rest_kernel, first), [field] * 6,
            values, r, p, s, w, z, az, w_next, xy, *z_args, *(() if first else (x,)), cost=COST,
        )
        w = w_next
        recv = swap(parts)
        z, products, *rest = call(
            functools.partial(dots_kernel, sizes, last),
            [field, row] + ([] if last else [field] * 2 + faces),
            b, r, s, w, zpart, inverse, q, *recv, *(() if last else coefs),
            scratch=() if last else side,
        )
        if not last:
            aw, xy, *parts = rest
            (q,) = call(z_kernel, [field], z, xy, *z_args, cost=COST)
    gathered = spread(products)
    x, r = call(last_kernel, [field] * 2, gathered, r, p, s, w, z, x)
    return x.reshape(shape), r.reshape(shape)


def solution(mesh):
    sizes = (mesh.shape["gx"], mesh.shape["gy"])
    field = P("gx", "gy", None)
    return jax.shard_map(
        functools.partial(per_device, sizes),
        mesh=mesh,
        in_specs=(field, field, field, field, P()),
        out_specs=(field, field),
        check_vma=False,
    )
```

```python
import functools

import jax
import jax.numpy as jnp
import numpy as np
from jax import lax
from jax.experimental import pallas as pl
from jax.experimental.pallas import tpu as pltpu
from jax.sharding import PartitionSpec as P

ITERS = 3
N = 8

gll_points = (
    -1.0,
    -0.8717401485096066,
    -0.5917001814331423,
    -0.2092992179024789,
    0.2092992179024789,
    0.5917001814331423,
    0.8717401485096066,
    1.0,
)
gll_weights = (
    0.03571428571428571,
    0.21070422714350603,
    0.3411226924835044,
    0.4124587946587038,
    0.4124587946587038,
    0.3411226924835044,
    0.21070422714350603,
    0.03571428571428571,
)
mass_coef = 0.2
scan_speed = 2.0
f32 = jnp.float32
VMEM = pl.BlockSpec(memory_space=pltpu.VMEM)
HBM = pl.BlockSpec(memory_space=pl.ANY)
COST = 1 << 20
dot = functools.partial(jnp.dot, precision=lax.Precision.HIGHEST, preferred_element_type=f32)


def lagrange_derivative():
    points = np.array(gll_points)
    barycentric = np.array(
        [1.0 / np.prod([points[j] - points[m] for m in range(N) if m != j]) for j in range(N)]
    )
    derivative = np.zeros((N, N))
    for a in range(N):
        for b in range(N):
            if a != b:
                derivative[a, b] = barycentric[b] / barycentric[a] / (points[a] - points[b])
        derivative[a, a] = -np.sum(derivative[a])
    return derivative.astype(np.float32)


def constants(elems_z):
    group = min(elems_z, 32)
    z_back = np.kron(np.eye(group, dtype=np.float32), lagrange_derivative())
    lane = np.arange(N * elems_z)
    low = (lane % N == 0) & (lane > 0)
    high = (lane % N == N - 1) & (lane < N * elems_z - 1)
    lanes = np.stack([low, high] + [0 * lane] * 6).astype(np.float32)
    return np.ascontiguousarray(z_back.T), z_back, lanes


def weights_1d():
    return [float(np.float32(x)) for x in gll_weights]


def position():
    return lax.axis_index("gx"), lax.axis_index("gy")


def tiles(ref):
    return [ref[N * a : N * a + N, :] for a in range(N)]


def store(ref, values):
    for a in range(N):
        ref[N * a : N * a + N, :] = values[a]


def row_index(shape):
    return lax.broadcasted_iota(jnp.int32, shape, 0)


def along(shape, values, index):
    out = jnp.full(shape, values[0], f32)
    for i in range(1, len(values)):
        out = jnp.where(index == i, values[i], out)
    return out


def fold_z(v, lanes):
    size = v.shape[1]
    return (
        v
        + pltpu.roll(v, 1, axis=1) * lanes[0:1, :]
        + pltpu.roll(v, size - 1, axis=1) * lanes[1:2, :]
    )


def pick(pos, axis, even, odd):
    return jnp.where(pos[axis] % 2 == 0, even, odd)


def send(pos, axis, low, high, even_ref, odd_ref):
    even_ref[...] = pick(pos, axis, high, low)
    odd_ref[...] = pick(pos, axis, low, high)


def received(sizes, pos, axis, even, odd):
    low = jnp.where(pos[axis] > 0, pick(pos, axis, odd, even), 0.0)
    high = jnp.where(pos[axis] < sizes[axis] - 1, pick(pos, axis, even, odd), 0.0)
    return low, high


def place(low, high, a, row):
    return jnp.where(row == 0, low[a : a + 1], jnp.where(row == N - 1, high[a : a + 1], 0.0))


def robin_tiles(sizes, pos, table, flags, classes, size):
    elems_z = flags.shape[1]
    coefficient = jnp.zeros(flags.shape, f32)
    for c in range(table.shape[1]):
        coefficient = jnp.where(classes[...] == c, table[:, c : c + 1], coefficient)
    element = lax.broadcasted_iota(jnp.int32, flags.shape, 1)
    sides = [
        pos[0] == 0, pos[0] == sizes[0] - 1, pos[1] == 0, pos[1] == sizes[1] - 1,
        element == 0, element == elems_z - 1,
    ]
    rows = []
    for bit, side in enumerate(sides):
        flagged = (flags[...] >> bit) % 2 == 1
        rows.append(jnp.where(flagged & side, coefficient, 0.0))
    rows += [jnp.zeros(flags.shape, f32)] * 2
    spread = lax.broadcasted_iota(jnp.int32, (elems_z, size), 1) // N == row_index((elems_z, size))
    faces = dot(jnp.concatenate(rows, 0), spread.astype(f32))
    node = lax.broadcasted_iota(jnp.int32, (1, size), 1) % N
    w = weights_1d()
    w_z = along((1, size), w, node)
    row = row_index((N, size))
    w_b = along((N, size), w, row)
    w_bz = w_b * w_z
    ends_z = jnp.where(node == 0, faces[4:5], 0.0) + jnp.where(node == N - 1, faces[5:6], 0.0)
    common = place(faces[2:3] * w_z, faces[3:4] * w_z, 0, row) + w_b * ends_z
    robin = [w[a] * common for a in range(N)]
    robin[0] += w_bz * faces[0:1]
    robin[N - 1] += w_bz * faces[1:2]
    return robin, w_bz


def field_kernel(sizes, source, k, flags, classes, table, even_out, odd_out,
                 v_ref, k_ref, flags_ref, classes_ref, table_ref, low, high, sems):
    pairs = (
        (flags, flags_ref), (classes, classes_ref), (table, table_ref), (source, v_ref), (k, k_ref),
    )
    copies = [pltpu.make_async_copy(*pair, sems.at[i]) for i, pair in enumerate(pairs)]
    for copy in copies:
        copy.start()
    for copy in copies[:3]:
        copy.wait()
    pos = position()
    robin, w_bz = robin_tiles(sizes, pos, table_ref, flags_ref, classes_ref, source.shape[1])
    for copy in copies[3:]:
        copy.wait()
    w = weights_1d()
    ws = [w[a] * w_bz * v for a, v in enumerate(tiles(v_ref))]
    wk = [w[a] * w_bz * v for a, v in enumerate(tiles(k_ref))]
    for i, field in enumerate((ws, wk, robin)):
        for a in range(N):
            low[N * i + a : N * i + a + 1, :] = field[a][0:1]
            high[N * i + a : N * i + a + 1, :] = field[a][N - 1 : N]
    send(pos, 1, low[...], high[...], even_out, odd_out)


def whole_field_kernel(sizes, source, k, flags, classes, table, ws_out, wk_out, robin_out):
    robin, w_bz = robin_tiles(sizes, position(), table, flags, classes, source.shape[1])
    w = weights_1d()
    store(robin_out, robin)
    store(ws_out, [w[a] * w_bz * v for a, v in enumerate(tiles(source))])
    store(wk_out, [w[a] * w_bz * v for a, v in enumerate(tiles(k))])


def fold_y_kernel(sizes, ws, wk, robin, even, odd, even_out, odd_out):
    pos = position()
    low, high = received(sizes, pos, 1, even[...], odd[...])
    row = row_index((N, ws.shape[1]))
    sides = []
    for a in (0, N - 1):
        part = [
            field[N * a : N * a + N, :] + place(low, high, N * i + a, row)
            for i, field in enumerate((ws, wk, robin))
        ]
        sides.append(jnp.concatenate(part + [wk[N * a : N * a + N, :]], 0))
    send(pos, 0, sides[0], sides[1], even_out, odd_out)


def prepare_kernel(sizes, ws, wk, robin, even, odd, lanes,
                   b_out, kx_out, ky_out, kz_out, advect_out, diagonal_out, inverse_out):
    pos = position()
    low, high = received(sizes, pos, 1, even[...], odd[...])
    shape = (N, ws.shape[1])
    row = row_index(shape)
    w = weights_1d()
    node = lax.broadcasted_iota(jnp.int32, (1, shape[1]), 1) % N
    copies_z = 1.0 + lanes[0:1, :] + lanes[1:2, :]
    shared_y = ((row == 0) & (pos[1] > 0)) | ((row == N - 1) & (pos[1] < sizes[1] - 1))
    copies_yz = jnp.where(shared_y, 2.0, 1.0) * copies_z
    weights_yz = along(shape, w, row) * along((1, shape[1]), w, node) * copies_yz
    inverse_yz = 1.0 / copies_yz
    for a in range(N):
        at = slice(N * a, N * a + N)
        summed = [
            field[at, :] + place(low, high, N * i + a, row) for i, field in enumerate((ws, wk, robin))
        ]
        b_out[at, :] = fold_z(summed[0], lanes)
        kz_out[at, :] = summed[1]
        kx_out[at, :] = fold_z(summed[1], lanes)
        ky_out[at, :] = fold_z(wk[at, :], lanes)
        copies_x = 1.0
        if a == 0:
            copies_x = jnp.where(pos[0] > 0, 2.0, 1.0)
        if a == N - 1:
            copies_x = jnp.where(pos[0] < sizes[0] - 1, 2.0, 1.0)
        weights_a = w[a] * weights_yz
        advect_out[at, :] = scan_speed * weights_a
        diagonal_out[at, :] = fold_z(summed[2], lanes) + mass_coef * copies_x * weights_a
        inverse_out[at, :] = inverse_yz * (1.0 / copies_x)


def contract(m, values):
    half = N // 2
    total = [values[b] + values[N - 1 - b] for b in range(half)]
    apart = [values[b] - values[N - 1 - b] for b in range(half)]
    out = [None] * N
    for a in range(half):
        even = sum(float((m[a][b] + m[a][N - 1 - b]) / 2) * total[b] for b in range(half))
        odd = sum(float((m[a][b] - m[a][N - 1 - b]) / 2) * apart[b] for b in range(half))
        out[a] = even + odd
        out[N - 1 - a] = odd - even
    return out


def rotations(m, row):
    return [along(row.shape, [float(m[b][(b + s) % N]) for b in range(N)], row) for s in range(N)]


def contract_rows(coefs, v):
    out = coefs[0] * v
    for s in range(1, N):
        out += coefs[s] * pltpu.roll(v, N - s, axis=0)
    return out


def operate(pos, v, kx, ky, advect, xy_out, sends, low, high):
    d = lagrange_derivative()
    k, speed = tiles(kx), tiles(advect)
    flux = [k[a] * g - speed[a] * v[a] for a, g in enumerate(contract(d, v))]
    x = contract(d.T, flux)
    send(pos, 0, x[0], x[N - 1], sends[0], sends[1])
    row = row_index(v[0].shape)
    forward, back = rotations(d, row), rotations(d.T, row)
    for a in range(N):
        at = slice(N * a, N * a + N)
        y = contract_rows(back, ky[at, :] * contract_rows(forward, v[a]))
        low[a : a + 1, :] = y[0:1]
        high[a : a + 1, :] = y[N - 1 : N]
        xy_out[at, :] = x[a] + y
    send(pos, 1, low[...], high[...], sends[2], sends[3])


def along_z(v, xy, kz, diagonal, z_forward, z_back, lanes, q_out):
    group = z_forward.shape[0]
    rows, size = v.shape
    columns = [slice(i, i + group) for i in range(0, size, group)]
    grad = dot(jnp.concatenate([v[:, c] for c in columns], 0), z_forward[...])
    flux = [kz[:, c] * grad[i * rows : (i + 1) * rows] for i, c in enumerate(columns)]
    back = dot(jnp.concatenate(flux, 0), z_back[...])
    back = jnp.concatenate([back[i * rows : (i + 1) * rows] for i in range(len(columns))], 1)
    q_out[...] = fold_z(back, lanes) + (xy[...] + diagonal[...] * v[...])


def assemble(sizes, pos, q, recv):
    x_even, x_odd, y_even, y_odd = recv
    x_low, x_high = received(sizes, pos, 0, x_even[...], x_odd[...])
    y_low, y_high = received(sizes, pos, 1, y_even[...], y_odd[...])
    row = row_index(y_low.shape)
    out = [q[N * a : N * a + N, :] + place(y_low, y_high, a, row) for a in range(N)]
    out[0] += x_low
    out[N - 1] += x_high
    return out


def first_kernel(sizes, b_in, kx, ky_in, advect, even, odd, lanes,
                 b_out, ky_out, xy_out, *refs):
    pos = position()
    low, high = received(sizes, pos, 0, even[...], odd[...])
    b, ky = tiles(b_in), tiles(ky_in)
    for a, side in ((0, low), (N - 1, high)):
        b[a] += fold_z(side[0:N], lanes)
        ky[a] += fold_z(side[3 * N : 4 * N], lanes)
    store(b_out, b)
    store(ky_out, ky)
    operate(pos, b, kx, ky_out, advect, xy_out, refs[:4], *refs[4:])


def first_z_kernel(sizes, b, xy, kz_in, diagonal_in, even, odd, z_forward, z_back, lanes,
                   kz_out, diagonal_out, q_out):
    pos = position()
    low, high = received(sizes, pos, 0, even[...], odd[...])
    kz_out[...] = kz_in[...]
    diagonal_out[...] = diagonal_in[...]
    for a, side in ((0, low), (N - 1, high)):
        at = slice(N * a, N * a + N)
        kz_out[at, :] += side[N : 2 * N]
        diagonal_out[at, :] += fold_z(side[2 * N : 3 * N], lanes)
    along_z(b, xy, kz_out, diagonal_out, z_forward, z_back, lanes, q_out)


def dots_row(pairs, inverse, out):
    width = out.shape[-1]
    rows = []
    for u, v in pairs:
        product = sum(x * (y * m) for x, y, m in zip(u, v, inverse))
        product = sum(product[:, i : i + width] for i in range(0, product.shape[1], width))
        rows.append(jnp.sum(product, axis=0, keepdims=True))
    rows += [jnp.zeros_like(rows[0])] * (-len(rows) % N)
    sums = jnp.sum(jnp.concatenate(rows, 0), axis=1, keepdims=True)
    shape = (len(rows), width)
    lane = lax.broadcasted_iota(jnp.int32, shape, 1)
    row = jnp.sum(jnp.where(lane == row_index(shape), sums, 0.0), axis=0, keepdims=True)
    for i in range(out.shape[0]):
        out[i] = row


def totals(gathered, count):
    row = jnp.sum(gathered[...], axis=0)
    return [jnp.broadcast_to(row[:, i : i + 1], row.shape) for i in range(count)]


def wide(scalar, like):
    return jnp.concatenate([scalar] * (like.shape[1] // scalar.shape[1]), 1)


def inner_pairs(b, r, s, w, z):
    return [(b, r), (b, s), (b, w), (b, z), (w, r), (w, s), (r, z), (s, z), (w, w), (w, z), (z, z)]


def steps(g):
    br, bs, bw, bz, wr, ws, rz, sz, ww, wz, zz = g
    alpha = br / bs
    omega = (wr - alpha * (ws + rz) + alpha * alpha * sz) / (
        ww - 2.0 * alpha * wz + alpha * alpha * zz
    )
    rho_next = (br - alpha * bs) - omega * (bw - alpha * bz)
    beta = rho_next / br * (alpha / omega)
    return alpha, omega, beta


def apply_kernel(sizes, q, x0, x1, y0, y1, kx, ky, advect, v_out, xy_out, *refs):
    pos = position()
    v = assemble(sizes, pos, q, (x0, x1, y0, y1))
    store(v_out, v)
    operate(pos, v, kx, ky, advect, xy_out, refs[:4], *refs[4:])


def z_kernel(v, xy, kz, diagonal, z_forward, z_back, lanes, q_out):
    along_z(v, xy, kz, diagonal, z_forward, z_back, lanes, q_out)


def first_dots_kernel(b, s, z, inverse, row):
    b, s, z = tiles(b), tiles(s), tiles(z)
    dots_row([(b, b), (b, s), (b, z), (s, s), (s, z), (z, z)], tiles(inverse), row)


def update_kernel(sizes, gathered, s, z, az, q, x0, x1, y0, y1, kx, ky, advect,
                  z_out, aw_out, scalars, z_xy_out, aw_xy_out, *refs):
    pos = position()
    bb, bs, bz, ss, sz, zz = totals(gathered, 6)
    values = steps((bb, bs, bs, bz, bs, ss, bz, sz, ss, sz, zz))
    for i, value in enumerate(values):
        scalars[i : i + 1, :] = value
    alpha, omega, beta = (wide(value, s) for value in values)
    aaz = assemble(sizes, pos, q, (x0, x1, y0, y1))
    z, az = tiles(z), tiles(az)
    aw = [(z[i] - alpha * az[i]) - omega * (az[i] - alpha * aaz[i]) for i in range(N)]
    z_next = [aw[i] + beta * (z[i] - omega * az[i]) for i in range(N)]
    store(aw_out, aw)
    store(z_out, z_next)
    sends, sides = refs[:4], refs[4:]
    halves = [[ref.at[pl.ds(i * N, N)] for ref in sends] for i in range(2)]
    operate(pos, z_next, kx, ky, advect, z_xy_out, halves[0], *sides)
    operate(pos, aw, kx, ky, advect, aw_xy_out, halves[1], *sides)


def update_rest_kernel(scalars, b, s, z, az, z_next, inverse, x_out, r_out, p_out, s_out, w_out, row):
    alpha, omega, beta = (wide(scalars[i : i + 1, :], s) for i in range(3))
    fields = [], [], [], []
    for i in range(N):
        at = slice(N * i, N * i + N)
        b_, s_, z_, az_ = b[at, :], s[at, :], z[at, :], az[at, :]
        half, applied_half = b_ - alpha * s_, s_ - alpha * z_
        x_out[at, :] = alpha * b_ + omega * half
        r = half - omega * applied_half
        w = applied_half - omega * (z_ - alpha * az_)
        s_next = w + beta * (s_ - omega * z_)
        p_out[at, :] = r + beta * (b_ - omega * s_)
        r_out[at, :], w_out[at, :], s_out[at, :] = r, w, s_next
        for values, value in zip(fields, (b_, r, s_next, w)):
            values.append(value)
    dots_row(inner_pairs(*fields, tiles(z_next)), tiles(inverse), row)


def two_z_kernel(z, z_xy, aw, aw_xy, kz, diagonal, z_forward, z_back, lanes, z_q_out, aw_q_out):
    along_z(z, z_xy, kz, diagonal, z_forward, z_back, lanes, z_q_out)
    along_z(aw, aw_xy, kz, diagonal, z_forward, z_back, lanes, aw_q_out)


def apply_two_kernel(sizes, z_q, aw_q, x0, x1, y0, y1, kx, ky, advect, az_out, aaw_out, xy_out, *refs):
    pos = position()
    halves = [[ref.at[pl.ds(i * N, N)] for ref in (x0, x1, y0, y1)] for i in range(2)]
    az = assemble(sizes, pos, z_q, halves[0])
    store(az_out, az)
    operate(pos, az, kx, ky, advect, xy_out, refs[:4], *refs[4:])
    store(aaw_out, assemble(sizes, pos, aw_q, halves[1]))


def second_kernel(sizes, gathered, b, x, r, p, s, w, z, az, aw, aaw, inverse, q, x0, x1, y0, y1,
                  x_out, r_out, p_out, s_out, w_out, z_out, row):
    pos = position()
    alpha, omega, beta = (wide(value, s) for value in steps(totals(gathered, 11)))
    aaz = assemble(sizes, pos, q, (x0, x1, y0, y1))
    fields = [], [], [], []
    for i in range(N):
        at = slice(N * i, N * i + N)
        r_, s_, w_, z_, az_ = r[at, :], s[at, :], w[at, :], z[at, :], az[at, :]
        applied_half = w_ - alpha * z_
        applied_twice = aw[at, :] - alpha * az_
        half = r_ - alpha * s_
        r_next = half - omega * applied_half
        x_out[at, :] = x[at, :] + alpha * p[at, :] + omega * half
        p_out[at, :] = r_next + beta * (p[at, :] - omega * s_)
        w_next = applied_half - omega * applied_twice
        aw_next = applied_twice - omega * (aaw[at, :] - alpha * aaz[i])
        s_next = w_next + beta * (s_ - omega * z_)
        z_next = aw_next + beta * (z_ - omega * az_)
        r_out[at, :], w_out[at, :], s_out[at, :], z_out[at, :] = r_next, w_next, s_next, z_next
        for values, value in zip(fields, (r_next, s_next, w_next, z_next)):
            values.append(value)
    dots_row(inner_pairs(tiles(b), *fields), tiles(inverse), row)


def last_kernel(gathered, r, p, s, w, z, x, x_out, r_out):
    alpha, omega, _ = steps(totals(gathered, 11))
    alpha, omega = wide(alpha, s), wide(omega, s)
    half = r[...] - alpha * s[...]
    x_out[...] = x[...] + alpha * p[...] + omega * half
    r_out[...] = half - omega * (w[...] - alpha * z[...])


def pairings(sizes):
    count_x, count_y = sizes
    grid = [(i, j) for i in range(count_x) for j in range(count_y)]
    number = lambda i, j: i * count_y + j
    step = lambda i: i + 1 if i % 2 else i - 1
    x_even = [(number(i, j), number(i ^ 1, j)) for i, j in grid]
    x_odd = [
        (number(i, j), number(step(i), j) if 0 < i < count_x - 1 else number(i, j ^ 1)) for i, j in grid
    ]
    y_even = [(number(i, j), number(i, j ^ 1)) for i, j in grid]
    y_odd = [(number(i, j), number(i, step(j) % count_y)) for i, j in grid]
    return (x_even, x_odd), (y_even, y_odd)


def per_device(sizes, source, conductivity, robin_flags, htc_class, htc_table):
    shape = source.shape
    elems_z = robin_flags.shape[2]
    rows, size = shape[0] * shape[1], shape[2]
    assert robin_flags.shape[:2] == (1, 1) and sizes[0] % 2 == 0 and sizes[1] % 2 == 0
    devices = sizes[0] * sizes[1]
    z_forward, z_back, lanes = (jnp.asarray(value) for value in constants(elems_z))
    x_pairs, y_pairs = pairings(sizes)

    def struct(n=rows):
        return jax.ShapeDtypeStruct((n, size), f32)

    field = struct()
    faces = [struct(N)] * 4
    row = jax.ShapeDtypeStruct((devices, 1, 128), f32)
    scalars = jax.ShapeDtypeStruct((N, 128), f32)
    side = [pltpu.VMEM((N, size), f32)] * 2

    def call(kernel, outs, *operands, scratch=(), hbm=0, limit=32, cost=0):
        specs = [HBM] * hbm + [VMEM] * (len(operands) - hbm)
        return pl.pallas_call(
            kernel,
            out_shape=outs,
            in_specs=specs,
            out_specs=[VMEM] * len(outs),
            scratch_shapes=list(scratch),
            compiler_params=pltpu.CompilerParams(vmem_limit_bytes=limit * 1024 * 1024),
            cost_estimate=pl.CostEstimate(flops=cost, bytes_accessed=cost, transcendentals=0)
            if cost
            else None,
        )(*operands)

    def permute(values, pairs):
        return lax.ppermute(values, ("gx", "gy"), pairs)

    def exchange(pairs, even, odd):
        odd = permute(odd, pairs[1])
        return permute(even, pairs[0]), odd

    def swap(parts):
        x_odd = permute(parts[1], x_pairs[1])
        y_odd = permute(parts[3], y_pairs[1])
        x_even = permute(parts[0], x_pairs[0])
        return x_even, x_odd, permute(parts[2], y_pairs[0]), y_odd

    def spread(values):
        return lax.all_to_all(values, ("gx", "gy"), 0, 0)

    given = (
        source.reshape(rows, size), conductivity.reshape(rows, size),
        robin_flags.reshape(1, elems_z), htc_class.reshape(1, elems_z), htc_table.reshape(1, -1),
    )
    parts = call(
        functools.partial(field_kernel, sizes), [struct(3 * N)] * 2, *given,
        hbm=5,
        limit=60,
        scratch=[pltpu.VMEM(v.shape, v.dtype) for v in given]
        + [pltpu.VMEM((3 * N, size), f32)] * 2
        + [pltpu.SemaphoreType.DMA((5,))],
    )
    recv = exchange(y_pairs, *parts)
    ws, wk, robin = call(functools.partial(whole_field_kernel, sizes), [field] * 3, *given, cost=COST)
    parts = call(
        functools.partial(fold_y_kernel, sizes), [struct(4 * N)] * 2, ws, wk, robin, *recv
    )
    b, kx, ky, kz, advect, diagonal, inverse = call(
        functools.partial(prepare_kernel, sizes), [field] * 7, ws, wk, robin, *recv, lanes,
        cost=COST,
    )
    recv = exchange(x_pairs, *parts)
    b, ky, xy, *parts = call(
        functools.partial(first_kernel, sizes), [field] * 3 + faces,
        b, kx, ky, advect, *recv, lanes, scratch=side,
    )
    kz, diagonal, q = call(
        functools.partial(first_z_kernel, sizes), [field] * 3,
        b, xy, kz, diagonal, *recv, z_forward, z_back, lanes, cost=COST,
    )
    coefs = (kx, ky, advect)
    z_args = (kz, diagonal, z_forward, z_back, lanes)
    recv = swap(parts)

    def apply(q, recv):
        v, xy, *parts = call(
            functools.partial(apply_kernel, sizes), [field] * 2 + faces, q, *recv, *coefs, scratch=side
        )
        recv = swap(parts)
        (q,) = call(z_kernel, [field], v, xy, *z_args, cost=COST)
        return v, q, recv

    s, q, recv = apply(q, recv)
    z, q, recv = apply(q, recv)
    (products,) = call(first_dots_kernel, [row], b, s, z, inverse, cost=COST)
    gathered = spread(products)
    az, q, recv = apply(q, recv)
    z_next, aw, values, z_xy, aw_xy, *parts = call(
        functools.partial(update_kernel, sizes),
        [field] * 2 + [scalars] + [field] * 2 + [struct(2 * N)] * 4,
        gathered, s, z, az, q, *recv, *coefs, scratch=side,
    )
    recv = swap(parts)
    x, r, p, s, w, products = call(
        update_rest_kernel, [field] * 5 + [row], values, b, s, z, az, z_next, inverse, cost=COST
    )
    gathered = spread(products)
    z = z_next
    z_q, aw_q = call(two_z_kernel, [field] * 2, z, z_xy, aw, aw_xy, *z_args, cost=COST)
    az, aaw, xy, *parts = call(
        functools.partial(apply_two_kernel, sizes), [field] * 3 + faces,
        z_q, aw_q, *recv, *coefs, scratch=side,
    )
    recv = swap(parts)
    (q,) = call(z_kernel, [field], az, xy, *z_args, cost=COST)
    x, r, p, s, w, z, products = call(
        functools.partial(second_kernel, sizes), [field] * 6 + [row],
        gathered, b, x, r, p, s, w, z, az, aw, aaw, inverse, q, *recv,
    )
    x, r = call(last_kernel, [field] * 2, spread(products), r, p, s, w, z, x)
    return x.reshape(shape), r.reshape(shape)


def solution(mesh):
    sizes = (mesh.shape["gx"], mesh.shape["gy"])
    field = P("gx", "gy", None)
    return jax.shard_map(
        functools.partial(per_device, sizes),
        mesh=mesh,
        in_specs=(field, field, field, field, P()),
        out_specs=(field, field),
        check_vma=False,
    )
```

```python
import functools

import jax
import jax.numpy as jnp
import numpy as np
from jax import lax
from jax.experimental import pallas as pl
from jax.experimental.pallas import tpu as pltpu
from jax.sharding import PartitionSpec as P

ITERS = 3
N = 8

gll_points = (
    -1.0,
    -0.8717401485096066,
    -0.5917001814331423,
    -0.2092992179024789,
    0.2092992179024789,
    0.5917001814331423,
    0.8717401485096066,
    1.0,
)
gll_weights = (
    0.03571428571428571,
    0.21070422714350603,
    0.3411226924835044,
    0.4124587946587038,
    0.4124587946587038,
    0.3411226924835044,
    0.21070422714350603,
    0.03571428571428571,
)
mass_coef = 0.2
scan_speed = 2.0
f32 = jnp.float32
VMEM = pl.BlockSpec(memory_space=pltpu.VMEM)
HBM = pl.BlockSpec(memory_space=pl.ANY)
COST = 1 << 20
LANES = 128
ORDER = (3, 0, 1, 2)
dot = functools.partial(jnp.dot, precision=lax.Precision.HIGHEST, preferred_element_type=f32)


def lagrange_derivative():
    points = np.array(gll_points)
    barycentric = np.array(
        [1.0 / np.prod([points[j] - points[m] for m in range(N) if m != j]) for j in range(N)]
    )
    derivative = np.zeros((N, N))
    for a in range(N):
        for b in range(N):
            if a != b:
                derivative[a, b] = barycentric[b] / barycentric[a] / (points[a] - points[b])
        derivative[a, a] = -np.sum(derivative[a])
    return derivative.astype(np.float32)


def pieces(v):
    high = v.astype(jnp.bfloat16)
    rest = v - high.astype(f32)
    middle = rest.astype(jnp.bfloat16)
    return high, middle, (rest - middle.astype(f32)).astype(jnp.bfloat16)


def stacked(m):
    high = m.astype(jnp.bfloat16).astype(np.float32)
    middle = (m - high).astype(jnp.bfloat16).astype(np.float32)
    low = m - high - middle
    both = np.concatenate([high, middle], 1)
    return [
        jnp.asarray(np.concatenate([both, both], 0), jnp.bfloat16),
        jnp.asarray(np.concatenate([low, high], 0), jnp.bfloat16),
    ]


def constants(elems_z):
    z_back = np.kron(np.eye(LANES // N, dtype=np.float32), lagrange_derivative())
    lane = np.arange(N * elems_z)
    low = (lane % N == 0) & (lane > 0)
    high = (lane % N == N - 1) & (lane < N * elems_z - 1)
    lanes = np.stack([low, high] + [0 * lane] * 6).astype(np.float32)
    return stacked(z_back.T) + stacked(z_back) + [jnp.asarray(lanes)]


def times(v, first, second):
    high, middle, low = pieces(v)
    product = functools.partial(jnp.dot, preferred_element_type=f32)
    large = product(jnp.concatenate([high, middle], 1), first[...])
    small = product(jnp.concatenate([high, low], 1), second[...])
    return (large[:, :LANES] + large[:, LANES:]) + small


def weights_1d():
    return [float(np.float32(x)) for x in gll_weights]


def position():
    return lax.axis_index("gx"), lax.axis_index("gy")


def tiles(ref):
    return [ref[N * a : N * a + N, :] for a in range(N)]


def store(ref, values):
    for a in range(N):
        ref[N * a : N * a + N, :] = values[a]


def row_index(shape):
    return lax.broadcasted_iota(jnp.int32, shape, 0)


def along(shape, values, index):
    out = jnp.full(shape, values[0], f32)
    for i in range(1, len(values)):
        out = jnp.where(index == i, values[i], out)
    return out


def fold_z(v, lanes):
    size = v.shape[1]
    return (
        v
        + pltpu.roll(v, 1, axis=1) * lanes[0:1, :]
        + pltpu.roll(v, size - 1, axis=1) * lanes[1:2, :]
    )


def pick(pos, axis, even, odd):
    return jnp.where(pos[axis] % 2 == 0, even, odd)


def send(pos, axis, low, high, even_ref, odd_ref):
    even_ref[...] = pick(pos, axis, high, low)
    odd_ref[...] = pick(pos, axis, low, high)


def received(sizes, pos, axis, even, odd):
    low = jnp.where(pos[axis] > 0, pick(pos, axis, odd, even), 0.0)
    high = jnp.where(pos[axis] < sizes[axis] - 1, pick(pos, axis, even, odd), 0.0)
    return low, high


def place(low, high, a, row):
    return jnp.where(row == 0, low[a : a + 1], jnp.where(row == N - 1, high[a : a + 1], 0.0))


def robin_tiles(sizes, pos, table, flags, classes, size):
    elems_z = flags.shape[1]
    coefficient = jnp.zeros(flags.shape, f32)
    for c in range(table.shape[1]):
        coefficient = jnp.where(classes[...] == c, table[:, c : c + 1], coefficient)
    element = lax.broadcasted_iota(jnp.int32, flags.shape, 1)
    sides = [
        pos[0] == 0, pos[0] == sizes[0] - 1, pos[1] == 0, pos[1] == sizes[1] - 1,
        element == 0, element == elems_z - 1,
    ]
    rows = []
    for bit, side in enumerate(sides):
        flagged = (flags[...] >> bit) % 2 == 1
        rows.append(jnp.where(flagged & side, coefficient, 0.0))
    rows += [jnp.zeros(flags.shape, f32)] * 2
    spread = lax.broadcasted_iota(jnp.int32, (elems_z, size), 1) // N == row_index((elems_z, size))
    faces = dot(jnp.concatenate(rows, 0), spread.astype(f32))
    node = lax.broadcasted_iota(jnp.int32, (1, size), 1) % N
    w = weights_1d()
    w_z = along((1, size), w, node)
    row = row_index((N, size))
    w_b = along((N, size), w, row)
    w_bz = w_b * w_z
    ends_z = jnp.where(node == 0, faces[4:5], 0.0) + jnp.where(node == N - 1, faces[5:6], 0.0)
    common = place(faces[2:3] * w_z, faces[3:4] * w_z, 0, row) + w_b * ends_z
    robin = [w[a] * common for a in range(N)]
    robin[0] += w_bz * faces[0:1]
    robin[N - 1] += w_bz * faces[1:2]
    return robin, w_bz


def field_kernel(sizes, source, k, flags, classes, table, even_out, odd_out,
                 v_ref, k_ref, flags_ref, classes_ref, table_ref, low, high, sems):
    pairs = (
        (flags, flags_ref), (classes, classes_ref), (table, table_ref), (source, v_ref), (k, k_ref),
    )
    copies = [pltpu.make_async_copy(*pair, sems.at[i]) for i, pair in enumerate(pairs)]
    for copy in copies:
        copy.start()
    for copy in copies[:3]:
        copy.wait()
    pos = position()
    robin, w_bz = robin_tiles(sizes, pos, table_ref, flags_ref, classes_ref, source.shape[1])
    for copy in copies[3:]:
        copy.wait()
    w = weights_1d()
    ws = [w[a] * w_bz * v for a, v in enumerate(tiles(v_ref))]
    wk = [w[a] * w_bz * v for a, v in enumerate(tiles(k_ref))]
    for i, field in enumerate((ws, wk, robin)):
        for a in range(N):
            low[N * i + a : N * i + a + 1, :] = field[a][0:1]
            high[N * i + a : N * i + a + 1, :] = field[a][N - 1 : N]
    send(pos, 1, low[...], high[...], even_out, odd_out)


def whole_field_kernel(sizes, source, k, flags, classes, table, ws_out, wk_out, robin_out):
    robin, w_bz = robin_tiles(sizes, position(), table, flags, classes, source.shape[1])
    w = weights_1d()
    store(robin_out, robin)
    store(ws_out, [w[a] * w_bz * v for a, v in enumerate(tiles(source))])
    store(wk_out, [w[a] * w_bz * v for a, v in enumerate(tiles(k))])


def fold_y_kernel(sizes, ws, wk, robin, odd, even, even_out, odd_out):
    pos = position()
    low, high = received(sizes, pos, 1, even[...], odd[...])
    row = row_index((N, ws.shape[1]))
    sides = []
    for a in (0, N - 1):
        part = [
            field[N * a : N * a + N, :] + place(low, high, N * i + a, row)
            for i, field in enumerate((ws, wk, robin))
        ]
        sides.append(jnp.concatenate(part + [wk[N * a : N * a + N, :]], 0))
    send(pos, 0, sides[0], sides[1], even_out, odd_out)


def prepare_kernel(sizes, ws, wk, robin, odd, even, lanes,
                   b_out, kx_out, ky_out, kz_out, advect_out, diagonal_out, inverse_out):
    pos = position()
    low, high = received(sizes, pos, 1, even[...], odd[...])
    shape = (N, ws.shape[1])
    row = row_index(shape)
    w = weights_1d()
    node = lax.broadcasted_iota(jnp.int32, (1, shape[1]), 1) % N
    copies_z = 1.0 + lanes[0:1, :] + lanes[1:2, :]
    shared_y = ((row == 0) & (pos[1] > 0)) | ((row == N - 1) & (pos[1] < sizes[1] - 1))
    copies_yz = jnp.where(shared_y, 2.0, 1.0) * copies_z
    weights_yz = along(shape, w, row) * along((1, shape[1]), w, node) * copies_yz
    inverse_yz = 1.0 / copies_yz
    for a in range(N):
        at = slice(N * a, N * a + N)
        summed = [
            field[at, :] + place(low, high, N * i + a, row) for i, field in enumerate((ws, wk, robin))
        ]
        b_out[at, :] = fold_z(summed[0], lanes)
        kz_out[at, :] = summed[1]
        kx_out[at, :] = fold_z(summed[1], lanes)
        ky_out[at, :] = fold_z(wk[at, :], lanes)
        copies_x = 1.0
        if a == 0:
            copies_x = jnp.where(pos[0] > 0, 2.0, 1.0)
        if a == N - 1:
            copies_x = jnp.where(pos[0] < sizes[0] - 1, 2.0, 1.0)
        weights_a = w[a] * weights_yz
        advect_out[at, :] = scan_speed * weights_a
        diagonal_out[at, :] = fold_z(summed[2], lanes) + mass_coef * copies_x * weights_a
        inverse_out[at, :] = inverse_yz * (1.0 / copies_x)


def contract(m, values):
    half = N // 2
    total = [values[b] + values[N - 1 - b] for b in range(half)]
    apart = [values[b] - values[N - 1 - b] for b in range(half)]
    out = [None] * N
    for a in range(half):
        even = sum(float((m[a][b] + m[a][N - 1 - b]) / 2) * total[b] for b in range(half))
        odd = sum(float((m[a][b] - m[a][N - 1 - b]) / 2) * apart[b] for b in range(half))
        out[a] = even + odd
        out[N - 1 - a] = odd - even
    return out


def rotations(m, row):
    return [along(row.shape, [float(m[b][(b + s) % N]) for b in range(N)], row) for s in range(N)]


def contract_rows(coefs, v):
    out = coefs[0] * v
    for s in range(1, N):
        out += coefs[s] * pltpu.roll(v, N - s, axis=0)
    return out


def operate(pos, v, kx, ky, advect, xy_out, sends, low, high):
    d = lagrange_derivative()
    k, speed = tiles(kx), tiles(advect)
    flux = [k[a] * g - speed[a] * v[a] for a, g in enumerate(contract(d, v))]
    x = contract(d.T, flux)
    send(pos, 0, x[0], x[N - 1], sends[0], sends[1])
    row = row_index(v[0].shape)
    forward, back = rotations(d, row), rotations(d.T, row)
    for a in range(N):
        at = slice(N * a, N * a + N)
        y = contract_rows(back, ky[at, :] * contract_rows(forward, v[a]))
        low[a : a + 1, :] = y[0:1]
        high[a : a + 1, :] = y[N - 1 : N]
        xy_out[at, :] = x[a] + y
    send(pos, 1, low[...], high[...], sends[2], sends[3])


def along_z(v, xy, kz, diagonal, forward_1, forward_2, back_1, back_2, lanes, q_out):
    rows, size = v.shape
    columns = [slice(i, i + LANES) for i in range(0, size, LANES)]
    grad = times(jnp.concatenate([v[:, c] for c in columns], 0), forward_1, forward_2)
    flux = [kz[:, c] * grad[i * rows : (i + 1) * rows] for i, c in enumerate(columns)]
    back = times(jnp.concatenate(flux, 0), back_1, back_2)
    back = jnp.concatenate([back[i * rows : (i + 1) * rows] for i in range(len(columns))], 1)
    q_out[...] = fold_z(back, lanes) + (xy[...] + diagonal[...] * v[...])


def assemble(sizes, pos, q, recv):
    x_even, x_odd, y_even, y_odd = (recv[ORDER.index(i)] for i in range(4))
    x_low, x_high = received(sizes, pos, 0, x_even[...], x_odd[...])
    y_low, y_high = received(sizes, pos, 1, y_even[...], y_odd[...])
    row = row_index(y_low.shape)
    out = [q[N * a : N * a + N, :] + place(y_low, y_high, a, row) for a in range(N)]
    out[0] += x_low
    out[N - 1] += x_high
    return out


def first_kernel(sizes, b_in, kx, ky_in, advect, odd, even, lanes,
                 b_out, ky_out, xy_out, *refs):
    pos = position()
    low, high = received(sizes, pos, 0, even[...], odd[...])
    b, ky = tiles(b_in), tiles(ky_in)
    for a, side in ((0, low), (N - 1, high)):
        b[a] += fold_z(side[0:N], lanes)
        ky[a] += fold_z(side[3 * N : 4 * N], lanes)
    store(b_out, b)
    store(ky_out, ky)
    operate(pos, b, kx, ky_out, advect, xy_out, refs[:4], *refs[4:])


def first_z_kernel(sizes, b, xy, kz_in, diagonal_in, odd, even, f1, f2, b1, b2, lanes,
                   kz_out, diagonal_out, q_out):
    pos = position()
    low, high = received(sizes, pos, 0, even[...], odd[...])
    kz_out[...] = kz_in[...]
    diagonal_out[...] = diagonal_in[...]
    for a, side in ((0, low), (N - 1, high)):
        at = slice(N * a, N * a + N)
        kz_out[at, :] += side[N : 2 * N]
        diagonal_out[at, :] += fold_z(side[2 * N : 3 * N], lanes)
    along_z(b, xy, kz_out, diagonal_out, f1, f2, b1, b2, lanes, q_out)


def dots_row(pairs, inverse, out):
    width = out.shape[-1]
    rows = []
    for u, v in pairs:
        product = sum(x * (y * m) for x, y, m in zip(u, v, inverse))
        product = sum(product[:, i : i + width] for i in range(0, product.shape[1], width))
        rows.append(jnp.sum(product, axis=0, keepdims=True))
    rows += [jnp.zeros_like(rows[0])] * (-len(rows) % N)
    sums = jnp.sum(jnp.concatenate(rows, 0), axis=1, keepdims=True)
    shape = (len(rows), width)
    lane = lax.broadcasted_iota(jnp.int32, shape, 1)
    row = jnp.sum(jnp.where(lane == row_index(shape), sums, 0.0), axis=0, keepdims=True)
    for i in range(out.shape[0]):
        out[i] = row


def totals(gathered, count):
    row = jnp.sum(gathered[...], axis=0)
    return [jnp.broadcast_to(row[:, i : i + 1], row.shape) for i in range(count)]


def wide(scalar, like):
    return jnp.concatenate([scalar] * (like.shape[1] // scalar.shape[1]), 1)


def inner_pairs(b, r, s, w, z):
    return [(b, r), (b, s), (b, w), (b, z), (w, r), (w, s), (r, z), (s, z), (w, w), (w, z), (z, z)]


def steps(g):
    br, bs, bw, bz, wr, ws, rz, sz, ww, wz, zz = g
    alpha = br / bs
    omega = (wr - alpha * (ws + rz) + alpha * alpha * sz) / (
        ww - 2.0 * alpha * wz + alpha * alpha * zz
    )
    rho_next = (br - alpha * bs) - omega * (bw - alpha * bz)
    beta = rho_next / br * (alpha / omega)
    return alpha, omega, beta


def apply_kernel(sizes, q, x0, x1, y0, y1, kx, ky, advect, v_out, xy_out, *refs):
    pos = position()
    v = assemble(sizes, pos, q, (x0, x1, y0, y1))
    store(v_out, v)
    operate(pos, v, kx, ky, advect, xy_out, refs[:4], *refs[4:])


def z_kernel(*refs):
    along_z(*refs)


def first_dots_kernel(b, s, z, inverse, row):
    b, s, z = tiles(b), tiles(s), tiles(z)
    dots_row([(b, b), (b, s), (b, z), (s, s), (s, z), (z, z)], tiles(inverse), row)


def update_kernel(sizes, gathered, s, z, az, q, x0, x1, y0, y1, kx, ky, advect,
                  z_out, aw_out, scalars, z_xy_out, aw_xy_out, *refs):
    pos = position()
    bb, bs, bz, ss, sz, zz = totals(gathered, 6)
    values = steps((bb, bs, bs, bz, bs, ss, bz, sz, ss, sz, zz))
    for i, value in enumerate(values):
        scalars[i : i + 1, :] = value
    alpha, omega, beta = (wide(value, s) for value in values)
    aaz = assemble(sizes, pos, q, (x0, x1, y0, y1))
    z, az = tiles(z), tiles(az)
    aw = [(z[i] - alpha * az[i]) - omega * (az[i] - alpha * aaz[i]) for i in range(N)]
    z_next = [aw[i] + beta * (z[i] - omega * az[i]) for i in range(N)]
    store(aw_out, aw)
    store(z_out, z_next)
    sends, sides = refs[:4], refs[4:]
    halves = [[ref.at[pl.ds(i * N, N)] for ref in sends] for i in range(2)]
    operate(pos, z_next, kx, ky, advect, z_xy_out, halves[0], *sides)
    operate(pos, aw, kx, ky, advect, aw_xy_out, halves[1], *sides)


def update_rest_kernel(scalars, b, s, z, az, z_next, inverse, x_out, r_out, p_out, s_out, w_out, row):
    alpha, omega, beta = (wide(scalars[i : i + 1, :], s) for i in range(3))
    fields = [], [], [], []
    for i in range(N):
        at = slice(N * i, N * i + N)
        b_, s_, z_, az_ = b[at, :], s[at, :], z[at, :], az[at, :]
        half, applied_half = b_ - alpha * s_, s_ - alpha * z_
        x_out[at, :] = alpha * b_ + omega * half
        r = half - omega * applied_half
        w = applied_half - omega * (z_ - alpha * az_)
        s_next = w + beta * (s_ - omega * z_)
        p_out[at, :] = r + beta * (b_ - omega * s_)
        r_out[at, :], w_out[at, :], s_out[at, :] = r, w, s_next
        for values, value in zip(fields, (b_, r, s_next, w)):
            values.append(value)
    dots_row(inner_pairs(*fields, tiles(z_next)), tiles(inverse), row)


def two_z_kernel(z, z_xy, aw, aw_xy, *refs):
    *shared, z_q_out, aw_q_out = refs
    along_z(z, z_xy, *shared, z_q_out)
    along_z(aw, aw_xy, *shared, aw_q_out)


def apply_two_kernel(sizes, z_q, aw_q, x0, x1, y0, y1, kx, ky, advect, az_out, aaw_out, xy_out, *refs):
    pos = position()
    halves = [[ref.at[pl.ds(i * N, N)] for ref in (x0, x1, y0, y1)] for i in range(2)]
    az = assemble(sizes, pos, z_q, halves[0])
    store(az_out, az)
    operate(pos, az, kx, ky, advect, xy_out, refs[:4], *refs[4:])
    store(aaw_out, assemble(sizes, pos, aw_q, halves[1]))


def second_kernel(sizes, gathered, b, x, r, p, s, w, z, az, aw, aaw, inverse, q, x0, x1, y0, y1,
                  x_out, r_out, p_out, s_out, w_out, z_out, row):
    pos = position()
    alpha, omega, beta = (wide(value, s) for value in steps(totals(gathered, 11)))
    aaz = assemble(sizes, pos, q, (x0, x1, y0, y1))
    fields = [], [], [], []
    for i in range(N):
        at = slice(N * i, N * i + N)
        r_, s_, w_, z_, az_ = r[at, :], s[at, :], w[at, :], z[at, :], az[at, :]
        applied_half = w_ - alpha * z_
        applied_twice = aw[at, :] - alpha * az_
        half = r_ - alpha * s_
        r_next = half - omega * applied_half
        x_out[at, :] = x[at, :] + alpha * p[at, :] + omega * half
        p_out[at, :] = r_next + beta * (p[at, :] - omega * s_)
        w_next = applied_half - omega * applied_twice
        aw_next = applied_twice - omega * (aaw[at, :] - alpha * aaz[i])
        s_next = w_next + beta * (s_ - omega * z_)
        z_next = aw_next + beta * (z_ - omega * az_)
        r_out[at, :], w_out[at, :], s_out[at, :], z_out[at, :] = r_next, w_next, s_next, z_next
        for values, value in zip(fields, (r_next, s_next, w_next, z_next)):
            values.append(value)
    dots_row(inner_pairs(tiles(b), *fields), tiles(inverse), row)


def last_kernel(gathered, r, p, s, w, z, x, x_out, r_out):
    alpha, omega, _ = steps(totals(gathered, 11))
    alpha, omega = wide(alpha, s), wide(omega, s)
    half = r[...] - alpha * s[...]
    x_out[...] = x[...] + alpha * p[...] + omega * half
    r_out[...] = half - omega * (w[...] - alpha * z[...])


def pairings(sizes):
    count_x, count_y = sizes
    grid = [(i, j) for i in range(count_x) for j in range(count_y)]
    number = lambda i, j: i * count_y + j
    step = lambda i: i + 1 if i % 2 else i - 1
    x_even = [(number(i, j), number(i ^ 1, j)) for i, j in grid]
    x_odd = [
        (number(i, j), number(step(i), j) if 0 < i < count_x - 1 else number(i, j ^ 1)) for i, j in grid
    ]
    y_even = [(number(i, j), number(i, j ^ 1)) for i, j in grid]
    y_odd = [
        (number(i, j), number(i, step(j)) if 0 < j < count_y - 1 else number(i ^ 1, j)) for i, j in grid
    ]
    return (x_even, x_odd), (y_even, y_odd)


def per_device(sizes, source, conductivity, robin_flags, htc_class, htc_table):
    shape = source.shape
    elems_z = robin_flags.shape[2]
    rows, size = shape[0] * shape[1], shape[2]
    assert robin_flags.shape[:2] == (1, 1) and size % LANES == 0
    assert sizes[0] % 2 == 0 and sizes[1] % 2 == 0
    devices = sizes[0] * sizes[1]
    *z_mats, lanes = constants(elems_z)
    x_pairs, y_pairs = pairings(sizes)

    def struct(n=rows):
        return jax.ShapeDtypeStruct((n, size), f32)

    field = struct()
    faces = [struct(N)] * 4
    row = jax.ShapeDtypeStruct((devices, 1, 128), f32)
    scalars = jax.ShapeDtypeStruct((N, 128), f32)
    side = [pltpu.VMEM((N, size), f32)] * 2

    def call(kernel, outs, *operands, scratch=(), hbm=0, limit=32, cost=0):
        specs = [HBM] * hbm + [VMEM] * (len(operands) - hbm)
        return pl.pallas_call(
            kernel,
            out_shape=outs,
            in_specs=specs,
            out_specs=[VMEM] * len(outs),
            scratch_shapes=list(scratch),
            compiler_params=pltpu.CompilerParams(vmem_limit_bytes=limit * 1024 * 1024),
            cost_estimate=pl.CostEstimate(flops=cost, bytes_accessed=cost, transcendentals=0)
            if cost
            else None,
        )(*operands)

    def permute(values, pairs):
        return lax.ppermute(values, ("gx", "gy"), pairs)

    def exchange(pairs, even, odd):
        return permute(odd, pairs[1]), permute(even, pairs[0])

    def swap(parts):
        x_odd = permute(parts[1], x_pairs[1])
        y_odd = permute(parts[3], y_pairs[1])
        x_even = permute(parts[0], x_pairs[0])
        recv = x_even, x_odd, permute(parts[2], y_pairs[0]), y_odd
        return tuple(recv[i] for i in ORDER)

    def spread(values):
        return lax.all_to_all(values, ("gx", "gy"), 0, 0)

    given = (
        source.reshape(rows, size), conductivity.reshape(rows, size),
        robin_flags.reshape(1, elems_z), htc_class.reshape(1, elems_z), htc_table.reshape(1, -1),
    )
    parts = call(
        functools.partial(field_kernel, sizes), [struct(3 * N)] * 2, *given,
        hbm=5,
        limit=60,
        scratch=[pltpu.VMEM(v.shape, v.dtype) for v in given]
        + [pltpu.VMEM((3 * N, size), f32)] * 2
        + [pltpu.SemaphoreType.DMA((5,))],
    )
    recv = exchange(y_pairs, *parts)
    ws, wk, robin = call(functools.partial(whole_field_kernel, sizes), [field] * 3, *given, cost=COST)
    parts = call(
        functools.partial(fold_y_kernel, sizes), [struct(4 * N)] * 2, ws, wk, robin, *recv
    )
    b, kx, ky, kz, advect, diagonal, inverse = call(
        functools.partial(prepare_kernel, sizes), [field] * 7, ws, wk, robin, *recv, lanes,
        cost=COST,
    )
    recv = exchange(x_pairs, *parts)
    b, ky, xy, *parts = call(
        functools.partial(first_kernel, sizes), [field] * 3 + faces,
        b, kx, ky, advect, *recv, lanes, scratch=side,
    )
    kz, diagonal, q = call(
        functools.partial(first_z_kernel, sizes), [field] * 3,
        b, xy, kz, diagonal, *recv, *z_mats, lanes, cost=COST,
    )
    coefs = (kx, ky, advect)
    z_args = (kz, diagonal, *z_mats, lanes)
    recv = swap(parts)

    def apply(q, recv):
        v, xy, *parts = call(
            functools.partial(apply_kernel, sizes), [field] * 2 + faces, q, *recv, *coefs, scratch=side
        )
        recv = swap(parts)
        (q,) = call(z_kernel, [field], v, xy, *z_args, cost=COST)
        return v, q, recv

    s, q, recv = apply(q, recv)
    z, q, recv = apply(q, recv)
    (products,) = call(first_dots_kernel, [row], b, s, z, inverse, cost=COST)
    gathered = spread(products)
    az, q, recv = apply(q, recv)
    z_next, aw, values, z_xy, aw_xy, *parts = call(
        functools.partial(update_kernel, sizes),
        [field] * 2 + [scalars] + [field] * 2 + [struct(2 * N)] * 4,
        gathered, s, z, az, q, *recv, *coefs, scratch=side,
    )
    recv = swap(parts)
    x, r, p, s, w, products = call(
        update_rest_kernel, [field] * 5 + [row], values, b, s, z, az, z_next, inverse, cost=COST
    )
    gathered = spread(products)
    z = z_next
    z_q, aw_q = call(two_z_kernel, [field] * 2, z, z_xy, aw, aw_xy, *z_args, cost=COST)
    az, aaw, xy, *parts = call(
        functools.partial(apply_two_kernel, sizes), [field] * 3 + faces,
        z_q, aw_q, *recv, *coefs, scratch=side,
    )
    recv = swap(parts)
    (q,) = call(z_kernel, [field], az, xy, *z_args, cost=COST)
    x, r, p, s, w, z, products = call(
        functools.partial(second_kernel, sizes), [field] * 6 + [row],
        gathered, b, x, r, p, s, w, z, az, aw, aaw, inverse, q, *recv,
    )
    x, r = call(last_kernel, [field] * 2, spread(products), r, p, s, w, z, x)
    return x.reshape(shape), r.reshape(shape)


def solution(mesh):
    sizes = (mesh.shape["gx"], mesh.shape["gy"])
    field = P("gx", "gy", None)
    return jax.shard_map(
        functools.partial(per_device, sizes),
        mesh=mesh,
        in_specs=(field, field, field, field, P()),
        out_specs=(field, field),
        check_vma=False,
    )
```

```python
import functools

import jax
import jax.numpy as jnp
import numpy as np
from jax import lax
from jax.experimental import pallas as pl
from jax.experimental.pallas import tpu as pltpu
from jax.sharding import PartitionSpec as P

ITERS = 3
N = 8

gll_points = (
    -1.0,
    -0.8717401485096066,
    -0.5917001814331423,
    -0.2092992179024789,
    0.2092992179024789,
    0.5917001814331423,
    0.8717401485096066,
    1.0,
)
gll_weights = (
    0.03571428571428571,
    0.21070422714350603,
    0.3411226924835044,
    0.4124587946587038,
    0.4124587946587038,
    0.3411226924835044,
    0.21070422714350603,
    0.03571428571428571,
)
mass_coef = 0.2
scan_speed = 2.0
f32 = jnp.float32
VMEM = pl.BlockSpec(memory_space=pltpu.VMEM)
HBM = pl.BlockSpec(memory_space=pl.ANY)
COST = 1 << 20
LANES = 128
ORDER = (3, 0, 1, 2)
dot = functools.partial(jnp.dot, precision=lax.Precision.HIGHEST, preferred_element_type=f32)


def lagrange_derivative():
    points = np.array(gll_points)
    barycentric = np.array(
        [1.0 / np.prod([points[j] - points[m] for m in range(N) if m != j]) for j in range(N)]
    )
    derivative = np.zeros((N, N))
    for a in range(N):
        for b in range(N):
            if a != b:
                derivative[a, b] = barycentric[b] / barycentric[a] / (points[a] - points[b])
        derivative[a, a] = -np.sum(derivative[a])
    return derivative.astype(np.float32)


def pieces(v):
    high = v.astype(jnp.bfloat16)
    rest = v - high.astype(f32)
    middle = rest.astype(jnp.bfloat16)
    return high, middle, (rest - middle.astype(f32)).astype(jnp.bfloat16)


def stacked(m):
    high = m.astype(jnp.bfloat16).astype(np.float32)
    middle = (m - high).astype(jnp.bfloat16).astype(np.float32)
    low = m - high - middle
    both = np.concatenate([high, middle], 1)
    return [
        jnp.asarray(np.concatenate([both, both], 0), jnp.bfloat16),
        jnp.asarray(np.concatenate([low, high], 0), jnp.bfloat16),
    ]


def constants(elems_z):
    z_back = np.kron(np.eye(LANES // N, dtype=np.float32), lagrange_derivative())
    lane = np.arange(N * elems_z)
    low = (lane % N == 0) & (lane > 0)
    high = (lane % N == N - 1) & (lane < N * elems_z - 1)
    lanes = np.stack([low, high] + [0 * lane] * 6).astype(np.float32)
    return stacked(z_back.T) + stacked(z_back) + [jnp.asarray(lanes)]


def times(v, first, second):
    high, middle, low = pieces(v)
    product = functools.partial(jnp.dot, preferred_element_type=f32)
    large = product(jnp.concatenate([high, middle], 1), first[...])
    small = product(jnp.concatenate([high, low], 1), second[...])
    return (large[:, :LANES] + large[:, LANES:]) + small


def weights_1d():
    return [float(np.float32(x)) for x in gll_weights]


def position():
    return lax.axis_index("gx"), lax.axis_index("gy")


def tiles(ref):
    return [ref[N * a : N * a + N, :] for a in range(N)]


def store(ref, values):
    for a in range(N):
        ref[N * a : N * a + N, :] = values[a]


def row_index(shape):
    return lax.broadcasted_iota(jnp.int32, shape, 0)


def along(shape, values, index):
    out = jnp.full(shape, values[0], f32)
    for i in range(1, len(values)):
        out = jnp.where(index == i, values[i], out)
    return out


def fold_z(v, lanes):
    size = v.shape[1]
    return (
        v
        + pltpu.roll(v, 1, axis=1) * lanes[0:1, :]
        + pltpu.roll(v, size - 1, axis=1) * lanes[1:2, :]
    )


def pick(pos, axis, even, odd):
    return jnp.where(pos[axis] % 2 == 0, even, odd)


def send(pos, axis, low, high, even_ref, odd_ref):
    even_ref[...] = pick(pos, axis, high, low)
    odd_ref[...] = pick(pos, axis, low, high)


def received(sizes, pos, axis, even, odd):
    low = jnp.where(pos[axis] > 0, pick(pos, axis, odd, even), 0.0)
    high = jnp.where(pos[axis] < sizes[axis] - 1, pick(pos, axis, even, odd), 0.0)
    return low, high


def place(low, high, a, row):
    return jnp.where(row == 0, low[a : a + 1], jnp.where(row == N - 1, high[a : a + 1], 0.0))


def robin_tiles(sizes, pos, table, flags, classes, size):
    elems_z = flags.shape[1]
    coefficient = jnp.zeros(flags.shape, f32)
    for c in range(table.shape[1]):
        coefficient = jnp.where(classes[...] == c, table[:, c : c + 1], coefficient)
    element = lax.broadcasted_iota(jnp.int32, flags.shape, 1)
    sides = [
        pos[0] == 0, pos[0] == sizes[0] - 1, pos[1] == 0, pos[1] == sizes[1] - 1,
        element == 0, element == elems_z - 1,
    ]
    rows = []
    for bit, side in enumerate(sides):
        flagged = (flags[...] >> bit) % 2 == 1
        rows.append(jnp.where(flagged & side, coefficient, 0.0))
    rows += [jnp.zeros(flags.shape, f32)] * 2
    spread = lax.broadcasted_iota(jnp.int32, (elems_z, size), 1) // N == row_index((elems_z, size))
    faces = dot(jnp.concatenate(rows, 0), spread.astype(f32))
    node = lax.broadcasted_iota(jnp.int32, (1, size), 1) % N
    w = weights_1d()
    w_z = along((1, size), w, node)
    row = row_index((N, size))
    w_b = along((N, size), w, row)
    w_bz = w_b * w_z
    ends_z = jnp.where(node == 0, faces[4:5], 0.0) + jnp.where(node == N - 1, faces[5:6], 0.0)
    common = place(faces[2:3] * w_z, faces[3:4] * w_z, 0, row) + w_b * ends_z
    robin = [w[a] * common for a in range(N)]
    robin[0] += w_bz * faces[0:1]
    robin[N - 1] += w_bz * faces[1:2]
    return robin, w_bz


def field_kernel(sizes, source, k, flags, classes, table, even_out, odd_out,
                 v_ref, k_ref, flags_ref, classes_ref, table_ref, low, high, sems):
    pairs = (
        (flags, flags_ref), (classes, classes_ref), (table, table_ref), (source, v_ref), (k, k_ref),
    )
    copies = [pltpu.make_async_copy(*pair, sems.at[i]) for i, pair in enumerate(pairs)]
    for copy in copies:
        copy.start()
    for copy in copies[:3]:
        copy.wait()
    pos = position()
    robin, w_bz = robin_tiles(sizes, pos, table_ref, flags_ref, classes_ref, source.shape[1])
    for copy in copies[3:]:
        copy.wait()
    w = weights_1d()
    ws = [w[a] * w_bz * v for a, v in enumerate(tiles(v_ref))]
    wk = [w[a] * w_bz * v for a, v in enumerate(tiles(k_ref))]
    for i, field in enumerate((ws, wk, robin)):
        for a in range(N):
            low[N * i + a : N * i + a + 1, :] = field[a][0:1]
            high[N * i + a : N * i + a + 1, :] = field[a][N - 1 : N]
    send(pos, 1, low[...], high[...], even_out, odd_out)


def whole_field_kernel(sizes, source, k, flags, classes, table, ws_out, wk_out, robin_out):
    robin, w_bz = robin_tiles(sizes, position(), table, flags, classes, source.shape[1])
    w = weights_1d()
    store(robin_out, robin)
    store(ws_out, [w[a] * w_bz * v for a, v in enumerate(tiles(source))])
    store(wk_out, [w[a] * w_bz * v for a, v in enumerate(tiles(k))])


def fold_y_kernel(sizes, ws, wk, robin, odd, even, even_out, odd_out):
    pos = position()
    low, high = received(sizes, pos, 1, even[...], odd[...])
    row = row_index((N, ws.shape[1]))
    sides = []
    for a in (0, N - 1):
        part = [
            field[N * a : N * a + N, :] + place(low, high, N * i + a, row)
            for i, field in enumerate((ws, wk, robin))
        ]
        sides.append(jnp.concatenate(part + [wk[N * a : N * a + N, :]], 0))
    send(pos, 0, sides[0], sides[1], even_out, odd_out)


def prepare_kernel(sizes, ws, wk, robin, odd, even, lanes,
                   b_out, kx_out, ky_out, kz_out, advect_out, diagonal_out, inverse_out):
    pos = position()
    low, high = received(sizes, pos, 1, even[...], odd[...])
    shape = (N, ws.shape[1])
    row = row_index(shape)
    w = weights_1d()
    node = lax.broadcasted_iota(jnp.int32, (1, shape[1]), 1) % N
    copies_z = 1.0 + lanes[0:1, :] + lanes[1:2, :]
    shared_y = ((row == 0) & (pos[1] > 0)) | ((row == N - 1) & (pos[1] < sizes[1] - 1))
    copies_yz = jnp.where(shared_y, 2.0, 1.0) * copies_z
    weights_yz = along(shape, w, row) * along((1, shape[1]), w, node) * copies_yz
    inverse_yz = 1.0 / copies_yz
    for a in range(N):
        at = slice(N * a, N * a + N)
        summed = [
            field[at, :] + place(low, high, N * i + a, row) for i, field in enumerate((ws, wk, robin))
        ]
        b_out[at, :] = fold_z(summed[0], lanes)
        kz_out[at, :] = summed[1]
        kx_out[at, :] = fold_z(summed[1], lanes)
        ky_out[at, :] = fold_z(wk[at, :], lanes)
        copies_x = 1.0
        if a == 0:
            copies_x = jnp.where(pos[0] > 0, 2.0, 1.0)
        if a == N - 1:
            copies_x = jnp.where(pos[0] < sizes[0] - 1, 2.0, 1.0)
        weights_a = w[a] * weights_yz
        advect_out[at, :] = scan_speed * weights_a
        diagonal_out[at, :] = fold_z(summed[2], lanes) + mass_coef * copies_x * weights_a
        inverse_out[at, :] = inverse_yz * (1.0 / copies_x)


def contract(m, values):
    half = N // 2
    total = [values[b] + values[N - 1 - b] for b in range(half)]
    apart = [values[b] - values[N - 1 - b] for b in range(half)]
    out = [None] * N
    for a in range(half):
        even = sum(float((m[a][b] + m[a][N - 1 - b]) / 2) * total[b] for b in range(half))
        odd = sum(float((m[a][b] - m[a][N - 1 - b]) / 2) * apart[b] for b in range(half))
        out[a] = even + odd
        out[N - 1 - a] = odd - even
    return out


def rotations(m, row):
    return [along(row.shape, [float(m[b][(b + s) % N]) for b in range(N)], row) for s in range(N)]


def contract_rows(coefs, v):
    out = coefs[0] * v
    for s in range(1, N):
        out += coefs[s] * pltpu.roll(v, N - s, axis=0)
    return out


def operate(pos, v, kx, ky, advect, xy_out, sends, low, high):
    d = lagrange_derivative()
    k, speed = tiles(kx), tiles(advect)
    flux = [k[a] * g - speed[a] * v[a] for a, g in enumerate(contract(d, v))]
    x = contract(d.T, flux)
    send(pos, 0, x[0], x[N - 1], sends[0], sends[1])
    row = row_index(v[0].shape)
    forward, back = rotations(d, row), rotations(d.T, row)
    for a in range(N):
        at = slice(N * a, N * a + N)
        y = contract_rows(back, ky[at, :] * contract_rows(forward, v[a]))
        low[a : a + 1, :] = y[0:1]
        high[a : a + 1, :] = y[N - 1 : N]
        xy_out[at, :] = x[a] + y
    send(pos, 1, low[...], high[...], sends[2], sends[3])


def along_z(v, xy, kz, diagonal, forward_1, forward_2, back_1, back_2, lanes, q_out):
    rows, size = v.shape
    columns = [slice(i, i + LANES) for i in range(0, size, LANES)]
    grad = times(jnp.concatenate([v[:, c] for c in columns], 0), forward_1, forward_2)
    flux = [kz[:, c] * grad[i * rows : (i + 1) * rows] for i, c in enumerate(columns)]
    back = times(jnp.concatenate(flux, 0), back_1, back_2)
    back = jnp.concatenate([back[i * rows : (i + 1) * rows] for i in range(len(columns))], 1)
    q_out[...] = fold_z(back, lanes) + (xy[...] + diagonal[...] * v[...])


def assemble(sizes, pos, q, recv):
    x_even, x_odd, y_even, y_odd = (recv[ORDER.index(i)] for i in range(4))
    x_low, x_high = received(sizes, pos, 0, x_even[...], x_odd[...])
    y_low, y_high = received(sizes, pos, 1, y_even[...], y_odd[...])
    row = row_index(y_low.shape)
    out = [q[N * a : N * a + N, :] + place(y_low, y_high, a, row) for a in range(N)]
    out[0] += x_low
    out[N - 1] += x_high
    return out


def first_kernel(sizes, b_in, kx, ky_in, advect, odd, even, lanes,
                 b_out, ky_out, xy_out, *refs):
    pos = position()
    low, high = received(sizes, pos, 0, even[...], odd[...])
    b, ky = tiles(b_in), tiles(ky_in)
    for a, side in ((0, low), (N - 1, high)):
        b[a] += fold_z(side[0:N], lanes)
        ky[a] += fold_z(side[3 * N : 4 * N], lanes)
    store(b_out, b)
    store(ky_out, ky)
    operate(pos, b, kx, ky_out, advect, xy_out, refs[:4], *refs[4:])


def first_z_kernel(sizes, b, xy, kz_in, diagonal_in, odd, even, f1, f2, b1, b2, lanes,
                   kz_out, diagonal_out, q_out):
    pos = position()
    low, high = received(sizes, pos, 0, even[...], odd[...])
    kz_out[...] = kz_in[...]
    diagonal_out[...] = diagonal_in[...]
    for a, side in ((0, low), (N - 1, high)):
        at = slice(N * a, N * a + N)
        kz_out[at, :] += side[N : 2 * N]
        diagonal_out[at, :] += fold_z(side[2 * N : 3 * N], lanes)
    along_z(b, xy, kz_out, diagonal_out, f1, f2, b1, b2, lanes, q_out)


def dots_row(pairs, inverse, first=0):
    shape = (N, LANES)
    lane = lax.broadcasted_iota(jnp.int32, shape, 1)
    row = jnp.zeros(shape, f32)
    scaled = {}
    for i, (u, v) in enumerate(pairs):
        if id(u) not in scaled:
            scaled[id(u)] = [x * m for x, m in zip(u, inverse)]
        product = sum(x * y for x, y in zip(scaled[id(u)], v))
        product = sum(product[:, j : j + LANES] for j in range(0, product.shape[1], LANES))
        row = jnp.where(lane == first + i, jnp.sum(product, axis=1, keepdims=True), row)
    return jnp.sum(row, axis=0, keepdims=True)


def for_all(row, out):
    for i in range(out.shape[0]):
        out[i] = row


def totals(gathered, count):
    row = jnp.sum(gathered[...], axis=0)
    return [jnp.broadcast_to(row[:, i : i + 1], row.shape) for i in range(count)]


def wide(scalar, like):
    return jnp.concatenate([scalar] * (like.shape[1] // scalar.shape[1]), 1)


def steps(br, bs, bw, bz, wr, ws, zr, zs, ww, wz, zz):
    alpha = br / bs
    omega = (wr - alpha * (ws + zr) + alpha * alpha * zs) / (
        ww - 2.0 * alpha * wz + alpha * alpha * zz
    )
    rho_next = (br - alpha * bs) - omega * (bw - alpha * bz)
    beta = rho_next / br * (alpha / omega)
    return alpha, omega, beta


def early_pairs(b, e):
    return [(e[i], b) for i in range(6)] + [(e[i], e[j]) for i in range(6) for j in range(i, 6)]


def late_pairs(b, e):
    return [(e[i], b) for i in (6, 7)] + [(e[j], e[i]) for j in (6, 7) for i in range(j + 1)]


EARLY = 27


def last_steps(sums):
    keys = early_pairs("b", range(6)) + late_pairs("b", range(8))
    value = dict(zip(keys, sums))
    g = lambda i, j: value[i, j] if (i, j) in value else value[j, i]
    second = steps(
        g(0, "b"), g(1, "b"), g(2, "b"), g(3, "b"),
        g(2, 0), g(2, 1), g(3, 0), g(3, 1), g(2, 2), g(2, 3), g(3, 3),
    )
    alpha, omega, beta = second
    one, cross = jnp.ones_like(alpha), alpha * omega
    both = -alpha - beta * omega
    r = {0: one, 1: -alpha, 2: -omega, 3: cross}
    w = {2: one, 3: -alpha, 4: -omega, 5: cross}
    s = {1: beta, 2: one, 3: both, 4: -omega, 5: cross}
    z = {3: beta, 4: one, 5: both, 6: -omega, 7: cross}
    with_b = lambda u: sum(c * g(i, "b") for i, c in u.items())
    times = lambda u: {i: sum(c * g(i, j) for j, c in u.items()) for i in range(8)}
    inner = lambda image, u: sum(c * image[i] for i, c in u.items())
    gw, gz = times(w), times(z)
    third = steps(
        with_b(r), with_b(s), with_b(w), with_b(z),
        inner(gw, r), inner(gw, s), inner(gz, r), inner(gz, s),
        inner(gw, w), inner(gw, z), inner(gz, z),
    )
    return second, third


def apply_kernel(sizes, q, x0, x1, y0, y1, kx, ky, advect, v_out, xy_out, *refs):
    pos = position()
    v = assemble(sizes, pos, q, (x0, x1, y0, y1))
    store(v_out, v)
    operate(pos, v, kx, ky, advect, xy_out, refs[:4], *refs[4:])


def z_kernel(*refs):
    along_z(*refs)


def first_dots_kernel(sizes, b, s, inverse, q, x0, x1, y0, y1, kx, ky, advect, z_out, xy_out, *refs):
    *sends, row_out, low, high, row, sem = refs
    pos = position()
    z = assemble(sizes, pos, q, (x0, x1, y0, y1))
    store(z_out, z)
    b, s = tiles(b), tiles(s)
    for_all(dots_row([(b, b), (b, s), (b, z), (s, s), (s, z), (z, z)], tiles(inverse)), row)
    copy = pltpu.make_async_copy(row, row_out, sem)
    copy.start()
    operate(pos, z, kx, ky, advect, xy_out, sends, low, high)
    copy.wait()


def update_kernel(sizes, gathered, s, z, az, q, x0, x1, y0, y1, kx, ky, advect,
                  z_out, aw_out, scalars, xy_out, *refs):
    pos = position()
    bb, bs, bz, ss, sz, zz = totals(gathered, 6)
    values = steps(bb, bs, bs, bz, bs, ss, bz, sz, ss, sz, zz)
    for i, value in enumerate(values):
        scalars[i : i + 1, :] = value
    alpha, omega, beta = (wide(value, s) for value in values)
    aaz = assemble(sizes, pos, q, (x0, x1, y0, y1))
    z, az = tiles(z), tiles(az)
    aw = [(z[i] - alpha * az[i]) - omega * (az[i] - alpha * aaz[i]) for i in range(N)]
    z_next = [aw[i] + beta * (z[i] - omega * az[i]) for i in range(N)]
    store(aw_out, aw)
    store(z_out, z_next)
    operate(pos, z_next, kx, ky, advect, xy_out, refs[:4], *refs[4:])


def update_rest_kernel(scalars, b, s, z, az, x_out, r_out, p_out, s_out, w_out):
    alpha, omega, beta = (wide(scalars[i : i + 1, :], s) for i in range(3))
    for i in range(N):
        at = slice(N * i, N * i + N)
        b_, s_, z_, az_ = b[at, :], s[at, :], z[at, :], az[at, :]
        half, applied_half = b_ - alpha * s_, s_ - alpha * z_
        x_out[at, :] = alpha * b_ + omega * half
        r = half - omega * applied_half
        w = applied_half - omega * (z_ - alpha * az_)
        p_out[at, :] = r + beta * (b_ - omega * s_)
        r_out[at, :], w_out[at, :], s_out[at, :] = r, w, w + beta * (s_ - omega * z_)


def two_z_kernel(z, z_xy, aw, kx, ky, advect, *refs):
    *shared, z_q_out, aw_q_out, f0, f1, f2, f3, xy, low, high = refs
    along_z(z, z_xy, *shared, z_q_out)
    operate(position(), tiles(aw), kx, ky, advect, xy, (f0, f1, f2, f3), low, high)
    along_z(aw, xy, *shared, aw_q_out)


def apply_beside_kernel(sizes, f0, f1, f2, f3, q, x0, x1, y0, y1, kx, ky, advect, v_out, xy_out, *refs):
    sends, sides = refs[:4], refs[4:]
    pos = position()
    v = assemble(sizes, pos, q, (x0, x1, y0, y1))
    store(v_out, v)
    operate(pos, v, kx, ky, advect, xy_out, [ref.at[pl.ds(0, N)] for ref in sends], *sides)
    for ref, face in zip(sends, (f0, f1, f2, f3)):
        ref[N : 2 * N, :] = face[...]


def early_dots_kernel(b, r, s, w, z, aw, az, inverse, row):
    e = [tiles(ref) for ref in (r, s, w, z, aw, az)]
    row[...] = dots_row(early_pairs(tiles(b), e), tiles(inverse))


def late_dots_kernel(sizes, b, r, s, w, z, aw, az, inverse, early, aaz_q, aaw_q, x0, x1, y0, y1,
                     aaw_out, aaz_out, row):
    pos = position()
    halves = [[ref.at[pl.ds(i * N, N)] for ref in (x0, x1, y0, y1)] for i in range(2)]
    aaz = assemble(sizes, pos, aaz_q, halves[0])
    aaw = assemble(sizes, pos, aaw_q, halves[1])
    store(aaz_out, aaz)
    store(aaw_out, aaw)
    e = [tiles(ref) for ref in (r, s, w, z, aw, az)] + [aaw, aaz]
    for_all(early[...] + dots_row(late_pairs(tiles(b), e), tiles(inverse), EARLY), row)


def last_kernel(gathered, x, p, r, s, w, z, aw, az, aaw, aaz, x_out, r_out):
    second, third = last_steps(totals(gathered, EARLY + 17))
    alpha, omega, beta = (wide(value, s) for value in second)
    last_alpha, last_omega, _ = (wide(value, s) for value in third)
    for i in range(N):
        at = slice(N * i, N * i + N)
        p_, s_, z_, az_ = p[at, :], s[at, :], z[at, :], az[at, :]
        half, applied_half = r[at, :] - alpha * s_, w[at, :] - alpha * z_
        applied_twice = aw[at, :] - alpha * az_
        r_next = half - omega * applied_half
        w_next = applied_half - omega * applied_twice
        aw_next = applied_twice - omega * (aaw[at, :] - alpha * aaz[at, :])
        p_next = r_next + beta * (p_ - omega * s_)
        s_next = w_next + beta * (s_ - omega * z_)
        z_next = aw_next + beta * (z_ - omega * az_)
        last_half = r_next - last_alpha * s_next
        x_out[at, :] = (x[at, :] + alpha * p_ + omega * half) + (
            last_alpha * p_next + last_omega * last_half
        )
        r_out[at, :] = last_half - last_omega * (w_next - last_alpha * z_next)


def pairings(sizes):
    count_x, count_y = sizes
    grid = [(i, j) for i in range(count_x) for j in range(count_y)]
    number = lambda i, j: i * count_y + j
    step = lambda i: i + 1 if i % 2 else i - 1
    x_even = [(number(i, j), number(i ^ 1, j)) for i, j in grid]
    x_odd = [
        (number(i, j), number(step(i), j) if 0 < i < count_x - 1 else number(i, j ^ 1)) for i, j in grid
    ]
    y_even = [(number(i, j), number(i, j ^ 1)) for i, j in grid]
    y_odd = [
        (number(i, j), number(i, step(j)) if 0 < j < count_y - 1 else number(i ^ 1, j)) for i, j in grid
    ]
    return (x_even, x_odd), (y_even, y_odd)


def per_device(sizes, source, conductivity, robin_flags, htc_class, htc_table):
    shape = source.shape
    elems_z = robin_flags.shape[2]
    rows, size = shape[0] * shape[1], shape[2]
    assert robin_flags.shape[:2] == (1, 1) and size % LANES == 0
    assert sizes[0] % 2 == 0 and sizes[1] % 2 == 0
    devices = sizes[0] * sizes[1]
    *z_mats, lanes = constants(elems_z)
    x_pairs, y_pairs = pairings(sizes)

    def struct(n=rows):
        return jax.ShapeDtypeStruct((n, size), f32)

    field = struct()
    faces = [struct(N)] * 4
    row = jax.ShapeDtypeStruct((devices, 1, 128), f32)
    scalars = jax.ShapeDtypeStruct((N, 128), f32)
    side = [pltpu.VMEM((N, size), f32)] * 2
    row_side = [pltpu.VMEM(row.shape, f32), pltpu.SemaphoreType.DMA]

    def call(kernel, outs, *operands, scratch=(), hbm=0, limit=32, cost=0, hbm_out=0):
        specs = [HBM] * hbm + [VMEM] * (len(operands) - hbm)
        return pl.pallas_call(
            kernel,
            out_shape=outs,
            in_specs=specs,
            out_specs=[VMEM] * (len(outs) - hbm_out) + [HBM] * hbm_out,
            scratch_shapes=list(scratch),
            compiler_params=pltpu.CompilerParams(vmem_limit_bytes=limit * 1024 * 1024),
            cost_estimate=pl.CostEstimate(flops=cost, bytes_accessed=cost, transcendentals=0)
            if cost
            else None,
        )(*operands)

    def permute(values, pairs):
        return lax.ppermute(values, ("gx", "gy"), pairs)

    def exchange(pairs, even, odd):
        return permute(odd, pairs[1]), permute(even, pairs[0])

    def swap(parts):
        x_odd = permute(parts[1], x_pairs[1])
        y_odd = permute(parts[3], y_pairs[1])
        x_even = permute(parts[0], x_pairs[0])
        recv = x_even, x_odd, permute(parts[2], y_pairs[0]), y_odd
        return tuple(recv[i] for i in ORDER)

    def spread(values):
        return lax.all_to_all(values, ("gx", "gy"), 0, 0)

    given = (
        source.reshape(rows, size), conductivity.reshape(rows, size),
        robin_flags.reshape(1, elems_z), htc_class.reshape(1, elems_z), htc_table.reshape(1, -1),
    )
    parts = call(
        functools.partial(field_kernel, sizes), [struct(3 * N)] * 2, *given,
        hbm=5,
        limit=60,
        scratch=[pltpu.VMEM(v.shape, v.dtype) for v in given]
        + [pltpu.VMEM((3 * N, size), f32)] * 2
        + [pltpu.SemaphoreType.DMA((5,))],
    )
    recv = exchange(y_pairs, *parts)
    ws, wk, robin = call(functools.partial(whole_field_kernel, sizes), [field] * 3, *given, cost=COST)
    parts = call(
        functools.partial(fold_y_kernel, sizes), [struct(4 * N)] * 2, ws, wk, robin, *recv
    )
    b, kx, ky, kz, advect, diagonal, inverse = call(
        functools.partial(prepare_kernel, sizes), [field] * 7, ws, wk, robin, *recv, lanes,
        cost=COST,
    )
    recv = exchange(x_pairs, *parts)
    b, ky, xy, *parts = call(
        functools.partial(first_kernel, sizes), [field] * 3 + faces,
        b, kx, ky, advect, *recv, lanes, scratch=side,
    )
    kz, diagonal, q = call(
        functools.partial(first_z_kernel, sizes), [field] * 3,
        b, xy, kz, diagonal, *recv, *z_mats, lanes, cost=COST,
    )
    coefs = (kx, ky, advect)
    z_args = (kz, diagonal, *z_mats, lanes)
    recv = swap(parts)

    def apply(q, recv):
        v, xy, *parts = call(
            functools.partial(apply_kernel, sizes), [field] * 2 + faces, q, *recv, *coefs, scratch=side
        )
        recv = swap(parts)
        (q,) = call(z_kernel, [field], v, xy, *z_args, cost=COST)
        return v, q, recv

    s, q, recv = apply(q, recv)
    z, xy, *parts, products = call(
        functools.partial(first_dots_kernel, sizes), [field] * 2 + faces + [row],
        b, s, inverse, q, *recv, *coefs, scratch=side + row_side, hbm_out=1,
    )
    gathered = spread(products)
    recv = swap(parts)
    (q,) = call(z_kernel, [field], z, xy, *z_args, cost=COST)
    az, q, recv = apply(q, recv)
    z_next, aw, values, z_xy, *parts = call(
        functools.partial(update_kernel, sizes),
        [field] * 2 + [scalars] + [field] + faces,
        gathered, s, z, az, q, *recv, *coefs, scratch=side,
    )
    recv = swap(parts)
    x, r, p, s, w = call(update_rest_kernel, [field] * 5, values, b, s, z, az, cost=COST)
    z = z_next
    z_q, aw_q, *aw_parts = call(
        two_z_kernel, [field] * 2 + faces, z, z_xy, aw, *coefs, *z_args,
        cost=COST, scratch=[pltpu.VMEM((rows, size), f32)] + side,
    )
    az, xy, *parts = call(
        functools.partial(apply_beside_kernel, sizes), [field] * 2 + [struct(2 * N)] * 4,
        *aw_parts, z_q, *recv, *coefs, scratch=side,
    )
    recv = swap(parts)
    (q,) = call(z_kernel, [field], az, xy, *z_args, cost=COST)
    (early,) = call(
        early_dots_kernel, [jax.ShapeDtypeStruct((1, LANES), f32)], b, r, s, w, z, aw, az, inverse, cost=COST
    )
    aaw, aaz, products = call(
        functools.partial(late_dots_kernel, sizes), [field] * 2 + [row],
        b, r, s, w, z, aw, az, inverse, early, q, aw_q, *recv,
    )
    x, r = call(
        last_kernel, [field] * 2, spread(products), x, p, r, s, w, z, aw, az, aaw, aaz
    )
    return x.reshape(shape), r.reshape(shape)


def solution(mesh):
    sizes = (mesh.shape["gx"], mesh.shape["gy"])
    field = P("gx", "gy", None)
    return jax.shard_map(
        functools.partial(per_device, sizes),
        mesh=mesh,
        in_specs=(field, field, field, field, P()),
        out_specs=(field, field),
        check_vma=False,
    )
```

```python
import functools

import jax
import jax.numpy as jnp
import numpy as np
from jax import lax
from jax.experimental import pallas as pl
from jax.experimental.pallas import tpu as pltpu
from jax.sharding import PartitionSpec as P

ITERS = 3
N = 8

gll_points = (
    -1.0,
    -0.8717401485096066,
    -0.5917001814331423,
    -0.2092992179024789,
    0.2092992179024789,
    0.5917001814331423,
    0.8717401485096066,
    1.0,
)
gll_weights = (
    0.03571428571428571,
    0.21070422714350603,
    0.3411226924835044,
    0.4124587946587038,
    0.4124587946587038,
    0.3411226924835044,
    0.21070422714350603,
    0.03571428571428571,
)
mass_coef = 0.2
scan_speed = 2.0
f32 = jnp.float32
VMEM = pl.BlockSpec(memory_space=pltpu.VMEM)
HBM = pl.BlockSpec(memory_space=pl.ANY)
COST = 1 << 20
LANES = 128
ORDER = (3, 0, 1, 2)
dot = functools.partial(jnp.dot, precision=lax.Precision.HIGHEST, preferred_element_type=f32)


def lagrange_derivative():
    points = np.array(gll_points)
    barycentric = np.array(
        [1.0 / np.prod([points[j] - points[m] for m in range(N) if m != j]) for j in range(N)]
    )
    derivative = np.zeros((N, N))
    for a in range(N):
        for b in range(N):
            if a != b:
                derivative[a, b] = barycentric[b] / barycentric[a] / (points[a] - points[b])
        derivative[a, a] = -np.sum(derivative[a])
    return derivative.astype(np.float32)


def pieces(v):
    high = v.astype(jnp.bfloat16)
    rest = v - high.astype(f32)
    middle = rest.astype(jnp.bfloat16)
    return high, middle, (rest - middle.astype(f32)).astype(jnp.bfloat16)


def stacked(m):
    high = m.astype(jnp.bfloat16).astype(np.float32)
    middle = (m - high).astype(jnp.bfloat16).astype(np.float32)
    low = m - high - middle
    both = np.concatenate([high, middle], 1)
    return [
        jnp.asarray(np.concatenate([both, both], 0), jnp.bfloat16),
        jnp.asarray(np.concatenate([low, high], 0), jnp.bfloat16),
    ]


def constants(elems_z):
    z_back = np.kron(np.eye(LANES // N, dtype=np.float32), lagrange_derivative())
    lane = np.arange(N * elems_z)
    low = (lane % N == 0) & (lane > 0)
    high = (lane % N == N - 1) & (lane < N * elems_z - 1)
    lanes = np.stack([low, high] + [0 * lane] * 6).astype(np.float32)
    return stacked(z_back.T) + stacked(z_back) + [jnp.asarray(lanes)]


def times(v, first, second):
    high, middle, low = pieces(v)
    product = functools.partial(jnp.dot, preferred_element_type=f32)
    large = product(jnp.concatenate([high, middle], 1), first[...])
    small = product(jnp.concatenate([high, low], 1), second[...])
    return (large[:, :LANES] + large[:, LANES:]) + small


def weights_1d():
    return [float(np.float32(x)) for x in gll_weights]


def position():
    return lax.axis_index("gx"), lax.axis_index("gy")


def tiles(ref):
    return [ref[N * a : N * a + N, :] for a in range(N)]


def store(ref, values):
    for a in range(N):
        ref[N * a : N * a + N, :] = values[a]


def row_index(shape):
    return lax.broadcasted_iota(jnp.int32, shape, 0)


def along(shape, values, index):
    out = jnp.full(shape, values[0], f32)
    for i in range(1, len(values)):
        out = jnp.where(index == i, values[i], out)
    return out


def fold_z(v, lanes):
    size = v.shape[1]
    return (
        v
        + pltpu.roll(v, 1, axis=1) * lanes[0:1, :]
        + pltpu.roll(v, size - 1, axis=1) * lanes[1:2, :]
    )


def pick(pos, axis, even, odd):
    return jnp.where(pos[axis] % 2 == 0, even, odd)


def send(pos, axis, low, high, even_ref, odd_ref):
    even_ref[...] = pick(pos, axis, high, low)
    odd_ref[...] = pick(pos, axis, low, high)


def received(sizes, pos, axis, even, odd):
    low = jnp.where(pos[axis] > 0, pick(pos, axis, odd, even), 0.0)
    high = jnp.where(pos[axis] < sizes[axis] - 1, pick(pos, axis, even, odd), 0.0)
    return low, high


def place(low, high, a, row):
    return jnp.where(row == 0, low[a : a + 1], jnp.where(row == N - 1, high[a : a + 1], 0.0))


def robin_tiles(sizes, pos, table, flags, classes, size):
    elems_z = flags.shape[1]
    coefficient = jnp.zeros(flags.shape, f32)
    for c in range(table.shape[1]):
        coefficient = jnp.where(classes[...] == c, table[:, c : c + 1], coefficient)
    element = lax.broadcasted_iota(jnp.int32, flags.shape, 1)
    sides = [
        pos[0] == 0, pos[0] == sizes[0] - 1, pos[1] == 0, pos[1] == sizes[1] - 1,
        element == 0, element == elems_z - 1,
    ]
    rows = []
    for bit, side in enumerate(sides):
        flagged = (flags[...] >> bit) % 2 == 1
        rows.append(jnp.where(flagged & side, coefficient, 0.0))
    rows += [jnp.zeros(flags.shape, f32)] * 2
    spread = lax.broadcasted_iota(jnp.int32, (elems_z, size), 1) // N == row_index((elems_z, size))
    faces = dot(jnp.concatenate(rows, 0), spread.astype(f32))
    node = lax.broadcasted_iota(jnp.int32, (1, size), 1) % N
    w = weights_1d()
    w_z = along((1, size), w, node)
    row = row_index((N, size))
    w_b = along((N, size), w, row)
    w_bz = w_b * w_z
    ends_z = jnp.where(node == 0, faces[4:5], 0.0) + jnp.where(node == N - 1, faces[5:6], 0.0)
    common = place(faces[2:3] * w_z, faces[3:4] * w_z, 0, row) + w_b * ends_z
    robin = [w[a] * common for a in range(N)]
    robin[0] += w_bz * faces[0:1]
    robin[N - 1] += w_bz * faces[1:2]
    return robin, w_bz


def field_kernel(sizes, source, k, flags, classes, table, even_out, odd_out,
                 v_ref, k_ref, flags_ref, classes_ref, table_ref, low, high, sems):
    pairs = (
        (flags, flags_ref), (classes, classes_ref), (table, table_ref), (source, v_ref), (k, k_ref),
    )
    copies = [pltpu.make_async_copy(*pair, sems.at[i]) for i, pair in enumerate(pairs)]
    for copy in copies:
        copy.start()
    for copy in copies[:3]:
        copy.wait()
    pos = position()
    robin, w_bz = robin_tiles(sizes, pos, table_ref, flags_ref, classes_ref, source.shape[1])
    for copy in copies[3:]:
        copy.wait()
    w = weights_1d()
    ws = [w[a] * w_bz * v for a, v in enumerate(tiles(v_ref))]
    wk = [w[a] * w_bz * v for a, v in enumerate(tiles(k_ref))]
    for i, field in enumerate((ws, wk, robin)):
        for a in range(N):
            low[N * i + a : N * i + a + 1, :] = field[a][0:1]
            high[N * i + a : N * i + a + 1, :] = field[a][N - 1 : N]
    send(pos, 1, low[...], high[...], even_out, odd_out)


def whole_field_kernel(sizes, source, k, flags, classes, table, ws_out, wk_out, robin_out):
    robin, w_bz = robin_tiles(sizes, position(), table, flags, classes, source.shape[1])
    w = weights_1d()
    store(robin_out, robin)
    store(ws_out, [w[a] * w_bz * v for a, v in enumerate(tiles(source))])
    store(wk_out, [w[a] * w_bz * v for a, v in enumerate(tiles(k))])


def fold_y_kernel(sizes, ws, wk, robin, odd, even, even_out, odd_out):
    pos = position()
    low, high = received(sizes, pos, 1, even[...], odd[...])
    row = row_index((N, ws.shape[1]))
    sides = []
    for a in (0, N - 1):
        part = [
            field[N * a : N * a + N, :] + place(low, high, N * i + a, row)
            for i, field in enumerate((ws, wk, robin))
        ]
        sides.append(jnp.concatenate(part + [wk[N * a : N * a + N, :]], 0))
    send(pos, 0, sides[0], sides[1], even_out, odd_out)


def prepare_kernel(sizes, ws, wk, robin, odd, even, lanes,
                   b_out, kx_out, ky_out, kz_out, advect_out, diagonal_out, inverse_out):
    pos = position()
    low, high = received(sizes, pos, 1, even[...], odd[...])
    shape = (N, ws.shape[1])
    row = row_index(shape)
    w = weights_1d()
    node = lax.broadcasted_iota(jnp.int32, (1, shape[1]), 1) % N
    copies_z = 1.0 + lanes[0:1, :] + lanes[1:2, :]
    shared_y = ((row == 0) & (pos[1] > 0)) | ((row == N - 1) & (pos[1] < sizes[1] - 1))
    copies_yz = jnp.where(shared_y, 2.0, 1.0) * copies_z
    weights_yz = along(shape, w, row) * along((1, shape[1]), w, node) * copies_yz
    inverse_yz = 1.0 / copies_yz
    for a in range(N):
        at = slice(N * a, N * a + N)
        summed = [
            field[at, :] + place(low, high, N * i + a, row) for i, field in enumerate((ws, wk, robin))
        ]
        b_out[at, :] = fold_z(summed[0], lanes)
        kz_out[at, :] = summed[1]
        kx_out[at, :] = fold_z(summed[1], lanes)
        ky_out[at, :] = fold_z(wk[at, :], lanes)
        copies_x = 1.0
        if a == 0:
            copies_x = jnp.where(pos[0] > 0, 2.0, 1.0)
        if a == N - 1:
            copies_x = jnp.where(pos[0] < sizes[0] - 1, 2.0, 1.0)
        weights_a = w[a] * weights_yz
        advect_out[at, :] = scan_speed * weights_a
        diagonal_out[at, :] = fold_z(summed[2], lanes) + mass_coef * copies_x * weights_a
        inverse_out[at, :] = inverse_yz * (1.0 / copies_x)


def contract(m, values):
    half = N // 2
    total = [values[b] + values[N - 1 - b] for b in range(half)]
    apart = [values[b] - values[N - 1 - b] for b in range(half)]
    out = [None] * N
    for a in range(half):
        even = sum(float((m[a][b] + m[a][N - 1 - b]) / 2) * total[b] for b in range(half))
        odd = sum(float((m[a][b] - m[a][N - 1 - b]) / 2) * apart[b] for b in range(half))
        out[a] = even + odd
        out[N - 1 - a] = odd - even
    return out


def rotations(m, row):
    return [along(row.shape, [float(m[b][(b + s) % N]) for b in range(N)], row) for s in range(N)]


def contract_rows(coefs, v):
    out = coefs[0] * v
    for s in range(1, N):
        out += coefs[s] * pltpu.roll(v, N - s, axis=0)
    return out


def operate(pos, v, kx, ky, advect, xy_out, sends, low, high):
    d = lagrange_derivative()
    k, speed = tiles(kx), tiles(advect)
    flux = [k[a] * g - speed[a] * v[a] for a, g in enumerate(contract(d, v))]
    x = contract(d.T, flux)
    send(pos, 0, x[0], x[N - 1], sends[0], sends[1])
    row = row_index(v[0].shape)
    forward, back = rotations(d, row), rotations(d.T, row)
    for a in range(N):
        at = slice(N * a, N * a + N)
        y = contract_rows(back, ky[at, :] * contract_rows(forward, v[a]))
        low[a : a + 1, :] = y[0:1]
        high[a : a + 1, :] = y[N - 1 : N]
        xy_out[at, :] = x[a] + y
    send(pos, 1, low[...], high[...], sends[2], sends[3])


def along_z(v, xy, kz, diagonal, forward_1, forward_2, back_1, back_2, lanes, q_out):
    rows, size = v.shape
    columns = [slice(i, i + LANES) for i in range(0, size, LANES)]
    grad = times(jnp.concatenate([v[:, c] for c in columns], 0), forward_1, forward_2)
    flux = [kz[:, c] * grad[i * rows : (i + 1) * rows] for i, c in enumerate(columns)]
    back = times(jnp.concatenate(flux, 0), back_1, back_2)
    back = jnp.concatenate([back[i * rows : (i + 1) * rows] for i in range(len(columns))], 1)
    q_out[...] = fold_z(back, lanes) + (xy[...] + diagonal[...] * v[...])


def assemble(sizes, pos, q, recv):
    x_even, x_odd, y_even, y_odd = (recv[ORDER.index(i)] for i in range(4))
    x_low, x_high = received(sizes, pos, 0, x_even[...], x_odd[...])
    y_low, y_high = received(sizes, pos, 1, y_even[...], y_odd[...])
    row = row_index(y_low.shape)
    out = [q[N * a : N * a + N, :] + place(y_low, y_high, a, row) for a in range(N)]
    out[0] += x_low
    out[N - 1] += x_high
    return out


def first_kernel(sizes, b_in, kx, ky_in, advect, odd, even, lanes,
                 b_out, ky_out, xy_out, *refs):
    pos = position()
    low, high = received(sizes, pos, 0, even[...], odd[...])
    b, ky = tiles(b_in), tiles(ky_in)
    for a, side in ((0, low), (N - 1, high)):
        b[a] += fold_z(side[0:N], lanes)
        ky[a] += fold_z(side[3 * N : 4 * N], lanes)
    store(b_out, b)
    store(ky_out, ky)
    operate(pos, b, kx, ky_out, advect, xy_out, refs[:4], *refs[4:])


def first_z_kernel(sizes, b, xy, kz_in, diagonal_in, odd, even, f1, f2, b1, b2, lanes,
                   kz_out, diagonal_out, q_out):
    pos = position()
    low, high = received(sizes, pos, 0, even[...], odd[...])
    kz_out[...] = kz_in[...]
    diagonal_out[...] = diagonal_in[...]
    for a, side in ((0, low), (N - 1, high)):
        at = slice(N * a, N * a + N)
        kz_out[at, :] += side[N : 2 * N]
        diagonal_out[at, :] += fold_z(side[2 * N : 3 * N], lanes)
    along_z(b, xy, kz_out, diagonal_out, f1, f2, b1, b2, lanes, q_out)


def dots_row(pairs, inverse, first=0):
    shape = (N, LANES)
    lane = lax.broadcasted_iota(jnp.int32, shape, 1)
    row = jnp.zeros(shape, f32)
    scaled = {}
    for i, (u, v) in enumerate(pairs):
        if id(u) not in scaled:
            scaled[id(u)] = [x * m for x, m in zip(u, inverse)]
        product = sum(x * y for x, y in zip(scaled[id(u)], v))
        product = sum(product[:, j : j + LANES] for j in range(0, product.shape[1], LANES))
        row = jnp.where(lane == first + i, jnp.sum(product, axis=1, keepdims=True), row)
    return jnp.sum(row, axis=0, keepdims=True)


def for_all(row, out):
    for i in range(out.shape[0]):
        out[i] = row


def totals(gathered, count):
    row = jnp.sum(gathered[...], axis=0)
    return [jnp.broadcast_to(row[:, i : i + 1], row.shape) for i in range(count)]


def wide(scalar, like):
    return jnp.concatenate([scalar] * (like.shape[1] // scalar.shape[1]), 1)


def steps(br, bs, bw, bz, wr, ws, zr, zs, ww, wz, zz):
    alpha = br / bs
    omega = (wr - alpha * (ws + zr) + alpha * alpha * zs) / (
        ww - 2.0 * alpha * wz + alpha * alpha * zz
    )
    rho_next = (br - alpha * bs) - omega * (bw - alpha * bz)
    beta = rho_next / br * (alpha / omega)
    return alpha, omega, beta


def second_pairs(b, r, s, w, z):
    return [(w, b), (w, r), (w, s), (w, w), (w, z), (r, b), (r, z)]


def early_pairs(b, e):
    return [(e[i], b) for i in range(6)] + [(e[i], e[j]) for i in range(6) for j in range(i, 6)]


def late_pairs(b, e):
    return [(e[i], b) for i in (6, 7)] + [(e[j], e[i]) for j in (6, 7) for i in range(j + 1)]


EARLY = 34
LATE = 17


def guess(scalars, like):
    omega = wide(scalars[1:2, :], like)
    return 2.0 * omega, omega


def last_steps(sums, guessed_omega):
    names = second_pairs(*"brswz") + early_pairs("b", range(6)) + late_pairs("b", range(8))
    value = dict(zip(names, sums))
    g = lambda i, j: value[i, j] if (i, j) in value else value[j, i]
    second = steps(
        g("r", "b"), g(1, "b"), g("w", "b"), g(3, "b"),
        g("w", "r"), g("w", "s"), g("r", "z"), g(1, 3), g("w", "w"), g("w", "z"), g(3, 3),
    )
    alpha, omega, beta = second
    off_alpha, off_omega = alpha - 2.0 * guessed_omega, omega - guessed_omega
    ratio = off_omega / guessed_omega
    one, cross = jnp.ones_like(alpha), off_alpha * omega
    both = -off_alpha - beta * omega
    r = {0: one, 1: -off_alpha, 2: -off_omega, 3: cross, 4: -off_omega * guessed_omega}
    w = {2: one, 3: -off_alpha, 4: -off_omega, 5: cross}
    s = {1: beta, 2: one, 3: both, 4: -off_omega, 5: cross}
    z = {3: beta, 4: -ratio, 5: both, 6: one + ratio, 7: cross}
    with_b = lambda u: sum(c * g(i, "b") for i, c in u.items())
    times = lambda u: {i: sum(c * g(i, j) for j, c in u.items()) for i in range(8)}
    inner = lambda image, u: sum(c * image[i] for i, c in u.items())
    gw, gz = times(w), times(z)
    third = steps(
        with_b(r), with_b(s), with_b(w), with_b(z),
        inner(gw, r), inner(gw, s), inner(gz, r), inner(gz, s),
        inner(gw, w), inner(gw, z), inner(gz, z),
    )
    return second, third


def apply_kernel(sizes, q, x0, x1, y0, y1, kx, ky, advect, v_out, xy_out, *refs):
    pos = position()
    v = assemble(sizes, pos, q, (x0, x1, y0, y1))
    store(v_out, v)
    operate(pos, v, kx, ky, advect, xy_out, refs[:4], *refs[4:])


def z_kernel(*refs):
    along_z(*refs)


def first_dots_kernel(sizes, b, s, inverse, q, x0, x1, y0, y1, kx, ky, advect, z_out, xy_out, *refs):
    *sends, row_out, low, high, row, sem = refs
    pos = position()
    z = assemble(sizes, pos, q, (x0, x1, y0, y1))
    store(z_out, z)
    b, s = tiles(b), tiles(s)
    for_all(dots_row([(b, b), (b, s), (b, z), (s, s), (s, z), (z, z)], tiles(inverse)), row)
    copy = pltpu.make_async_copy(row, row_out, sem)
    copy.start()
    operate(pos, z, kx, ky, advect, xy_out, sends, low, high)
    copy.wait()


def update_kernel(sizes, gathered, s, z, az, q, x0, x1, y0, y1, kx, ky, advect,
                  z_out, aw_out, scalars, xy_out, *refs):
    pos = position()
    bb, bs, bz, ss, sz, zz = totals(gathered, 6)
    values = steps(bb, bs, bs, bz, bs, ss, bz, sz, ss, sz, zz)
    for i, value in enumerate(values):
        scalars[i : i + 1, :] = value
    alpha, omega, beta = (wide(value, s) for value in values)
    aaz = assemble(sizes, pos, q, (x0, x1, y0, y1))
    z, az = tiles(z), tiles(az)
    aw = [(z[i] - alpha * az[i]) - omega * (az[i] - alpha * aaz[i]) for i in range(N)]
    z_next = [aw[i] + beta * (z[i] - omega * az[i]) for i in range(N)]
    store(aw_out, aw)
    store(z_out, z_next)
    operate(pos, z_next, kx, ky, advect, xy_out, refs[:4], *refs[4:])


def update_rest_kernel(scalars, b, s, z, az, x_out, r_out, p_out, s_out, w_out):
    alpha, omega, beta = (wide(scalars[i : i + 1, :], s) for i in range(3))
    for i in range(N):
        at = slice(N * i, N * i + N)
        b_, s_, z_, az_ = b[at, :], s[at, :], z[at, :], az[at, :]
        half, applied_half = b_ - alpha * s_, s_ - alpha * z_
        x_out[at, :] = alpha * b_ + omega * half
        r = half - omega * applied_half
        w = applied_half - omega * (z_ - alpha * az_)
        p_out[at, :] = r + beta * (b_ - omega * s_)
        r_out[at, :], w_out[at, :], s_out[at, :] = r, w, w + beta * (s_ - omega * z_)


def two_z_kernel(z, z_xy, aw, kx, ky, advect, *refs):
    *shared, z_q_out, aw_q_out, f0, f1, f2, f3, xy, low, high = refs
    along_z(z, z_xy, *shared, z_q_out)
    operate(position(), tiles(aw), kx, ky, advect, xy, (f0, f1, f2, f3), low, high)
    along_z(aw, xy, *shared, aw_q_out)


def apply_beside_kernel(sizes, f0, f1, f2, f3, q, x0, x1, y0, y1, kx, ky, advect, v_out, xy_out, *refs):
    sends, sides = refs[:4], refs[4:]
    pos = position()
    v = assemble(sizes, pos, q, (x0, x1, y0, y1))
    store(v_out, v)
    operate(pos, v, kx, ky, advect, xy_out, [ref.at[pl.ds(0, N)] for ref in sends], *sides)
    for ref, face in zip(sends, (f0, f1, f2, f3)):
        ref[N : 2 * N, :] = face[...]


def early_dots_kernel(scalars, b, r, s, w, z, aw, az, inverse, near_r_out, y_out, au_out, row):
    alpha, omega = guess(scalars, s)
    au, y, near_r = [], [], []
    for i in range(N):
        at = slice(N * i, N * i + N)
        u = w[at, :] - alpha * z[at, :]
        au.append(aw[at, :] - alpha * az[at, :])
        y.append(u - omega * au[i])
        near_r.append((r[at, :] - alpha * s[at, :]) - omega * u)
    store(near_r_out, near_r)
    store(y_out, y)
    store(au_out, au)
    b, r, s, w, z, az = (tiles(ref) for ref in (b, r, s, w, z, az))
    pairs = second_pairs(b, r, s, w, z) + early_pairs(b, [near_r, s, y, z, au, az])
    row[...] = dots_row(pairs, tiles(inverse))


def late_dots_kernel(sizes, scalars, b, near_r, s, y, z, au, az, inverse, early, aaz_q, aaw_q,
                     x0, x1, y0, y1, aaw_out, aaz_out, row):
    pos = position()
    halves = [[ref.at[pl.ds(i * N, N)] for ref in (x0, x1, y0, y1)] for i in range(2)]
    aaz = assemble(sizes, pos, aaz_q, halves[0])
    aaw = assemble(sizes, pos, aaw_q, halves[1])
    store(aaz_out, aaz)
    store(aaw_out, aaw)
    alpha, omega = guess(scalars, s)
    e = [tiles(ref) for ref in (near_r, s, y, z, au, az)]
    ay = [e[4][i] - omega * (aaw[i] - alpha * aaz[i]) for i in range(N)]
    pairs = late_pairs(tiles(b), e + [ay, aaz])
    for_all(early[...] + dots_row(pairs, tiles(inverse), EARLY), row)


def last_kernel(gathered, scalars, x, p, r, s, w, z, aw, az, aaw, aaz, x_out, r_out):
    second, third = last_steps(totals(gathered, EARLY + LATE), scalars[1:2, :])
    alpha, omega, beta = (wide(value, s) for value in second)
    last_alpha, last_omega, _ = (wide(value, s) for value in third)
    for i in range(N):
        at = slice(N * i, N * i + N)
        p_, s_, z_, az_ = p[at, :], s[at, :], z[at, :], az[at, :]
        half, applied_half = r[at, :] - alpha * s_, w[at, :] - alpha * z_
        applied_twice = aw[at, :] - alpha * az_
        r_next = half - omega * applied_half
        w_next = applied_half - omega * applied_twice
        aw_next = applied_twice - omega * (aaw[at, :] - alpha * aaz[at, :])
        p_next = r_next + beta * (p_ - omega * s_)
        s_next = w_next + beta * (s_ - omega * z_)
        z_next = aw_next + beta * (z_ - omega * az_)
        last_half = r_next - last_alpha * s_next
        x_out[at, :] = (x[at, :] + alpha * p_ + omega * half) + (
            last_alpha * p_next + last_omega * last_half
        )
        r_out[at, :] = last_half - last_omega * (w_next - last_alpha * z_next)


def pairings(sizes):
    count_x, count_y = sizes
    grid = [(i, j) for i in range(count_x) for j in range(count_y)]
    number = lambda i, j: i * count_y + j
    step = lambda i: i + 1 if i % 2 else i - 1
    x_even = [(number(i, j), number(i ^ 1, j)) for i, j in grid]
    x_odd = [
        (number(i, j), number(step(i), j) if 0 < i < count_x - 1 else number(i, j ^ 1)) for i, j in grid
    ]
    y_even = [(number(i, j), number(i, j ^ 1)) for i, j in grid]
    y_odd = [
        (number(i, j), number(i, step(j)) if 0 < j < count_y - 1 else number(i ^ 1, j)) for i, j in grid
    ]
    return (x_even, x_odd), (y_even, y_odd)


def per_device(sizes, source, conductivity, robin_flags, htc_class, htc_table):
    shape = source.shape
    elems_z = robin_flags.shape[2]
    rows, size = shape[0] * shape[1], shape[2]
    assert robin_flags.shape[:2] == (1, 1) and size % LANES == 0
    assert sizes[0] % 2 == 0 and sizes[1] % 2 == 0
    devices = sizes[0] * sizes[1]
    *z_mats, lanes = constants(elems_z)
    x_pairs, y_pairs = pairings(sizes)

    def struct(n=rows):
        return jax.ShapeDtypeStruct((n, size), f32)

    field = struct()
    faces = [struct(N)] * 4
    row = jax.ShapeDtypeStruct((devices, 1, 128), f32)
    scalars = jax.ShapeDtypeStruct((N, 128), f32)
    side = [pltpu.VMEM((N, size), f32)] * 2
    row_side = [pltpu.VMEM(row.shape, f32), pltpu.SemaphoreType.DMA]

    def call(kernel, outs, *operands, scratch=(), hbm=0, limit=32, cost=0, hbm_out=0):
        specs = [HBM] * hbm + [VMEM] * (len(operands) - hbm)
        return pl.pallas_call(
            kernel,
            out_shape=outs,
            in_specs=specs,
            out_specs=[VMEM] * (len(outs) - hbm_out) + [HBM] * hbm_out,
            scratch_shapes=list(scratch),
            compiler_params=pltpu.CompilerParams(vmem_limit_bytes=limit * 1024 * 1024),
            cost_estimate=pl.CostEstimate(flops=cost, bytes_accessed=cost, transcendentals=0)
            if cost
            else None,
        )(*operands)

    def permute(values, pairs):
        return lax.ppermute(values, ("gx", "gy"), pairs)

    def exchange(pairs, even, odd):
        return permute(odd, pairs[1]), permute(even, pairs[0])

    def swap(parts):
        x_odd = permute(parts[1], x_pairs[1])
        y_odd = permute(parts[3], y_pairs[1])
        x_even = permute(parts[0], x_pairs[0])
        recv = x_even, x_odd, permute(parts[2], y_pairs[0]), y_odd
        return tuple(recv[i] for i in ORDER)

    def spread(values):
        return lax.all_to_all(values, ("gx", "gy"), 0, 0)

    given = (
        source.reshape(rows, size), conductivity.reshape(rows, size),
        robin_flags.reshape(1, elems_z), htc_class.reshape(1, elems_z), htc_table.reshape(1, -1),
    )
    parts = call(
        functools.partial(field_kernel, sizes), [struct(3 * N)] * 2, *given,
        hbm=5,
        limit=60,
        scratch=[pltpu.VMEM(v.shape, v.dtype) for v in given]
        + [pltpu.VMEM((3 * N, size), f32)] * 2
        + [pltpu.SemaphoreType.DMA((5,))],
    )
    recv = exchange(y_pairs, *parts)
    ws, wk, robin = call(functools.partial(whole_field_kernel, sizes), [field] * 3, *given, cost=COST)
    parts = call(
        functools.partial(fold_y_kernel, sizes), [struct(4 * N)] * 2, ws, wk, robin, *recv
    )
    b, kx, ky, kz, advect, diagonal, inverse = call(
        functools.partial(prepare_kernel, sizes), [field] * 7, ws, wk, robin, *recv, lanes,
        cost=COST,
    )
    recv = exchange(x_pairs, *parts)
    b, ky, xy, *parts = call(
        functools.partial(first_kernel, sizes), [field] * 3 + faces,
        b, kx, ky, advect, *recv, lanes, scratch=side,
    )
    kz, diagonal, q = call(
        functools.partial(first_z_kernel, sizes), [field] * 3,
        b, xy, kz, diagonal, *recv, *z_mats, lanes, cost=COST,
    )
    coefs = (kx, ky, advect)
    z_args = (kz, diagonal, *z_mats, lanes)
    recv = swap(parts)

    def apply(q, recv):
        v, xy, *parts = call(
            functools.partial(apply_kernel, sizes), [field] * 2 + faces, q, *recv, *coefs, scratch=side
        )
        recv = swap(parts)
        (q,) = call(z_kernel, [field], v, xy, *z_args, cost=COST)
        return v, q, recv

    s, q, recv = apply(q, recv)
    z, xy, *parts, products = call(
        functools.partial(first_dots_kernel, sizes), [field] * 2 + faces + [row],
        b, s, inverse, q, *recv, *coefs, scratch=side + row_side, hbm_out=1,
    )
    gathered = spread(products)
    recv = swap(parts)
    (q,) = call(z_kernel, [field], z, xy, *z_args, cost=COST)
    az, q, recv = apply(q, recv)
    z_next, aw, values, z_xy, *parts = call(
        functools.partial(update_kernel, sizes),
        [field] * 2 + [scalars] + [field] + faces,
        gathered, s, z, az, q, *recv, *coefs, scratch=side,
    )
    recv = swap(parts)
    x, r, p, s, w = call(update_rest_kernel, [field] * 5, values, b, s, z, az, cost=COST)
    z = z_next
    z_q, aw_q, *aw_parts = call(
        two_z_kernel, [field] * 2 + faces, z, z_xy, aw, *coefs, *z_args,
        cost=COST, scratch=[pltpu.VMEM((rows, size), f32)] + side,
    )
    az, xy, *parts = call(
        functools.partial(apply_beside_kernel, sizes), [field] * 2 + [struct(2 * N)] * 4,
        *aw_parts, z_q, *recv, *coefs, scratch=side,
    )
    recv = swap(parts)
    (q,) = call(z_kernel, [field], az, xy, *z_args, cost=COST)
    near_r, y, au, early = call(
        early_dots_kernel, [field] * 3 + [jax.ShapeDtypeStruct((1, LANES), f32)],
        values, b, r, s, w, z, aw, az, inverse, cost=COST,
    )
    aaw, aaz, products = call(
        functools.partial(late_dots_kernel, sizes), [field] * 2 + [row],
        values, b, near_r, s, y, z, au, az, inverse, early, q, aw_q, *recv,
    )
    x, r = call(
        last_kernel, [field] * 2, spread(products), values, x, p, r, s, w, z, aw, az, aaw, aaz
    )
    return x.reshape(shape), r.reshape(shape)


def solution(mesh):
    sizes = (mesh.shape["gx"], mesh.shape["gy"])
    field = P("gx", "gy", None)
    return jax.shard_map(
        functools.partial(per_device, sizes),
        mesh=mesh,
        in_specs=(field, field, field, field, P()),
        out_specs=(field, field),
        check_vma=False,
    )
```

```python
import functools

import jax
import jax.numpy as jnp
import numpy as np
from jax import lax
from jax.experimental import pallas as pl
from jax.experimental.pallas import tpu as pltpu
from jax.sharding import PartitionSpec as P

ITERS = 3
N = 8

gll_points = (
    -1.0,
    -0.8717401485096066,
    -0.5917001814331423,
    -0.2092992179024789,
    0.2092992179024789,
    0.5917001814331423,
    0.8717401485096066,
    1.0,
)
gll_weights = (
    0.03571428571428571,
    0.21070422714350603,
    0.3411226924835044,
    0.4124587946587038,
    0.4124587946587038,
    0.3411226924835044,
    0.21070422714350603,
    0.03571428571428571,
)
mass_coef = 0.2
scan_speed = 2.0
f32 = jnp.float32
VMEM = pl.BlockSpec(memory_space=pltpu.VMEM)
HBM = pl.BlockSpec(memory_space=pl.ANY)
COST = 1 << 20
LANES = 128
ORDER = (3, 0, 1, 2)
dot = functools.partial(jnp.dot, precision=lax.Precision.HIGHEST, preferred_element_type=f32)


def lagrange_derivative():
    points = np.array(gll_points)
    barycentric = np.array(
        [1.0 / np.prod([points[j] - points[m] for m in range(N) if m != j]) for j in range(N)]
    )
    derivative = np.zeros((N, N))
    for a in range(N):
        for b in range(N):
            if a != b:
                derivative[a, b] = barycentric[b] / barycentric[a] / (points[a] - points[b])
        derivative[a, a] = -np.sum(derivative[a])
    return derivative.astype(np.float32)


def pieces(v):
    high = v.astype(jnp.bfloat16)
    rest = v - high.astype(f32)
    middle = rest.astype(jnp.bfloat16)
    return high, middle, (rest - middle.astype(f32)).astype(jnp.bfloat16)


def stacked(m):
    high = m.astype(jnp.bfloat16).astype(np.float32)
    middle = (m - high).astype(jnp.bfloat16).astype(np.float32)
    low = m - high - middle
    both = np.concatenate([high, middle], 1)
    return [
        jnp.asarray(np.concatenate([both, both], 0), jnp.bfloat16),
        jnp.asarray(np.concatenate([low, high], 0), jnp.bfloat16),
    ]


def constants(elems_z):
    z_back = np.kron(np.eye(LANES // N, dtype=np.float32), lagrange_derivative())
    lane = np.arange(N * elems_z)
    low = (lane % N == 0) & (lane > 0)
    high = (lane % N == N - 1) & (lane < N * elems_z - 1)
    lanes = np.stack([low, high] + [0 * lane] * 6).astype(np.float32)
    return stacked(z_back.T) + stacked(z_back) + [jnp.asarray(lanes)]


def times(v, first, second):
    high, middle, low = pieces(v)
    product = functools.partial(jnp.dot, preferred_element_type=f32)
    large = product(jnp.concatenate([high, middle], 1), first[...])
    small = product(jnp.concatenate([high, low], 1), second[...])
    return (large[:, :LANES] + large[:, LANES:]) + small


def weights_1d():
    return [float(np.float32(x)) for x in gll_weights]


def position():
    return lax.axis_index("gx"), lax.axis_index("gy")


def tiles(ref):
    return [ref[N * a : N * a + N, :] for a in range(N)]


def store(ref, values):
    for a in range(N):
        ref[N * a : N * a + N, :] = values[a]


def row_index(shape):
    return lax.broadcasted_iota(jnp.int32, shape, 0)


def along(shape, values, index):
    out = jnp.full(shape, values[0], f32)
    for i in range(1, len(values)):
        out = jnp.where(index == i, values[i], out)
    return out


def fold_z(v, lanes):
    size = v.shape[1]
    return (
        v
        + pltpu.roll(v, 1, axis=1) * lanes[0:1, :]
        + pltpu.roll(v, size - 1, axis=1) * lanes[1:2, :]
    )


def pick(pos, axis, even, odd):
    return jnp.where(pos[axis] % 2 == 0, even, odd)


def send(pos, axis, low, high, even_ref, odd_ref):
    even_ref[...] = pick(pos, axis, high, low)
    odd_ref[...] = pick(pos, axis, low, high)


def received(sizes, pos, axis, even, odd):
    low = jnp.where(pos[axis] > 0, pick(pos, axis, odd, even), 0.0)
    high = jnp.where(pos[axis] < sizes[axis] - 1, pick(pos, axis, even, odd), 0.0)
    return low, high


def place(low, high, a, row):
    return jnp.where(row == 0, low[a : a + 1], jnp.where(row == N - 1, high[a : a + 1], 0.0))


def robin_tiles(sizes, pos, table, flags, classes, size):
    elems_z = flags.shape[1]
    coefficient = jnp.zeros(flags.shape, f32)
    for c in range(table.shape[1]):
        coefficient = jnp.where(classes[...] == c, table[:, c : c + 1], coefficient)
    element = lax.broadcasted_iota(jnp.int32, flags.shape, 1)
    sides = [
        pos[0] == 0, pos[0] == sizes[0] - 1, pos[1] == 0, pos[1] == sizes[1] - 1,
        element == 0, element == elems_z - 1,
    ]
    rows = []
    for bit, side in enumerate(sides):
        flagged = (flags[...] >> bit) % 2 == 1
        rows.append(jnp.where(flagged & side, coefficient, 0.0))
    rows += [jnp.zeros(flags.shape, f32)] * 2
    spread = lax.broadcasted_iota(jnp.int32, (elems_z, size), 1) // N == row_index((elems_z, size))
    faces = dot(jnp.concatenate(rows, 0), spread.astype(f32))
    node = lax.broadcasted_iota(jnp.int32, (1, size), 1) % N
    w = weights_1d()
    w_z = along((1, size), w, node)
    row = row_index((N, size))
    w_b = along((N, size), w, row)
    w_bz = w_b * w_z
    ends_z = jnp.where(node == 0, faces[4:5], 0.0) + jnp.where(node == N - 1, faces[5:6], 0.0)
    common = place(faces[2:3] * w_z, faces[3:4] * w_z, 0, row) + w_b * ends_z
    robin = [w[a] * common for a in range(N)]
    robin[0] += w_bz * faces[0:1]
    robin[N - 1] += w_bz * faces[1:2]
    return robin, w_bz


def field_kernel(sizes, source, k, flags, classes, table, even_out, odd_out,
                 v_ref, k_ref, flags_ref, classes_ref, table_ref, low, high, sems):
    pairs = (
        (flags, flags_ref), (classes, classes_ref), (table, table_ref), (source, v_ref), (k, k_ref),
    )
    copies = [pltpu.make_async_copy(*pair, sems.at[i]) for i, pair in enumerate(pairs)]
    for copy in copies:
        copy.start()
    for copy in copies[:3]:
        copy.wait()
    pos = position()
    robin, w_bz = robin_tiles(sizes, pos, table_ref, flags_ref, classes_ref, source.shape[1])
    for copy in copies[3:]:
        copy.wait()
    w = weights_1d()
    ws = [w[a] * w_bz * v for a, v in enumerate(tiles(v_ref))]
    wk = [w[a] * w_bz * v for a, v in enumerate(tiles(k_ref))]
    for i, field in enumerate((ws, wk, robin)):
        for a in range(N):
            low[N * i + a : N * i + a + 1, :] = field[a][0:1]
            high[N * i + a : N * i + a + 1, :] = field[a][N - 1 : N]
    send(pos, 1, low[...], high[...], even_out, odd_out)


def whole_field_kernel(sizes, source, k, flags, classes, table, ws_out, wk_out, robin_out):
    robin, w_bz = robin_tiles(sizes, position(), table, flags, classes, source.shape[1])
    w = weights_1d()
    store(robin_out, robin)
    store(ws_out, [w[a] * w_bz * v for a, v in enumerate(tiles(source))])
    store(wk_out, [w[a] * w_bz * v for a, v in enumerate(tiles(k))])


def fold_y_kernel(sizes, ws, wk, robin, odd, even, even_out, odd_out):
    pos = position()
    low, high = received(sizes, pos, 1, even[...], odd[...])
    row = row_index((N, ws.shape[1]))
    sides = []
    for a in (0, N - 1):
        part = [
            field[N * a : N * a + N, :] + place(low, high, N * i + a, row)
            for i, field in enumerate((ws, wk, robin))
        ]
        sides.append(jnp.concatenate(part + [wk[N * a : N * a + N, :]], 0))
    send(pos, 0, sides[0], sides[1], even_out, odd_out)


def prepare_kernel(sizes, ws, wk, robin, odd, even, lanes,
                   b_out, kx_out, ky_out, kz_out, advect_out, diagonal_out, inverse_out):
    pos = position()
    low, high = received(sizes, pos, 1, even[...], odd[...])
    shape = (N, ws.shape[1])
    row = row_index(shape)
    w = weights_1d()
    node = lax.broadcasted_iota(jnp.int32, (1, shape[1]), 1) % N
    copies_z = 1.0 + lanes[0:1, :] + lanes[1:2, :]
    shared_y = ((row == 0) & (pos[1] > 0)) | ((row == N - 1) & (pos[1] < sizes[1] - 1))
    copies_yz = jnp.where(shared_y, 2.0, 1.0) * copies_z
    weights_yz = along(shape, w, row) * along((1, shape[1]), w, node) * copies_yz
    inverse_yz = 1.0 / copies_yz
    for a in range(N):
        at = slice(N * a, N * a + N)
        summed = [
            field[at, :] + place(low, high, N * i + a, row) for i, field in enumerate((ws, wk, robin))
        ]
        b_out[at, :] = fold_z(summed[0], lanes)
        kz_out[at, :] = summed[1]
        kx_out[at, :] = fold_z(summed[1], lanes)
        ky_out[at, :] = fold_z(wk[at, :], lanes)
        copies_x = 1.0
        if a == 0:
            copies_x = jnp.where(pos[0] > 0, 2.0, 1.0)
        if a == N - 1:
            copies_x = jnp.where(pos[0] < sizes[0] - 1, 2.0, 1.0)
        weights_a = w[a] * weights_yz
        advect_out[at, :] = scan_speed * weights_a
        diagonal_out[at, :] = fold_z(summed[2], lanes) + mass_coef * copies_x * weights_a
        inverse_out[at, :] = inverse_yz * (1.0 / copies_x)


def contract(m, values):
    half = N // 2
    total = [values[b] + values[N - 1 - b] for b in range(half)]
    apart = [values[b] - values[N - 1 - b] for b in range(half)]
    out = [None] * N
    for a in range(half):
        even = sum(float((m[a][b] + m[a][N - 1 - b]) / 2) * total[b] for b in range(half))
        odd = sum(float((m[a][b] - m[a][N - 1 - b]) / 2) * apart[b] for b in range(half))
        out[a] = even + odd
        out[N - 1 - a] = odd - even
    return out


def rotations(m, row):
    return [along(row.shape, [float(m[b][(b + s) % N]) for b in range(N)], row) for s in range(N)]


def contract_rows(coefs, v):
    out = coefs[0] * v
    for s in range(1, N):
        out += coefs[s] * pltpu.roll(v, N - s, axis=0)
    return out


def operate(pos, v, kx, ky, advect, xy_out, sends, low, high):
    d = lagrange_derivative()
    k, speed = tiles(kx), tiles(advect)
    flux = [k[a] * g - speed[a] * v[a] for a, g in enumerate(contract(d, v))]
    x = contract(d.T, flux)
    send(pos, 0, x[0], x[N - 1], sends[0], sends[1])
    row = row_index(v[0].shape)
    forward, back = rotations(d, row), rotations(d.T, row)
    for a in range(N):
        at = slice(N * a, N * a + N)
        y = contract_rows(back, ky[at, :] * contract_rows(forward, v[a]))
        low[a : a + 1, :] = y[0:1]
        high[a : a + 1, :] = y[N - 1 : N]
        xy_out[at, :] = x[a] + y
    send(pos, 1, low[...], high[...], sends[2], sends[3])


def along_z(v, xy, kz, diagonal, forward_1, forward_2, back_1, back_2, lanes, q_out):
    rows, size = v.shape
    columns = [slice(i, i + LANES) for i in range(0, size, LANES)]
    grad = times(jnp.concatenate([v[:, c] for c in columns], 0), forward_1, forward_2)
    flux = [kz[:, c] * grad[i * rows : (i + 1) * rows] for i, c in enumerate(columns)]
    back = times(jnp.concatenate(flux, 0), back_1, back_2)
    back = jnp.concatenate([back[i * rows : (i + 1) * rows] for i in range(len(columns))], 1)
    q_out[...] = fold_z(back, lanes) + (xy[...] + diagonal[...] * v[...])


def assemble(sizes, pos, q, recv):
    x_even, x_odd, y_even, y_odd = (recv[ORDER.index(i)] for i in range(4))
    x_low, x_high = received(sizes, pos, 0, x_even[...], x_odd[...])
    y_low, y_high = received(sizes, pos, 1, y_even[...], y_odd[...])
    row = row_index(y_low.shape)
    out = [q[N * a : N * a + N, :] + place(y_low, y_high, a, row) for a in range(N)]
    out[0] += x_low
    out[N - 1] += x_high
    return out


def first_kernel(sizes, b_in, kx, ky_in, advect, odd, even, lanes,
                 b_out, ky_out, xy_out, *refs):
    pos = position()
    low, high = received(sizes, pos, 0, even[...], odd[...])
    b, ky = tiles(b_in), tiles(ky_in)
    for a, side in ((0, low), (N - 1, high)):
        b[a] += fold_z(side[0:N], lanes)
        ky[a] += fold_z(side[3 * N : 4 * N], lanes)
    store(b_out, b)
    store(ky_out, ky)
    operate(pos, b, kx, ky_out, advect, xy_out, refs[:4], *refs[4:])


def first_z_kernel(sizes, b, xy, kz_in, diagonal_in, odd, even, f1, f2, b1, b2, lanes,
                   kz_out, diagonal_out, q_out):
    pos = position()
    low, high = received(sizes, pos, 0, even[...], odd[...])
    kz_out[...] = kz_in[...]
    diagonal_out[...] = diagonal_in[...]
    for a, side in ((0, low), (N - 1, high)):
        at = slice(N * a, N * a + N)
        kz_out[at, :] += side[N : 2 * N]
        diagonal_out[at, :] += fold_z(side[2 * N : 3 * N], lanes)
    along_z(b, xy, kz_out, diagonal_out, f1, f2, b1, b2, lanes, q_out)


def dots_row(pairs, inverse, first=0):
    shape = (N, LANES)
    lane = lax.broadcasted_iota(jnp.int32, shape, 1)
    row = jnp.zeros(shape, f32)
    scaled = {}
    for i, (u, v) in enumerate(pairs):
        if id(u) not in scaled:
            scaled[id(u)] = [x * m for x, m in zip(u, inverse)]
        product = sum(x * y for x, y in zip(scaled[id(u)], v))
        product = sum(product[:, j : j + LANES] for j in range(0, product.shape[1], LANES))
        row = jnp.where(lane == first + i, jnp.sum(product, axis=1, keepdims=True), row)
    return jnp.sum(row, axis=0, keepdims=True)


def for_all(row, out):
    for i in range(out.shape[0]):
        out[i] = row


def totals(gathered, count):
    row = jnp.sum(gathered[...], axis=0)
    return [jnp.broadcast_to(row[:, i : i + 1], row.shape) for i in range(count)]


def wide(scalar, like):
    return jnp.concatenate([scalar] * (like.shape[1] // scalar.shape[1]), 1)


def steps(br, bs, bw, bz, wr, ws, zr, zs, ww, wz, zz):
    alpha = br / bs
    omega = (wr - alpha * (ws + zr) + alpha * alpha * zs) / (
        ww - 2.0 * alpha * wz + alpha * alpha * zz
    )
    rho_next = (br - alpha * bs) - omega * (bw - alpha * bz)
    beta = rho_next / br * (alpha / omega)
    return alpha, omega, beta


def second_pairs(b, r, s, w, z):
    return [(w, b), (w, r), (w, s), (w, w), (w, z), (r, b), (r, z)]


def early_pairs(b, e):
    return [(e[i], b) for i in range(6)] + [(e[i], e[j]) for i in range(6) for j in range(i, 6)]


def late_pairs(b, e):
    return [(e[i], b) for i in (6, 7)] + [(e[j], e[i]) for j in (6, 7) for i in range(j + 1)]


EARLY = 34
LATE = 17


def guess(scalars, like):
    omega = wide(scalars[1:2, :], like)
    return 2.0 * omega, omega


def last_steps(sums, guessed_omega):
    names = second_pairs(*"brswz") + early_pairs("b", range(6)) + late_pairs("b", range(8))
    value = dict(zip(names, sums))
    g = lambda i, j: value[i, j] if (i, j) in value else value[j, i]
    second = steps(
        g("r", "b"), g(1, "b"), g("w", "b"), g(3, "b"),
        g("w", "r"), g("w", "s"), g("r", "z"), g(1, 3), g("w", "w"), g("w", "z"), g(3, 3),
    )
    alpha, omega, beta = second
    off_alpha, off_omega = alpha - 2.0 * guessed_omega, omega - guessed_omega
    ratio = off_omega / guessed_omega
    one, cross = jnp.ones_like(alpha), off_alpha * omega
    both = -off_alpha - beta * omega
    r = {0: one, 1: -off_alpha, 2: -off_omega, 3: cross, 4: -off_omega * guessed_omega}
    w = {2: one, 3: -off_alpha, 4: -off_omega, 5: cross}
    s = {1: beta, 2: one, 3: both, 4: -off_omega, 5: cross}
    z = {3: beta, 4: -ratio, 5: both, 6: one + ratio, 7: cross}
    with_b = lambda u: sum(c * g(i, "b") for i, c in u.items())
    times = lambda u: {i: sum(c * g(i, j) for j, c in u.items()) for i in range(8)}
    inner = lambda image, u: sum(c * image[i] for i, c in u.items())
    gw, gz = times(w), times(z)
    third = steps(
        with_b(r), with_b(s), with_b(w), with_b(z),
        inner(gw, r), inner(gw, s), inner(gz, r), inner(gz, s),
        inner(gw, w), inner(gw, z), inner(gz, z),
    )
    return second, third


def apply_kernel(sizes, q, x0, x1, y0, y1, kx, ky, advect, v_out, xy_out, *refs):
    pos = position()
    v = assemble(sizes, pos, q, (x0, x1, y0, y1))
    store(v_out, v)
    operate(pos, v, kx, ky, advect, xy_out, refs[:4], *refs[4:])


def z_kernel(*refs):
    along_z(*refs)


def first_dots_kernel(sizes, b, s, inverse, q, x0, x1, y0, y1, kx, ky, advect, z_out, xy_out, *refs):
    *sends, row_out, low, high, row, sem = refs
    pos = position()
    z = assemble(sizes, pos, q, (x0, x1, y0, y1))
    store(z_out, z)
    b, s = tiles(b), tiles(s)
    for_all(dots_row([(b, b), (b, s), (b, z), (s, s), (s, z), (z, z)], tiles(inverse)), row)
    copy = pltpu.make_async_copy(row, row_out, sem)
    copy.start()
    operate(pos, z, kx, ky, advect, xy_out, sends, low, high)
    copy.wait()


def first_steps_kernel(_, gathered, scalars):
    bb, bs, bz, ss, sz, zz = totals(gathered, 6)
    for i, value in enumerate(steps(bb, bs, bs, bz, bs, ss, bz, sz, ss, sz, zz)):
        scalars[i : i + 1, :] = value


def update_kernel(sizes, scalars, az, aaz, q, x0, x1, y0, y1, kx, ky, advect,
                  az_out, aaw_out, xy_out, *refs):
    pos = position()
    alpha, omega, beta = (wide(scalars[i : i + 1, :], az) for i in range(3))
    aaaz = assemble(sizes, pos, q, (x0, x1, y0, y1))
    az, aaz = tiles(az), tiles(aaz)
    aaw = [(az[i] - alpha * aaz[i]) - omega * (aaz[i] - alpha * aaaz[i]) for i in range(N)]
    az_next = [aaw[i] + beta * (az[i] - omega * aaz[i]) for i in range(N)]
    store(aaw_out, aaw)
    store(az_out, az_next)
    operate(pos, az_next, kx, ky, advect, xy_out, refs[:4], *refs[4:])


def update_rest_kernel(scalars, b, s, z, az, aaz, az_next, inverse,
                       x_out, r_out, p_out, s_out, w_out, z_out, aw_out, near_r_out, y_out, au_out, row):
    alpha, omega, beta = (wide(scalars[i : i + 1, :], s) for i in range(3))
    near_alpha, near_omega = guess(scalars, s)
    fields = [[] for _ in range(9)]
    for i in range(N):
        at = slice(N * i, N * i + N)
        b_, s_, z_, az_ = b[at, :], s[at, :], z[at, :], az[at, :]
        half, applied_half = b_ - alpha * s_, s_ - alpha * z_
        applied_twice = z_ - alpha * az_
        x_out[at, :] = alpha * b_ + omega * half
        r = half - omega * applied_half
        w = applied_half - omega * applied_twice
        aw = applied_twice - omega * (az_ - alpha * aaz[at, :])
        s_next = w + beta * (s_ - omega * z_)
        z_next = aw + beta * (z_ - omega * az_)
        p_out[at, :] = r + beta * (b_ - omega * s_)
        u = w - near_alpha * z_next
        au = aw - near_alpha * az_next[at, :]
        y = u - near_omega * au
        near_r = (r - near_alpha * s_next) - near_omega * u
        outs = r_out, s_out, w_out, z_out, aw_out, near_r_out, y_out, au_out
        values = r, s_next, w, z_next, aw, near_r, y, au
        for out, value in zip(outs, values):
            out[at, :] = value
        for kept, value in zip(fields, (b_, r, s_next, w, z_next, near_r, y, au, az_next[at, :])):
            kept.append(value)
    b_, r, s_next, w, z_next, near_r, y, au, az_ = fields
    pairs = second_pairs(b_, r, s_next, w, z_next)
    pairs += early_pairs(b_, [near_r, s_next, y, z_next, au, az_])
    row[...] = dots_row(pairs, tiles(inverse))


def late_dots_kernel(sizes, scalars, b, near_r, s, y, z, au, az, aaw, inverse, early, q,
                     x0, x1, y0, y1, aaz_out, row):
    aaz = assemble(sizes, position(), q, (x0, x1, y0, y1))
    store(aaz_out, aaz)
    alpha, omega = guess(scalars, s)
    e = [tiles(ref) for ref in (near_r, s, y, z, au, az)]
    aaw = tiles(aaw)
    ay = [e[4][i] - omega * (aaw[i] - alpha * aaz[i]) for i in range(N)]
    pairs = late_pairs(tiles(b), e + [ay, aaz])
    for_all(early[...] + dots_row(pairs, tiles(inverse), EARLY), row)


def last_kernel(gathered, scalars, x, p, r, s, w, z, aw, az, aaw, aaz, x_out, r_out):
    second, third = last_steps(totals(gathered, EARLY + LATE), scalars[1:2, :])
    alpha, omega, beta = (wide(value, s) for value in second)
    last_alpha, last_omega, _ = (wide(value, s) for value in third)
    for i in range(N):
        at = slice(N * i, N * i + N)
        p_, s_, z_, az_ = p[at, :], s[at, :], z[at, :], az[at, :]
        half, applied_half = r[at, :] - alpha * s_, w[at, :] - alpha * z_
        applied_twice = aw[at, :] - alpha * az_
        r_next = half - omega * applied_half
        w_next = applied_half - omega * applied_twice
        aw_next = applied_twice - omega * (aaw[at, :] - alpha * aaz[at, :])
        p_next = r_next + beta * (p_ - omega * s_)
        s_next = w_next + beta * (s_ - omega * z_)
        z_next = aw_next + beta * (z_ - omega * az_)
        last_half = r_next - last_alpha * s_next
        x_out[at, :] = (x[at, :] + alpha * p_ + omega * half) + (
            last_alpha * p_next + last_omega * last_half
        )
        r_out[at, :] = last_half - last_omega * (w_next - last_alpha * z_next)


def pairings(sizes):
    count_x, count_y = sizes
    grid = [(i, j) for i in range(count_x) for j in range(count_y)]
    number = lambda i, j: i * count_y + j
    step = lambda i: i + 1 if i % 2 else i - 1
    x_even = [(number(i, j), number(i ^ 1, j)) for i, j in grid]
    x_odd = [
        (number(i, j), number(step(i), j) if 0 < i < count_x - 1 else number(i, j ^ 1)) for i, j in grid
    ]
    y_even = [(number(i, j), number(i, j ^ 1)) for i, j in grid]
    y_odd = [
        (number(i, j), number(i, step(j)) if 0 < j < count_y - 1 else number(i ^ 1, j)) for i, j in grid
    ]
    return (x_even, x_odd), (y_even, y_odd)


def per_device(sizes, source, conductivity, robin_flags, htc_class, htc_table):
    shape = source.shape
    elems_z = robin_flags.shape[2]
    rows, size = shape[0] * shape[1], shape[2]
    assert robin_flags.shape[:2] == (1, 1) and size % LANES == 0
    assert sizes[0] % 2 == 0 and sizes[1] % 2 == 0
    devices = sizes[0] * sizes[1]
    *z_mats, lanes = constants(elems_z)
    x_pairs, y_pairs = pairings(sizes)

    def struct(n=rows):
        return jax.ShapeDtypeStruct((n, size), f32)

    field = struct()
    faces = [struct(N)] * 4
    row = jax.ShapeDtypeStruct((devices, 1, 128), f32)
    scalars = jax.ShapeDtypeStruct((N, 128), f32)
    side = [pltpu.VMEM((N, size), f32)] * 2
    row_side = [pltpu.VMEM(row.shape, f32), pltpu.SemaphoreType.DMA]

    def call(kernel, outs, *operands, scratch=(), hbm=0, limit=32, cost=0, hbm_out=0):
        specs = [HBM] * hbm + [VMEM] * (len(operands) - hbm)
        return pl.pallas_call(
            kernel,
            out_shape=outs,
            in_specs=specs,
            out_specs=[VMEM] * (len(outs) - hbm_out) + [HBM] * hbm_out,
            scratch_shapes=list(scratch),
            compiler_params=pltpu.CompilerParams(vmem_limit_bytes=limit * 1024 * 1024),
            cost_estimate=pl.CostEstimate(flops=cost, bytes_accessed=cost, transcendentals=0)
            if cost
            else None,
        )(*operands)

    def permute(values, pairs):
        return lax.ppermute(values, ("gx", "gy"), pairs)

    def exchange(pairs, even, odd):
        return permute(odd, pairs[1]), permute(even, pairs[0])

    def swap(parts):
        x_odd = permute(parts[1], x_pairs[1])
        y_odd = permute(parts[3], y_pairs[1])
        x_even = permute(parts[0], x_pairs[0])
        recv = x_even, x_odd, permute(parts[2], y_pairs[0]), y_odd
        return tuple(recv[i] for i in ORDER)

    def spread(values):
        return lax.all_to_all(values, ("gx", "gy"), 0, 0)

    given = (
        source.reshape(rows, size), conductivity.reshape(rows, size),
        robin_flags.reshape(1, elems_z), htc_class.reshape(1, elems_z), htc_table.reshape(1, -1),
    )
    parts = call(
        functools.partial(field_kernel, sizes), [struct(3 * N)] * 2, *given,
        hbm=5,
        limit=60,
        scratch=[pltpu.VMEM(v.shape, v.dtype) for v in given]
        + [pltpu.VMEM((3 * N, size), f32)] * 2
        + [pltpu.SemaphoreType.DMA((5,))],
    )
    recv = exchange(y_pairs, *parts)
    ws, wk, robin = call(functools.partial(whole_field_kernel, sizes), [field] * 3, *given, cost=COST)
    parts = call(
        functools.partial(fold_y_kernel, sizes), [struct(4 * N)] * 2, ws, wk, robin, *recv
    )
    b, kx, ky, kz, advect, diagonal, inverse = call(
        functools.partial(prepare_kernel, sizes), [field] * 7, ws, wk, robin, *recv, lanes,
        cost=COST,
    )
    recv = exchange(x_pairs, *parts)
    b, ky, xy, *parts = call(
        functools.partial(first_kernel, sizes), [field] * 3 + faces,
        b, kx, ky, advect, *recv, lanes, scratch=side,
    )
    kz, diagonal, q = call(
        functools.partial(first_z_kernel, sizes), [field] * 3,
        b, xy, kz, diagonal, *recv, *z_mats, lanes, cost=COST,
    )
    coefs = (kx, ky, advect)
    z_args = (kz, diagonal, *z_mats, lanes)
    recv = swap(parts)

    def apply(q, recv):
        v, xy, *parts = call(
            functools.partial(apply_kernel, sizes), [field] * 2 + faces, q, *recv, *coefs, scratch=side
        )
        recv = swap(parts)
        (q,) = call(z_kernel, [field], v, xy, *z_args, cost=COST)
        return v, q, recv

    s, q, recv = apply(q, recv)
    z, xy, *parts, products = call(
        functools.partial(first_dots_kernel, sizes), [field] * 2 + faces + [row],
        b, s, inverse, q, *recv, *coefs, scratch=side + row_side, hbm_out=1,
    )
    gathered = spread(products)
    recv = swap(parts)
    (q,) = call(z_kernel, [field], z, xy, *z_args, cost=COST)
    az, q, recv = apply(q, recv)
    aaz, q, recv = apply(q, recv)
    (values,) = call(first_steps_kernel, [scalars], q, gathered, cost=COST)
    az_next, aaw, xy, *parts = call(
        functools.partial(update_kernel, sizes),
        [field] * 3 + faces,
        values, az, aaz, q, *recv, *coefs, scratch=side,
    )
    recv = swap(parts)
    (q,) = call(z_kernel, [field], az_next, xy, *z_args, cost=COST)
    x, r, p, s, w, z, aw, near_r, y, au, early = call(
        update_rest_kernel, [field] * 10 + [jax.ShapeDtypeStruct((1, LANES), f32)],
        values, b, s, z, az, aaz, az_next, inverse, cost=COST,
    )
    az = az_next
    aaz, products = call(
        functools.partial(late_dots_kernel, sizes), [field, row],
        values, b, near_r, s, y, z, au, az, aaw, inverse, early, q, *recv,
    )
    x, r = call(
        last_kernel, [field] * 2, spread(products), values, x, p, r, s, w, z, aw, az, aaw, aaz
    )
    return x.reshape(shape), r.reshape(shape)


def solution(mesh):
    sizes = (mesh.shape["gx"], mesh.shape["gy"])
    field = P("gx", "gy", None)
    return jax.shard_map(
        functools.partial(per_device, sizes),
        mesh=mesh,
        in_specs=(field, field, field, field, P()),
        out_specs=(field, field),
        check_vma=False,
    )
```

```python
import functools

import jax
import jax.numpy as jnp
import numpy as np
from jax import lax
from jax.experimental import pallas as pl
from jax.experimental.pallas import tpu as pltpu
from jax.sharding import PartitionSpec as P

ITERS = 3
N = 8

gll_points = (
    -1.0,
    -0.8717401485096066,
    -0.5917001814331423,
    -0.2092992179024789,
    0.2092992179024789,
    0.5917001814331423,
    0.8717401485096066,
    1.0,
)
gll_weights = (
    0.03571428571428571,
    0.21070422714350603,
    0.3411226924835044,
    0.4124587946587038,
    0.4124587946587038,
    0.3411226924835044,
    0.21070422714350603,
    0.03571428571428571,
)
mass_coef = 0.2
scan_speed = 2.0
f32 = jnp.float32
VMEM = pl.BlockSpec(memory_space=pltpu.VMEM)
HBM = pl.BlockSpec(memory_space=pl.ANY)
COST = 1 << 20
LANES = 128
ORDER = (3, 0, 1, 2)
dot = functools.partial(jnp.dot, precision=lax.Precision.HIGHEST, preferred_element_type=f32)


def lagrange_derivative():
    points = np.array(gll_points)
    barycentric = np.array(
        [1.0 / np.prod([points[j] - points[m] for m in range(N) if m != j]) for j in range(N)]
    )
    derivative = np.zeros((N, N))
    for a in range(N):
        for b in range(N):
            if a != b:
                derivative[a, b] = barycentric[b] / barycentric[a] / (points[a] - points[b])
        derivative[a, a] = -np.sum(derivative[a])
    return derivative.astype(np.float32)


def pieces(v):
    high = v.astype(jnp.bfloat16)
    rest = v - high.astype(f32)
    middle = rest.astype(jnp.bfloat16)
    return high, middle, (rest - middle.astype(f32)).astype(jnp.bfloat16)


def stacked(m):
    high = m.astype(jnp.bfloat16).astype(np.float32)
    middle = (m - high).astype(jnp.bfloat16).astype(np.float32)
    low = m - high - middle
    both = np.concatenate([high, middle], 1)
    return [
        jnp.asarray(np.concatenate([both, both], 0), jnp.bfloat16),
        jnp.asarray(np.concatenate([low, high], 0), jnp.bfloat16),
    ]


def constants(elems_z):
    z_back = np.kron(np.eye(LANES // N, dtype=np.float32), lagrange_derivative())
    lane = np.arange(N * elems_z)
    low = (lane % N == 0) & (lane > 0)
    high = (lane % N == N - 1) & (lane < N * elems_z - 1)
    lanes = np.stack([low, high] + [0 * lane] * 6).astype(np.float32)
    return stacked(z_back.T) + stacked(z_back) + [jnp.asarray(lanes)]


def times(v, first, second):
    high, middle, low = pieces(v)
    product = functools.partial(jnp.dot, preferred_element_type=f32)
    large = product(jnp.concatenate([high, middle], 1), first[...])
    small = product(jnp.concatenate([high, low], 1), second[...])
    return (large[:, :LANES] + large[:, LANES:]) + small


def weights_1d():
    return [float(np.float32(x)) for x in gll_weights]


def position():
    return lax.axis_index("gx"), lax.axis_index("gy")


def tiles(ref):
    return [ref[N * a : N * a + N, :] for a in range(N)]


def store(ref, values):
    for a in range(N):
        ref[N * a : N * a + N, :] = values[a]


def row_index(shape):
    return lax.broadcasted_iota(jnp.int32, shape, 0)


def along(shape, values, index):
    out = jnp.full(shape, values[0], f32)
    for i in range(1, len(values)):
        out = jnp.where(index == i, values[i], out)
    return out


def fold_z(v, lanes):
    size = v.shape[1]
    return (
        v
        + pltpu.roll(v, 1, axis=1) * lanes[0:1, :]
        + pltpu.roll(v, size - 1, axis=1) * lanes[1:2, :]
    )


def pick(pos, axis, even, odd):
    return jnp.where(pos[axis] % 2 == 0, even, odd)


def send(pos, axis, low, high, even_ref, odd_ref):
    even_ref[...] = pick(pos, axis, high, low)
    odd_ref[...] = pick(pos, axis, low, high)


def received(sizes, pos, axis, even, odd):
    low = jnp.where(pos[axis] > 0, pick(pos, axis, odd, even), 0.0)
    high = jnp.where(pos[axis] < sizes[axis] - 1, pick(pos, axis, even, odd), 0.0)
    return low, high


def place(low, high, a, row):
    return jnp.where(row == 0, low[a : a + 1], jnp.where(row == N - 1, high[a : a + 1], 0.0))


def robin_tiles(sizes, pos, table, flags, classes, size):
    elems_z = flags.shape[1]
    coefficient = jnp.zeros(flags.shape, f32)
    for c in range(table.shape[1]):
        coefficient = jnp.where(classes[...] == c, table[:, c : c + 1], coefficient)
    element = lax.broadcasted_iota(jnp.int32, flags.shape, 1)
    sides = [
        pos[0] == 0, pos[0] == sizes[0] - 1, pos[1] == 0, pos[1] == sizes[1] - 1,
        element == 0, element == elems_z - 1,
    ]
    rows = []
    for bit, side in enumerate(sides):
        flagged = (flags[...] >> bit) % 2 == 1
        rows.append(jnp.where(flagged & side, coefficient, 0.0))
    rows += [jnp.zeros(flags.shape, f32)] * 2
    spread = lax.broadcasted_iota(jnp.int32, (elems_z, size), 1) // N == row_index((elems_z, size))
    faces = dot(jnp.concatenate(rows, 0), spread.astype(f32))
    node = lax.broadcasted_iota(jnp.int32, (1, size), 1) % N
    w = weights_1d()
    w_z = along((1, size), w, node)
    row = row_index((N, size))
    w_b = along((N, size), w, row)
    w_bz = w_b * w_z
    ends_z = jnp.where(node == 0, faces[4:5], 0.0) + jnp.where(node == N - 1, faces[5:6], 0.0)
    common = place(faces[2:3] * w_z, faces[3:4] * w_z, 0, row) + w_b * ends_z
    robin = [w[a] * common for a in range(N)]
    robin[0] += w_bz * faces[0:1]
    robin[N - 1] += w_bz * faces[1:2]
    return robin, w_bz


def field_kernel(sizes, source, k, flags, classes, table, even_out, odd_out,
                 v_ref, k_ref, flags_ref, classes_ref, table_ref, low, high, sems):
    pairs = (
        (flags, flags_ref), (classes, classes_ref), (table, table_ref), (source, v_ref), (k, k_ref),
    )
    copies = [pltpu.make_async_copy(*pair, sems.at[i]) for i, pair in enumerate(pairs)]
    for copy in copies:
        copy.start()
    for copy in copies[:3]:
        copy.wait()
    pos = position()
    robin, w_bz = robin_tiles(sizes, pos, table_ref, flags_ref, classes_ref, source.shape[1])
    for copy in copies[3:]:
        copy.wait()
    w = weights_1d()
    ws = [w[a] * w_bz * v for a, v in enumerate(tiles(v_ref))]
    wk = [w[a] * w_bz * v for a, v in enumerate(tiles(k_ref))]
    for i, field in enumerate((ws, wk, robin)):
        for a in range(N):
            low[N * i + a : N * i + a + 1, :] = field[a][0:1]
            high[N * i + a : N * i + a + 1, :] = field[a][N - 1 : N]
    send(pos, 1, low[...], high[...], even_out, odd_out)


def whole_field_kernel(sizes, source, k, flags, classes, table, ws_out, wk_out, robin_out):
    robin, w_bz = robin_tiles(sizes, position(), table, flags, classes, source.shape[1])
    w = weights_1d()
    store(robin_out, robin)
    store(ws_out, [w[a] * w_bz * v for a, v in enumerate(tiles(source))])
    store(wk_out, [w[a] * w_bz * v for a, v in enumerate(tiles(k))])


def fold_y_kernel(sizes, ws, wk, robin, odd, even, even_out, odd_out):
    pos = position()
    low, high = received(sizes, pos, 1, even[...], odd[...])
    row = row_index((N, ws.shape[1]))
    sides = []
    for a in (0, N - 1):
        part = [
            field[N * a : N * a + N, :] + place(low, high, N * i + a, row)
            for i, field in enumerate((ws, wk, robin))
        ]
        sides.append(jnp.concatenate(part + [wk[N * a : N * a + N, :]], 0))
    send(pos, 0, sides[0], sides[1], even_out, odd_out)


def prepare_kernel(sizes, ws, wk, robin, odd, even, lanes,
                   b_out, kx_out, ky_out, kz_out, advect_out, diagonal_out, inverse_out):
    pos = position()
    low, high = received(sizes, pos, 1, even[...], odd[...])
    shape = (N, ws.shape[1])
    row = row_index(shape)
    w = weights_1d()
    node = lax.broadcasted_iota(jnp.int32, (1, shape[1]), 1) % N
    copies_z = 1.0 + lanes[0:1, :] + lanes[1:2, :]
    shared_y = ((row == 0) & (pos[1] > 0)) | ((row == N - 1) & (pos[1] < sizes[1] - 1))
    copies_yz = jnp.where(shared_y, 2.0, 1.0) * copies_z
    weights_yz = along(shape, w, row) * along((1, shape[1]), w, node) * copies_yz
    inverse_yz = 1.0 / copies_yz
    for a in range(N):
        at = slice(N * a, N * a + N)
        summed = [
            field[at, :] + place(low, high, N * i + a, row) for i, field in enumerate((ws, wk, robin))
        ]
        b_out[at, :] = fold_z(summed[0], lanes)
        kz_out[at, :] = summed[1]
        kx_out[at, :] = fold_z(summed[1], lanes)
        ky_out[at, :] = fold_z(wk[at, :], lanes)
        copies_x = 1.0
        if a == 0:
            copies_x = jnp.where(pos[0] > 0, 2.0, 1.0)
        if a == N - 1:
            copies_x = jnp.where(pos[0] < sizes[0] - 1, 2.0, 1.0)
        weights_a = w[a] * weights_yz
        advect_out[at, :] = scan_speed * weights_a
        diagonal_out[at, :] = fold_z(summed[2], lanes) + mass_coef * copies_x * weights_a
        inverse_out[at, :] = inverse_yz * (1.0 / copies_x)


def contract(m, values):
    half = N // 2
    total = [values[b] + values[N - 1 - b] for b in range(half)]
    apart = [values[b] - values[N - 1 - b] for b in range(half)]
    out = [None] * N
    for a in range(half):
        even = sum(float((m[a][b] + m[a][N - 1 - b]) / 2) * total[b] for b in range(half))
        odd = sum(float((m[a][b] - m[a][N - 1 - b]) / 2) * apart[b] for b in range(half))
        out[a] = even + odd
        out[N - 1 - a] = odd - even
    return out


def rotations(m, row):
    return [along(row.shape, [float(m[b][(b + s) % N]) for b in range(N)], row) for s in range(N)]


def contract_rows(coefs, v):
    out = coefs[0] * v
    for s in range(1, N):
        out += coefs[s] * pltpu.roll(v, N - s, axis=0)
    return out


def operate(pos, v, kx, ky, advect, xy_out, sends, low, high):
    d = lagrange_derivative()
    k, speed = tiles(kx), tiles(advect)
    flux = [k[a] * g - speed[a] * v[a] for a, g in enumerate(contract(d, v))]
    x = contract(d.T, flux)
    send(pos, 0, x[0], x[N - 1], sends[0], sends[1])
    row = row_index(v[0].shape)
    forward, back = rotations(d, row), rotations(d.T, row)
    for a in range(N):
        at = slice(N * a, N * a + N)
        y = contract_rows(back, ky[at, :] * contract_rows(forward, v[a]))
        low[a : a + 1, :] = y[0:1]
        high[a : a + 1, :] = y[N - 1 : N]
        xy_out[at, :] = x[a] + y
    send(pos, 1, low[...], high[...], sends[2], sends[3])


def along_z(v, xy, kz, diagonal, forward_1, forward_2, back_1, back_2, lanes, q_out):
    rows, size = v.shape
    columns = [slice(i, i + LANES) for i in range(0, size, LANES)]
    grad = times(jnp.concatenate([v[:, c] for c in columns], 0), forward_1, forward_2)
    flux = [kz[:, c] * grad[i * rows : (i + 1) * rows] for i, c in enumerate(columns)]
    back = times(jnp.concatenate(flux, 0), back_1, back_2)
    back = jnp.concatenate([back[i * rows : (i + 1) * rows] for i in range(len(columns))], 1)
    q_out[...] = fold_z(back, lanes) + (xy[...] + diagonal[...] * v[...])


def assemble(sizes, pos, q, recv):
    x_even, x_odd, y_even, y_odd = (recv[ORDER.index(i)] for i in range(4))
    x_low, x_high = received(sizes, pos, 0, x_even[...], x_odd[...])
    y_low, y_high = received(sizes, pos, 1, y_even[...], y_odd[...])
    row = row_index(y_low.shape)
    out = [q[N * a : N * a + N, :] + place(y_low, y_high, a, row) for a in range(N)]
    out[0] += x_low
    out[N - 1] += x_high
    return out


def first_kernel(sizes, b_in, kx, ky_in, advect, odd, even, lanes,
                 b_out, ky_out, xy_out, *refs):
    pos = position()
    low, high = received(sizes, pos, 0, even[...], odd[...])
    b, ky = tiles(b_in), tiles(ky_in)
    for a, side in ((0, low), (N - 1, high)):
        b[a] += fold_z(side[0:N], lanes)
        ky[a] += fold_z(side[3 * N : 4 * N], lanes)
    store(b_out, b)
    store(ky_out, ky)
    operate(pos, b, kx, ky_out, advect, xy_out, refs[:4], *refs[4:])


def first_z_kernel(sizes, b, xy, kz_in, diagonal_in, odd, even, f1, f2, b1, b2, lanes,
                   kz_out, diagonal_out, q_out):
    pos = position()
    low, high = received(sizes, pos, 0, even[...], odd[...])
    kz_out[...] = kz_in[...]
    diagonal_out[...] = diagonal_in[...]
    for a, side in ((0, low), (N - 1, high)):
        at = slice(N * a, N * a + N)
        kz_out[at, :] += side[N : 2 * N]
        diagonal_out[at, :] += fold_z(side[2 * N : 3 * N], lanes)
    along_z(b, xy, kz_out, diagonal_out, f1, f2, b1, b2, lanes, q_out)


def dots_row(pairs, inverse, first=0):
    shape = (N, LANES)
    lane = lax.broadcasted_iota(jnp.int32, shape, 1)
    row = jnp.zeros(shape, f32)
    scaled = {}
    for i, (u, v) in enumerate(pairs):
        if id(u) not in scaled:
            scaled[id(u)] = [x * m for x, m in zip(u, inverse)]
        product = sum(x * y for x, y in zip(scaled[id(u)], v))
        product = sum(product[:, j : j + LANES] for j in range(0, product.shape[1], LANES))
        row = jnp.where(lane == first + i, jnp.sum(product, axis=1, keepdims=True), row)
    return jnp.sum(row, axis=0, keepdims=True)


def for_all(row, out):
    for i in range(out.shape[0]):
        out[i] = row


def totals(gathered, count):
    row = jnp.sum(gathered[...], axis=0)
    return [jnp.broadcast_to(row[:, i : i + 1], row.shape) for i in range(count)]


def wide(scalar, like):
    return jnp.concatenate([scalar] * (like.shape[1] // scalar.shape[1]), 1)


def steps(br, bs, bw, bz, wr, ws, zr, zs, ww, wz, zz):
    alpha = br / bs
    omega = (wr - alpha * (ws + zr) + alpha * alpha * zs) / (
        ww - 2.0 * alpha * wz + alpha * alpha * zz
    )
    rho_next = (br - alpha * bs) - omega * (bw - alpha * bz)
    beta = rho_next / br * (alpha / omega)
    return alpha, omega, beta


def second_pairs(b, r, s, w, z):
    return [(w, b), (w, r), (w, s), (w, w), (w, z), (r, b), (r, z)]


def early_pairs(b, e):
    return [(e[i], b) for i in range(6)] + [(e[i], e[j]) for i in range(6) for j in range(i, 6)]


def late_pairs(b, e):
    return [(e[i], b) for i in (6, 7)] + [(e[j], e[i]) for j in (6, 7) for i in range(j + 1)]


EARLY = 34
LATE = 17


def guess(scalars, like):
    omega = wide(scalars[1:2, :], like)
    return 2.0 * omega, omega


def last_steps(sums, guessed_omega):
    names = second_pairs(*"brswz") + early_pairs("b", range(6)) + late_pairs("b", range(8))
    value = dict(zip(names, sums))
    g = lambda i, j: value[i, j] if (i, j) in value else value[j, i]
    second = steps(
        g("r", "b"), g(1, "b"), g("w", "b"), g(3, "b"),
        g("w", "r"), g("w", "s"), g("r", "z"), g(1, 3), g("w", "w"), g("w", "z"), g(3, 3),
    )
    alpha, omega, beta = second
    off_alpha, off_omega = alpha - 2.0 * guessed_omega, omega - guessed_omega
    ratio = off_omega / guessed_omega
    one, cross = jnp.ones_like(alpha), off_alpha * omega
    both = -off_alpha - beta * omega
    r = {0: one, 1: -off_alpha, 2: -off_omega, 3: cross, 4: -off_omega * guessed_omega}
    w = {2: one, 3: -off_alpha, 4: -off_omega, 5: cross}
    s = {1: beta, 2: one, 3: both, 4: -off_omega, 5: cross}
    z = {3: beta, 4: -ratio, 5: both, 6: one + ratio, 7: cross}
    with_b = lambda u: sum(c * g(i, "b") for i, c in u.items())
    times = lambda u: {i: sum(c * g(i, j) for j, c in u.items()) for i in range(8)}
    inner = lambda image, u: sum(c * image[i] for i, c in u.items())
    gw, gz = times(w), times(z)
    third = steps(
        with_b(r), with_b(s), with_b(w), with_b(z),
        inner(gw, r), inner(gw, s), inner(gz, r), inner(gz, s),
        inner(gw, w), inner(gw, z), inner(gz, z),
    )
    return second, third


def apply_kernel(sizes, q, x0, x1, y0, y1, kx, ky, advect, v_out, xy_out, *refs):
    pos = position()
    v = assemble(sizes, pos, q, (x0, x1, y0, y1))
    store(v_out, v)
    operate(pos, v, kx, ky, advect, xy_out, refs[:4], *refs[4:])


def z_kernel(*refs):
    along_z(*refs)


def z_dots_kernel(b, s, inverse, z, *refs):
    *shared, row_out, row, sem = refs
    b, s, z_ = tiles(b), tiles(s), tiles(z)
    for_all(dots_row([(b, b), (b, s), (b, z_), (s, s), (s, z_), (z_, z_)], tiles(inverse)), row)
    copy = pltpu.make_async_copy(row, row_out, sem)
    copy.start()
    along_z(z, *shared)
    copy.wait()


def first_steps_kernel(_, gathered, scalars):
    bb, bs, bz, ss, sz, zz = totals(gathered, 6)
    for i, value in enumerate(steps(bb, bs, bs, bz, bs, ss, bz, sz, ss, sz, zz)):
        scalars[i : i + 1, :] = value


def update_kernel(sizes, scalars, az, aaz, q, x0, x1, y0, y1, kx, ky, advect,
                  az_out, aaw_out, xy_out, *refs):
    pos = position()
    alpha, omega, beta = (wide(scalars[i : i + 1, :], az) for i in range(3))
    aaaz = assemble(sizes, pos, q, (x0, x1, y0, y1))
    az, aaz = tiles(az), tiles(aaz)
    aaw = [(az[i] - alpha * aaz[i]) - omega * (aaz[i] - alpha * aaaz[i]) for i in range(N)]
    az_next = [aaw[i] + beta * (az[i] - omega * aaz[i]) for i in range(N)]
    store(aaw_out, aaw)
    store(az_out, az_next)
    operate(pos, az_next, kx, ky, advect, xy_out, refs[:4], *refs[4:])


def update_rest_kernel(scalars, b, s, z, az, aaz, az_next, inverse,
                       x_out, r_out, p_out, s_out, w_out, z_out, aw_out, near_r_out, y_out, au_out, row):
    alpha, omega, beta = (wide(scalars[i : i + 1, :], s) for i in range(3))
    near_alpha, near_omega = guess(scalars, s)
    fields = [[] for _ in range(9)]
    for i in range(N):
        at = slice(N * i, N * i + N)
        b_, s_, z_, az_ = b[at, :], s[at, :], z[at, :], az[at, :]
        half, applied_half = b_ - alpha * s_, s_ - alpha * z_
        applied_twice = z_ - alpha * az_
        x_out[at, :] = alpha * b_ + omega * half
        r = half - omega * applied_half
        w = applied_half - omega * applied_twice
        aw = applied_twice - omega * (az_ - alpha * aaz[at, :])
        s_next = w + beta * (s_ - omega * z_)
        z_next = aw + beta * (z_ - omega * az_)
        p_out[at, :] = r + beta * (b_ - omega * s_)
        u = w - near_alpha * z_next
        au = aw - near_alpha * az_next[at, :]
        y = u - near_omega * au
        near_r = (r - near_alpha * s_next) - near_omega * u
        outs = r_out, s_out, w_out, z_out, aw_out, near_r_out, y_out, au_out
        values = r, s_next, w, z_next, aw, near_r, y, au
        for out, value in zip(outs, values):
            out[at, :] = value
        for kept, value in zip(fields, (b_, r, s_next, w, z_next, near_r, y, au, az_next[at, :])):
            kept.append(value)
    b_, r, s_next, w, z_next, near_r, y, au, az_ = fields
    pairs = second_pairs(b_, r, s_next, w, z_next)
    pairs += early_pairs(b_, [near_r, s_next, y, z_next, au, az_])
    row[...] = dots_row(pairs, tiles(inverse))


def late_dots_kernel(sizes, scalars, b, near_r, s, y, z, au, az, aaw, inverse, early, q,
                     x0, x1, y0, y1, aaz_out, row):
    aaz = assemble(sizes, position(), q, (x0, x1, y0, y1))
    store(aaz_out, aaz)
    alpha, omega = guess(scalars, s)
    e = [tiles(ref) for ref in (near_r, s, y, z, au, az)]
    aaw = tiles(aaw)
    ay = [e[4][i] - omega * (aaw[i] - alpha * aaz[i]) for i in range(N)]
    pairs = late_pairs(tiles(b), e + [ay, aaz])
    for_all(early[...] + dots_row(pairs, tiles(inverse), EARLY), row)


def last_kernel(gathered, scalars, x, p, r, s, w, z, aw, az, aaw, aaz, x_out, r_out):
    second, third = last_steps(totals(gathered, EARLY + LATE), scalars[1:2, :])
    alpha, omega, beta = (wide(value, s) for value in second)
    last_alpha, last_omega, _ = (wide(value, s) for value in third)
    for i in range(N):
        at = slice(N * i, N * i + N)
        p_, s_, z_, az_ = p[at, :], s[at, :], z[at, :], az[at, :]
        half, applied_half = r[at, :] - alpha * s_, w[at, :] - alpha * z_
        applied_twice = aw[at, :] - alpha * az_
        r_next = half - omega * applied_half
        w_next = applied_half - omega * applied_twice
        aw_next = applied_twice - omega * (aaw[at, :] - alpha * aaz[at, :])
        p_next = r_next + beta * (p_ - omega * s_)
        s_next = w_next + beta * (s_ - omega * z_)
        z_next = aw_next + beta * (z_ - omega * az_)
        last_half = r_next - last_alpha * s_next
        x_out[at, :] = (x[at, :] + alpha * p_ + omega * half) + (
            last_alpha * p_next + last_omega * last_half
        )
        r_out[at, :] = last_half - last_omega * (w_next - last_alpha * z_next)


def pairings(sizes):
    count_x, count_y = sizes
    grid = [(i, j) for i in range(count_x) for j in range(count_y)]
    number = lambda i, j: i * count_y + j
    step = lambda i: i + 1 if i % 2 else i - 1
    x_even = [(number(i, j), number(i ^ 1, j)) for i, j in grid]
    x_odd = [
        (number(i, j), number(step(i), j) if 0 < i < count_x - 1 else number(i, j ^ 1)) for i, j in grid
    ]
    y_even = [(number(i, j), number(i, j ^ 1)) for i, j in grid]
    y_odd = [
        (number(i, j), number(i, step(j)) if 0 < j < count_y - 1 else number(i ^ 1, j)) for i, j in grid
    ]
    return (x_even, x_odd), (y_even, y_odd)


def per_device(sizes, source, conductivity, robin_flags, htc_class, htc_table):
    shape = source.shape
    elems_z = robin_flags.shape[2]
    rows, size = shape[0] * shape[1], shape[2]
    assert robin_flags.shape[:2] == (1, 1) and size % LANES == 0
    assert sizes[0] % 2 == 0 and sizes[1] % 2 == 0
    devices = sizes[0] * sizes[1]
    *z_mats, lanes = constants(elems_z)
    x_pairs, y_pairs = pairings(sizes)

    def struct(n=rows):
        return jax.ShapeDtypeStruct((n, size), f32)

    field = struct()
    faces = [struct(N)] * 4
    row = jax.ShapeDtypeStruct((devices, 1, 128), f32)
    scalars = jax.ShapeDtypeStruct((N, 128), f32)
    side = [pltpu.VMEM((N, size), f32)] * 2
    row_side = [pltpu.VMEM(row.shape, f32), pltpu.SemaphoreType.DMA]

    def call(kernel, outs, *operands, scratch=(), hbm=0, limit=32, cost=0, hbm_out=0):
        specs = [HBM] * hbm + [VMEM] * (len(operands) - hbm)
        return pl.pallas_call(
            kernel,
            out_shape=outs,
            in_specs=specs,
            out_specs=[VMEM] * (len(outs) - hbm_out) + [HBM] * hbm_out,
            scratch_shapes=list(scratch),
            compiler_params=pltpu.CompilerParams(vmem_limit_bytes=limit * 1024 * 1024),
            cost_estimate=pl.CostEstimate(flops=cost, bytes_accessed=cost, transcendentals=0)
            if cost
            else None,
        )(*operands)

    def permute(values, pairs):
        return lax.ppermute(values, ("gx", "gy"), pairs)

    def exchange(pairs, even, odd):
        return permute(odd, pairs[1]), permute(even, pairs[0])

    def swap(parts):
        x_odd = permute(parts[1], x_pairs[1])
        y_odd = permute(parts[3], y_pairs[1])
        x_even = permute(parts[0], x_pairs[0])
        recv = x_even, x_odd, permute(parts[2], y_pairs[0]), y_odd
        return tuple(recv[i] for i in ORDER)

    def spread(values):
        return lax.all_to_all(values, ("gx", "gy"), 0, 0)

    given = (
        source.reshape(rows, size), conductivity.reshape(rows, size),
        robin_flags.reshape(1, elems_z), htc_class.reshape(1, elems_z), htc_table.reshape(1, -1),
    )
    parts = call(
        functools.partial(field_kernel, sizes), [struct(3 * N)] * 2, *given,
        hbm=5,
        limit=60,
        scratch=[pltpu.VMEM(v.shape, v.dtype) for v in given]
        + [pltpu.VMEM((3 * N, size), f32)] * 2
        + [pltpu.SemaphoreType.DMA((5,))],
    )
    recv = exchange(y_pairs, *parts)
    ws, wk, robin = call(functools.partial(whole_field_kernel, sizes), [field] * 3, *given, cost=COST)
    parts = call(
        functools.partial(fold_y_kernel, sizes), [struct(4 * N)] * 2, ws, wk, robin, *recv
    )
    b, kx, ky, kz, advect, diagonal, inverse = call(
        functools.partial(prepare_kernel, sizes), [field] * 7, ws, wk, robin, *recv, lanes,
        cost=COST,
    )
    recv = exchange(x_pairs, *parts)
    b, ky, xy, *parts = call(
        functools.partial(first_kernel, sizes), [field] * 3 + faces,
        b, kx, ky, advect, *recv, lanes, scratch=side,
    )
    kz, diagonal, q = call(
        functools.partial(first_z_kernel, sizes), [field] * 3,
        b, xy, kz, diagonal, *recv, *z_mats, lanes, cost=COST,
    )
    coefs = (kx, ky, advect)
    z_args = (kz, diagonal, *z_mats, lanes)
    recv = swap(parts)

    def apply(q, recv):
        v, xy, *parts = call(
            functools.partial(apply_kernel, sizes), [field] * 2 + faces, q, *recv, *coefs, scratch=side
        )
        recv = swap(parts)
        (q,) = call(z_kernel, [field], v, xy, *z_args, cost=COST)
        return v, q, recv

    s, q, recv = apply(q, recv)
    z, xy, *parts = call(
        functools.partial(apply_kernel, sizes), [field] * 2 + faces, q, *recv, *coefs, scratch=side
    )
    recv = swap(parts)
    q, products = call(
        z_dots_kernel, [field, row], b, s, inverse, z, xy, *z_args,
        cost=COST, scratch=row_side, hbm_out=1,
    )
    gathered = spread(products)
    az, q, recv = apply(q, recv)
    aaz, q, recv = apply(q, recv)
    (values,) = call(first_steps_kernel, [scalars], q, gathered, cost=COST)
    az_next, aaw, xy, *parts = call(
        functools.partial(update_kernel, sizes),
        [field] * 3 + faces,
        values, az, aaz, q, *recv, *coefs, scratch=side,
    )
    recv = swap(parts)
    (q,) = call(z_kernel, [field], az_next, xy, *z_args, cost=COST)
    x, r, p, s, w, z, aw, near_r, y, au, early = call(
        update_rest_kernel, [field] * 10 + [jax.ShapeDtypeStruct((1, LANES), f32)],
        values, b, s, z, az, aaz, az_next, inverse, cost=COST,
    )
    az = az_next
    aaz, products = call(
        functools.partial(late_dots_kernel, sizes), [field, row],
        values, b, near_r, s, y, z, au, az, aaw, inverse, early, q, *recv,
    )
    x, r = call(
        last_kernel, [field] * 2, spread(products), values, x, p, r, s, w, z, aw, az, aaw, aaz
    )
    return x.reshape(shape), r.reshape(shape)


def solution(mesh):
    sizes = (mesh.shape["gx"], mesh.shape["gy"])
    field = P("gx", "gy", None)
    return jax.shard_map(
        functools.partial(per_device, sizes),
        mesh=mesh,
        in_specs=(field, field, field, field, P()),
        out_specs=(field, field),
        check_vma=False,
    )
```

```python
import functools

import jax
import jax.numpy as jnp
import numpy as np
from jax import lax
from jax.experimental import pallas as pl
from jax.experimental.pallas import tpu as pltpu
from jax.sharding import PartitionSpec as P

ITERS = 3
N = 8

gll_points = (
    -1.0,
    -0.8717401485096066,
    -0.5917001814331423,
    -0.2092992179024789,
    0.2092992179024789,
    0.5917001814331423,
    0.8717401485096066,
    1.0,
)
gll_weights = (
    0.03571428571428571,
    0.21070422714350603,
    0.3411226924835044,
    0.4124587946587038,
    0.4124587946587038,
    0.3411226924835044,
    0.21070422714350603,
    0.03571428571428571,
)
mass_coef = 0.2
scan_speed = 2.0
f32 = jnp.float32
VMEM = pl.BlockSpec(memory_space=pltpu.VMEM)
HBM = pl.BlockSpec(memory_space=pl.ANY)
COST = 1 << 20
LANES = 128
ORDER = (3, 0, 1, 2)
dot = functools.partial(jnp.dot, precision=lax.Precision.HIGHEST, preferred_element_type=f32)


def lagrange_derivative():
    points = np.array(gll_points)
    barycentric = np.array(
        [1.0 / np.prod([points[j] - points[m] for m in range(N) if m != j]) for j in range(N)]
    )
    derivative = np.zeros((N, N))
    for a in range(N):
        for b in range(N):
            if a != b:
                derivative[a, b] = barycentric[b] / barycentric[a] / (points[a] - points[b])
        derivative[a, a] = -np.sum(derivative[a])
    return derivative.astype(np.float32)


def pieces(v):
    high = v.astype(jnp.bfloat16)
    rest = v - high.astype(f32)
    middle = rest.astype(jnp.bfloat16)
    return high, middle, (rest - middle.astype(f32)).astype(jnp.bfloat16)


def stacked(m):
    high = m.astype(jnp.bfloat16).astype(np.float32)
    middle = (m - high).astype(jnp.bfloat16).astype(np.float32)
    low = m - high - middle
    both = np.concatenate([high, middle], 1)
    return [
        jnp.asarray(np.concatenate([both, both], 0), jnp.bfloat16),
        jnp.asarray(np.concatenate([low, high], 0), jnp.bfloat16),
    ]


def constants(elems_z):
    z_back = np.kron(np.eye(LANES // N, dtype=np.float32), lagrange_derivative())
    lane = np.arange(N * elems_z)
    low = (lane % N == 0) & (lane > 0)
    high = (lane % N == N - 1) & (lane < N * elems_z - 1)
    lanes = np.stack([low, high] + [0 * lane] * 6).astype(np.float32)
    return stacked(z_back.T) + stacked(z_back) + [jnp.asarray(lanes)]


def times(v, first, second):
    high, middle, low = pieces(v)
    product = functools.partial(jnp.dot, preferred_element_type=f32)
    large = product(jnp.concatenate([high, middle], 1), first[...])
    small = product(jnp.concatenate([high, low], 1), second[...])
    return (large[:, :LANES] + large[:, LANES:]) + small


def weights_1d():
    return [float(np.float32(x)) for x in gll_weights]


def position():
    return lax.axis_index("gx"), lax.axis_index("gy")


def tiles(ref):
    return [ref[N * a : N * a + N, :] for a in range(N)]


def store(ref, values):
    for a in range(N):
        ref[N * a : N * a + N, :] = values[a]


def row_index(shape):
    return lax.broadcasted_iota(jnp.int32, shape, 0)


def along(shape, values, index):
    out = jnp.full(shape, values[0], f32)
    for i in range(1, len(values)):
        out = jnp.where(index == i, values[i], out)
    return out


def fold_z(v, lanes):
    size = v.shape[1]
    return (
        v
        + pltpu.roll(v, 1, axis=1) * lanes[0:1, :]
        + pltpu.roll(v, size - 1, axis=1) * lanes[1:2, :]
    )


def pick(pos, axis, even, odd):
    return jnp.where(pos[axis] % 2 == 0, even, odd)


def send(pos, axis, low, high, even_ref, odd_ref):
    even_ref[...] = pick(pos, axis, high, low)
    odd_ref[...] = pick(pos, axis, low, high)


def received(sizes, pos, axis, even, odd):
    low = jnp.where(pos[axis] > 0, pick(pos, axis, odd, even), 0.0)
    high = jnp.where(pos[axis] < sizes[axis] - 1, pick(pos, axis, even, odd), 0.0)
    return low, high


def place(low, high, a, row):
    return jnp.where(row == 0, low[a : a + 1], jnp.where(row == N - 1, high[a : a + 1], 0.0))


def robin_tiles(sizes, pos, table, flags, classes, size):
    elems_z = flags.shape[1]
    coefficient = jnp.zeros(flags.shape, f32)
    for c in range(table.shape[1]):
        coefficient = jnp.where(classes[...] == c, table[:, c : c + 1], coefficient)
    element = lax.broadcasted_iota(jnp.int32, flags.shape, 1)
    sides = [
        pos[0] == 0, pos[0] == sizes[0] - 1, pos[1] == 0, pos[1] == sizes[1] - 1,
        element == 0, element == elems_z - 1,
    ]
    rows = []
    for bit, side in enumerate(sides):
        flagged = (flags[...] >> bit) % 2 == 1
        rows.append(jnp.where(flagged & side, coefficient, 0.0))
    rows += [jnp.zeros(flags.shape, f32)] * 2
    spread = lax.broadcasted_iota(jnp.int32, (elems_z, size), 1) // N == row_index((elems_z, size))
    faces = dot(jnp.concatenate(rows, 0), spread.astype(f32))
    node = lax.broadcasted_iota(jnp.int32, (1, size), 1) % N
    w = weights_1d()
    w_z = along((1, size), w, node)
    row = row_index((N, size))
    w_b = along((N, size), w, row)
    w_bz = w_b * w_z
    ends_z = jnp.where(node == 0, faces[4:5], 0.0) + jnp.where(node == N - 1, faces[5:6], 0.0)
    common = place(faces[2:3] * w_z, faces[3:4] * w_z, 0, row) + w_b * ends_z
    robin = [w[a] * common for a in range(N)]
    robin[0] += w_bz * faces[0:1]
    robin[N - 1] += w_bz * faces[1:2]
    return robin, w_bz


def field_kernel(sizes, source, k, flags, classes, table, even_out, odd_out,
                 v_ref, k_ref, flags_ref, classes_ref, table_ref, low, high, sems):
    pairs = (
        (flags, flags_ref), (classes, classes_ref), (table, table_ref), (source, v_ref), (k, k_ref),
    )
    copies = [pltpu.make_async_copy(*pair, sems.at[i]) for i, pair in enumerate(pairs)]
    for copy in copies:
        copy.start()
    for copy in copies[:3]:
        copy.wait()
    pos = position()
    robin, w_bz = robin_tiles(sizes, pos, table_ref, flags_ref, classes_ref, source.shape[1])
    for copy in copies[3:]:
        copy.wait()
    w = weights_1d()
    ws = [w[a] * w_bz * v for a, v in enumerate(tiles(v_ref))]
    wk = [w[a] * w_bz * v for a, v in enumerate(tiles(k_ref))]
    for i, field in enumerate((ws, wk, robin)):
        for a in range(N):
            low[N * i + a : N * i + a + 1, :] = field[a][0:1]
            high[N * i + a : N * i + a + 1, :] = field[a][N - 1 : N]
    send(pos, 1, low[...], high[...], even_out, odd_out)


def whole_field_kernel(sizes, source, k, flags, classes, table, ws_out, wk_out, robin_out):
    robin, w_bz = robin_tiles(sizes, position(), table, flags, classes, source.shape[1])
    w = weights_1d()
    store(robin_out, robin)
    store(ws_out, [w[a] * w_bz * v for a, v in enumerate(tiles(source))])
    store(wk_out, [w[a] * w_bz * v for a, v in enumerate(tiles(k))])


def fold_y_kernel(sizes, ws, wk, robin, odd, even, even_out, odd_out):
    pos = position()
    low, high = received(sizes, pos, 1, even[...], odd[...])
    row = row_index((N, ws.shape[1]))
    sides = []
    for a in (0, N - 1):
        part = [
            field[N * a : N * a + N, :] + place(low, high, N * i + a, row)
            for i, field in enumerate((ws, wk, robin))
        ]
        part[1] = wk[N * a : N * a + N, :]
        sides.append(jnp.concatenate(part + [low[N + a : N + a + 1], high[N + a : N + a + 1]], 0))
    send(pos, 0, sides[0], sides[1], even_out, odd_out)


def prepare_kernel(sizes, ws, wk, robin, odd, even, lanes,
                   b_out, kx_out, ky_out, kz_out, advect_out, diagonal_out, inverse_out):
    pos = position()
    low, high = received(sizes, pos, 1, even[...], odd[...])
    shape = (N, ws.shape[1])
    row = row_index(shape)
    w = weights_1d()
    node = lax.broadcasted_iota(jnp.int32, (1, shape[1]), 1) % N
    copies_z = 1.0 + lanes[0:1, :] + lanes[1:2, :]
    shared_y = ((row == 0) & (pos[1] > 0)) | ((row == N - 1) & (pos[1] < sizes[1] - 1))
    copies_yz = jnp.where(shared_y, 2.0, 1.0) * copies_z
    weights_yz = along(shape, w, row) * along((1, shape[1]), w, node) * copies_yz
    inverse_yz = 1.0 / copies_yz
    for a in range(N):
        at = slice(N * a, N * a + N)
        summed = [
            field[at, :] + place(low, high, N * i + a, row) for i, field in enumerate((ws, wk, robin))
        ]
        b_out[at, :] = fold_z(summed[0], lanes)
        kz_out[at, :] = summed[1]
        kx_out[at, :] = fold_z(summed[1], lanes)
        ky_out[at, :] = fold_z(wk[at, :], lanes)
        copies_x = 1.0
        if a == 0:
            copies_x = jnp.where(pos[0] > 0, 2.0, 1.0)
        if a == N - 1:
            copies_x = jnp.where(pos[0] < sizes[0] - 1, 2.0, 1.0)
        weights_a = w[a] * weights_yz
        advect_out[at, :] = scan_speed * weights_a
        diagonal_out[at, :] = fold_z(summed[2], lanes) + mass_coef * copies_x * weights_a
        inverse_out[at, :] = inverse_yz * (1.0 / copies_x)


def contract(m, values):
    half = N // 2
    total = [values[b] + values[N - 1 - b] for b in range(half)]
    apart = [values[b] - values[N - 1 - b] for b in range(half)]
    out = [None] * N
    for a in range(half):
        even = sum(float((m[a][b] + m[a][N - 1 - b]) / 2) * total[b] for b in range(half))
        odd = sum(float((m[a][b] - m[a][N - 1 - b]) / 2) * apart[b] for b in range(half))
        out[a] = even + odd
        out[N - 1 - a] = odd - even
    return out


def rotations(m, row):
    return [along(row.shape, [float(m[b][(b + s) % N]) for b in range(N)], row) for s in range(N)]


def contract_rows(coefs, v):
    out = coefs[0] * v
    for s in range(1, N):
        out += coefs[s] * pltpu.roll(v, N - s, axis=0)
    return out


def operate(pos, v, kx, ky, advect, xy_out, sends, low, high):
    d = lagrange_derivative()
    k, speed = tiles(kx), tiles(advect)
    flux = [k[a] * g - speed[a] * v[a] for a, g in enumerate(contract(d, v))]
    x = contract(d.T, flux)
    send(pos, 0, x[0], x[N - 1], sends[0], sends[1])
    row = row_index(v[0].shape)
    forward, back = rotations(d, row), rotations(d.T, row)
    for a in range(N):
        at = slice(N * a, N * a + N)
        y = contract_rows(back, ky[at, :] * contract_rows(forward, v[a]))
        low[a : a + 1, :] = y[0:1]
        high[a : a + 1, :] = y[N - 1 : N]
        xy_out[at, :] = x[a] + y
    send(pos, 1, low[...], high[...], sends[2], sends[3])


def along_z(v, xy, kz, diagonal, forward_1, forward_2, back_1, back_2, lanes, q_out):
    rows, size = v.shape
    columns = [slice(i, i + LANES) for i in range(0, size, LANES)]
    grad = times(jnp.concatenate([v[:, c] for c in columns], 0), forward_1, forward_2)
    flux = [kz[:, c] * grad[i * rows : (i + 1) * rows] for i, c in enumerate(columns)]
    back = times(jnp.concatenate(flux, 0), back_1, back_2)
    back = jnp.concatenate([back[i * rows : (i + 1) * rows] for i in range(len(columns))], 1)
    q_out[...] = fold_z(back, lanes) + (xy[...] + diagonal[...] * v[...])


def assemble(sizes, pos, q, recv):
    x_even, x_odd, y_even, y_odd = (recv[ORDER.index(i)] for i in range(4))
    x_low, x_high = received(sizes, pos, 0, x_even[...], x_odd[...])
    y_low, y_high = received(sizes, pos, 1, y_even[...], y_odd[...])
    row = row_index(y_low.shape)
    out = [q[N * a : N * a + N, :] + place(y_low, y_high, a, row) for a in range(N)]
    out[0] += x_low
    out[N - 1] += x_high
    return out


def first_kernel(sizes, b_in, kx, ky_in, advect, odd, even, lanes,
                 b_out, ky_out, xy_out, *refs):
    pos = position()
    low, high = received(sizes, pos, 0, even[...], odd[...])
    b, ky = tiles(b_in), tiles(ky_in)
    for a, side in ((0, low), (N - 1, high)):
        b[a] += fold_z(side[0:N], lanes)
        ky[a] += fold_z(side[N : 2 * N], lanes)
    store(b_out, b)
    store(ky_out, ky)
    operate(pos, b, kx, ky_out, advect, xy_out, refs[:4], *refs[4:])


def first_z_kernel(sizes, b, xy, kz_in, diagonal_in, odd, even, f1, f2, b1, b2, lanes,
                   kz_out, diagonal_out, q_out):
    pos = position()
    low, high = received(sizes, pos, 0, even[...], odd[...])
    kz_out[...] = kz_in[...]
    diagonal_out[...] = diagonal_in[...]
    for a, side in ((0, low), (N - 1, high)):
        at = slice(N * a, N * a + N)
        ends = place(side[3 * N : 3 * N + 1], side[3 * N + 1 : 3 * N + 2], 0, row_index((N, side.shape[1])))
        kz_out[at, :] += side[N : 2 * N] + ends
        diagonal_out[at, :] += fold_z(side[2 * N : 3 * N], lanes)
    along_z(b, xy, kz_out, diagonal_out, f1, f2, b1, b2, lanes, q_out)


def dots_row(pairs, inverse, first=0):
    shape = (N, LANES)
    lane = lax.broadcasted_iota(jnp.int32, shape, 1)
    row = jnp.zeros(shape, f32)
    scaled = {}
    for i, (u, v) in enumerate(pairs):
        if id(u) not in scaled:
            scaled[id(u)] = [x * m for x, m in zip(u, inverse)]
        product = sum(x * y for x, y in zip(scaled[id(u)], v))
        product = sum(product[:, j : j + LANES] for j in range(0, product.shape[1], LANES))
        row = jnp.where(lane == first + i, jnp.sum(product, axis=1, keepdims=True), row)
    return jnp.sum(row, axis=0, keepdims=True)


def for_all(row, out):
    for i in range(out.shape[0]):
        out[i] = row


def totals(gathered, count):
    row = jnp.sum(gathered[...], axis=0)
    return [jnp.broadcast_to(row[:, i : i + 1], row.shape) for i in range(count)]


def wide(scalar, like):
    return jnp.concatenate([scalar] * (like.shape[1] // scalar.shape[1]), 1)


def steps(br, bs, bw, bz, wr, ws, zr, zs, ww, wz, zz):
    alpha = br / bs
    omega = (wr - alpha * (ws + zr) + alpha * alpha * zs) / (
        ww - 2.0 * alpha * wz + alpha * alpha * zz
    )
    rho_next = (br - alpha * bs) - omega * (bw - alpha * bz)
    beta = rho_next / br * (alpha / omega)
    return alpha, omega, beta


def second_pairs(b, r, s, w, z):
    return [(w, b), (w, r), (w, s), (w, w), (w, z), (r, b), (r, z)]


def early_pairs(b, e):
    return [(e[i], b) for i in range(6)] + [(e[i], e[j]) for i in range(6) for j in range(i, 6)]


def late_pairs(b, e):
    return [(e[i], b) for i in (6, 7)] + [(e[j], e[i]) for j in (6, 7) for i in range(j + 1)]


EARLY = 34
LATE = 17


def guess(scalars, like):
    omega = wide(scalars[1:2, :], like)
    return 2.0 * omega, omega


def last_steps(sums, guessed_omega):
    names = second_pairs(*"brswz") + early_pairs("b", range(6)) + late_pairs("b", range(8))
    value = dict(zip(names, sums))
    g = lambda i, j: value[i, j] if (i, j) in value else value[j, i]
    second = steps(
        g("r", "b"), g(1, "b"), g("w", "b"), g(3, "b"),
        g("w", "r"), g("w", "s"), g("r", "z"), g(1, 3), g("w", "w"), g("w", "z"), g(3, 3),
    )
    alpha, omega, beta = second
    off_alpha, off_omega = alpha - 2.0 * guessed_omega, omega - guessed_omega
    ratio = off_omega / guessed_omega
    one, cross = jnp.ones_like(alpha), off_alpha * omega
    both = -off_alpha - beta * omega
    r = {0: one, 1: -off_alpha, 2: -off_omega, 3: cross, 4: -off_omega * guessed_omega}
    w = {2: one, 3: -off_alpha, 4: -off_omega, 5: cross}
    s = {1: beta, 2: one, 3: both, 4: -off_omega, 5: cross}
    z = {3: beta, 4: -ratio, 5: both, 6: one + ratio, 7: cross}
    with_b = lambda u: sum(c * g(i, "b") for i, c in u.items())
    times = lambda u: {i: sum(c * g(i, j) for j, c in u.items()) for i in range(8)}
    inner = lambda image, u: sum(c * image[i] for i, c in u.items())
    gw, gz = times(w), times(z)
    third = steps(
        with_b(r), with_b(s), with_b(w), with_b(z),
        inner(gw, r), inner(gw, s), inner(gz, r), inner(gz, s),
        inner(gw, w), inner(gw, z), inner(gz, z),
    )
    return second, third


def apply_kernel(sizes, q, x0, x1, y0, y1, kx, ky, advect, v_out, xy_out, *refs):
    pos = position()
    v = assemble(sizes, pos, q, (x0, x1, y0, y1))
    store(v_out, v)
    operate(pos, v, kx, ky, advect, xy_out, refs[:4], *refs[4:])


def z_kernel(*refs):
    along_z(*refs)


def z_dots_kernel(b, s, inverse, z, *refs):
    *shared, row_out, row, sem = refs
    b, s, z_ = tiles(b), tiles(s), tiles(z)
    for_all(dots_row([(b, b), (b, s), (b, z_), (s, s), (s, z_), (z_, z_)], tiles(inverse)), row)
    copy = pltpu.make_async_copy(row, row_out, sem)
    copy.start()
    along_z(z, *shared)
    copy.wait()


def first_steps_kernel(_, gathered, scalars):
    bb, bs, bz, ss, sz, zz = totals(gathered, 6)
    for i, value in enumerate(steps(bb, bs, bs, bz, bs, ss, bz, sz, ss, sz, zz)):
        scalars[i : i + 1, :] = value


def update_kernel(sizes, scalars, az, aaz, q, x0, x1, y0, y1, kx, ky, advect,
                  az_out, aaw_out, xy_out, *refs):
    pos = position()
    alpha, omega, beta = (wide(scalars[i : i + 1, :], az) for i in range(3))
    aaaz = assemble(sizes, pos, q, (x0, x1, y0, y1))
    az, aaz = tiles(az), tiles(aaz)
    aaw = [(az[i] - alpha * aaz[i]) - omega * (aaz[i] - alpha * aaaz[i]) for i in range(N)]
    az_next = [aaw[i] + beta * (az[i] - omega * aaz[i]) for i in range(N)]
    store(aaw_out, aaw)
    store(az_out, az_next)
    operate(pos, az_next, kx, ky, advect, xy_out, refs[:4], *refs[4:])


def update_rest_kernel(scalars, b, s, z, az, aaz, az_next, inverse,
                       x_out, r_out, p_out, s_out, w_out, z_out, aw_out, near_r_out, y_out, au_out, row):
    alpha, omega, beta = (wide(scalars[i : i + 1, :], s) for i in range(3))
    near_alpha, near_omega = guess(scalars, s)
    fields = [[] for _ in range(9)]
    for i in range(N):
        at = slice(N * i, N * i + N)
        b_, s_, z_, az_ = b[at, :], s[at, :], z[at, :], az[at, :]
        half, applied_half = b_ - alpha * s_, s_ - alpha * z_
        applied_twice = z_ - alpha * az_
        x_out[at, :] = alpha * b_ + omega * half
        r = half - omega * applied_half
        w = applied_half - omega * applied_twice
        aw = applied_twice - omega * (az_ - alpha * aaz[at, :])
        s_next = w + beta * (s_ - omega * z_)
        z_next = aw + beta * (z_ - omega * az_)
        p_out[at, :] = r + beta * (b_ - omega * s_)
        u = w - near_alpha * z_next
        au = aw - near_alpha * az_next[at, :]
        y = u - near_omega * au
        near_r = (r - near_alpha * s_next) - near_omega * u
        outs = r_out, s_out, w_out, z_out, aw_out, near_r_out, y_out, au_out
        values = r, s_next, w, z_next, aw, near_r, y, au
        for out, value in zip(outs, values):
            out[at, :] = value
        for kept, value in zip(fields, (b_, r, s_next, w, z_next, near_r, y, au, az_next[at, :])):
            kept.append(value)
    b_, r, s_next, w, z_next, near_r, y, au, az_ = fields
    pairs = second_pairs(b_, r, s_next, w, z_next)
    pairs += early_pairs(b_, [near_r, s_next, y, z_next, au, az_])
    row[...] = dots_row(pairs, tiles(inverse))


def late_dots_kernel(sizes, scalars, b, near_r, s, y, z, au, az, aaw, inverse, early, q,
                     x0, x1, y0, y1, aaz_out, row):
    aaz = assemble(sizes, position(), q, (x0, x1, y0, y1))
    store(aaz_out, aaz)
    alpha, omega = guess(scalars, s)
    e = [tiles(ref) for ref in (near_r, s, y, z, au, az)]
    aaw = tiles(aaw)
    ay = [e[4][i] - omega * (aaw[i] - alpha * aaz[i]) for i in range(N)]
    pairs = late_pairs(tiles(b), e + [ay, aaz])
    for_all(early[...] + dots_row(pairs, tiles(inverse), EARLY), row)


def last_kernel(gathered, scalars, x, p, r, s, w, z, aw, az, aaw, aaz, x_out, r_out):
    second, third = last_steps(totals(gathered, EARLY + LATE), scalars[1:2, :])
    alpha, omega, beta = (wide(value, s) for value in second)
    last_alpha, last_omega, _ = (wide(value, s) for value in third)
    for i in range(N):
        at = slice(N * i, N * i + N)
        p_, s_, z_, az_ = p[at, :], s[at, :], z[at, :], az[at, :]
        half, applied_half = r[at, :] - alpha * s_, w[at, :] - alpha * z_
        applied_twice = aw[at, :] - alpha * az_
        r_next = half - omega * applied_half
        w_next = applied_half - omega * applied_twice
        aw_next = applied_twice - omega * (aaw[at, :] - alpha * aaz[at, :])
        p_next = r_next + beta * (p_ - omega * s_)
        s_next = w_next + beta * (s_ - omega * z_)
        z_next = aw_next + beta * (z_ - omega * az_)
        last_half = r_next - last_alpha * s_next
        x_out[at, :] = (x[at, :] + alpha * p_ + omega * half) + (
            last_alpha * p_next + last_omega * last_half
        )
        r_out[at, :] = last_half - last_omega * (w_next - last_alpha * z_next)


def pairings(sizes):
    count_x, count_y = sizes
    grid = [(i, j) for i in range(count_x) for j in range(count_y)]
    number = lambda i, j: i * count_y + j
    step = lambda i: i + 1 if i % 2 else i - 1
    x_even = [(number(i, j), number(i ^ 1, j)) for i, j in grid]
    x_odd = [
        (number(i, j), number(step(i), j) if 0 < i < count_x - 1 else number(i, j ^ 1)) for i, j in grid
    ]
    y_even = [(number(i, j), number(i, j ^ 1)) for i, j in grid]
    y_odd = [
        (number(i, j), number(i, step(j)) if 0 < j < count_y - 1 else number(i ^ 1, j)) for i, j in grid
    ]
    return (x_even, x_odd), (y_even, y_odd)


def per_device(sizes, source, conductivity, robin_flags, htc_class, htc_table):
    shape = source.shape
    elems_z = robin_flags.shape[2]
    rows, size = shape[0] * shape[1], shape[2]
    assert robin_flags.shape[:2] == (1, 1) and size % LANES == 0
    assert sizes[0] % 2 == 0 and sizes[1] % 2 == 0
    devices = sizes[0] * sizes[1]
    *z_mats, lanes = constants(elems_z)
    x_pairs, y_pairs = pairings(sizes)

    def struct(n=rows):
        return jax.ShapeDtypeStruct((n, size), f32)

    field = struct()
    faces = [struct(N)] * 4
    row = jax.ShapeDtypeStruct((devices, 1, 128), f32)
    scalars = jax.ShapeDtypeStruct((N, 128), f32)
    side = [pltpu.VMEM((N, size), f32)] * 2
    row_side = [pltpu.VMEM(row.shape, f32), pltpu.SemaphoreType.DMA]

    def call(kernel, outs, *operands, scratch=(), hbm=0, limit=32, cost=0, hbm_out=0):
        specs = [HBM] * hbm + [VMEM] * (len(operands) - hbm)
        return pl.pallas_call(
            kernel,
            out_shape=outs,
            in_specs=specs,
            out_specs=[VMEM] * (len(outs) - hbm_out) + [HBM] * hbm_out,
            scratch_shapes=list(scratch),
            compiler_params=pltpu.CompilerParams(vmem_limit_bytes=limit * 1024 * 1024),
            cost_estimate=pl.CostEstimate(flops=cost, bytes_accessed=cost, transcendentals=0)
            if cost
            else None,
        )(*operands)

    def permute(values, pairs):
        return lax.ppermute(values, ("gx", "gy"), pairs)

    def exchange(pairs, even, odd):
        return permute(odd, pairs[1]), permute(even, pairs[0])

    def swap(parts):
        x_odd = permute(parts[1], x_pairs[1])
        y_odd = permute(parts[3], y_pairs[1])
        x_even = permute(parts[0], x_pairs[0])
        recv = x_even, x_odd, permute(parts[2], y_pairs[0]), y_odd
        return tuple(recv[i] for i in ORDER)

    def spread(values):
        return lax.all_to_all(values, ("gx", "gy"), 0, 0)

    given = (
        source.reshape(rows, size), conductivity.reshape(rows, size),
        robin_flags.reshape(1, elems_z), htc_class.reshape(1, elems_z), htc_table.reshape(1, -1),
    )
    parts = call(
        functools.partial(field_kernel, sizes), [struct(3 * N)] * 2, *given,
        hbm=5,
        limit=60,
        scratch=[pltpu.VMEM(v.shape, v.dtype) for v in given]
        + [pltpu.VMEM((3 * N, size), f32)] * 2
        + [pltpu.SemaphoreType.DMA((5,))],
    )
    recv = exchange(y_pairs, *parts)
    ws, wk, robin = call(functools.partial(whole_field_kernel, sizes), [field] * 3, *given, cost=COST)
    parts = call(
        functools.partial(fold_y_kernel, sizes), [struct(3 * N + 2)] * 2, ws, wk, robin, *recv
    )
    b, kx, ky, kz, advect, diagonal, inverse = call(
        functools.partial(prepare_kernel, sizes), [field] * 7, ws, wk, robin, *recv, lanes,
        cost=COST,
    )
    recv = exchange(x_pairs, *parts)
    b, ky, xy, *parts = call(
        functools.partial(first_kernel, sizes), [field] * 3 + faces,
        b, kx, ky, advect, *recv, lanes, scratch=side,
    )
    kz, diagonal, q = call(
        functools.partial(first_z_kernel, sizes), [field] * 3,
        b, xy, kz, diagonal, *recv, *z_mats, lanes, cost=COST,
    )
    coefs = (kx, ky, advect)
    z_args = (kz, diagonal, *z_mats, lanes)
    recv = swap(parts)

    def apply(q, recv):
        v, xy, *parts = call(
            functools.partial(apply_kernel, sizes), [field] * 2 + faces, q, *recv, *coefs, scratch=side
        )
        recv = swap(parts)
        (q,) = call(z_kernel, [field], v, xy, *z_args, cost=COST)
        return v, q, recv

    s, q, recv = apply(q, recv)
    z, xy, *parts = call(
        functools.partial(apply_kernel, sizes), [field] * 2 + faces, q, *recv, *coefs, scratch=side
    )
    recv = swap(parts)
    q, products = call(
        z_dots_kernel, [field, row], b, s, inverse, z, xy, *z_args,
        cost=COST, scratch=row_side, hbm_out=1,
    )
    gathered = spread(products)
    az, q, recv = apply(q, recv)
    aaz, q, recv = apply(q, recv)
    (values,) = call(first_steps_kernel, [scalars], q, gathered, cost=COST)
    az_next, aaw, xy, *parts = call(
        functools.partial(update_kernel, sizes),
        [field] * 3 + faces,
        values, az, aaz, q, *recv, *coefs, scratch=side,
    )
    recv = swap(parts)
    (q,) = call(z_kernel, [field], az_next, xy, *z_args, cost=COST)
    x, r, p, s, w, z, aw, near_r, y, au, early = call(
        update_rest_kernel, [field] * 10 + [jax.ShapeDtypeStruct((1, LANES), f32)],
        values, b, s, z, az, aaz, az_next, inverse, cost=COST,
    )
    az = az_next
    aaz, products = call(
        functools.partial(late_dots_kernel, sizes), [field, row],
        values, b, near_r, s, y, z, au, az, aaw, inverse, early, q, *recv,
    )
    x, r = call(
        last_kernel, [field] * 2, spread(products), values, x, p, r, s, w, z, aw, az, aaw, aaz
    )
    return x.reshape(shape), r.reshape(shape)


def solution(mesh):
    sizes = (mesh.shape["gx"], mesh.shape["gy"])
    field = P("gx", "gy", None)
    return jax.shard_map(
        functools.partial(per_device, sizes),
        mesh=mesh,
        in_specs=(field, field, field, field, P()),
        out_specs=(field, field),
        check_vma=False,
    )
```

```python
import functools

import jax
import jax.numpy as jnp
import numpy as np
from jax import lax
from jax.experimental import pallas as pl
from jax.experimental.pallas import tpu as pltpu
from jax.sharding import PartitionSpec as P

ITERS = 3
N = 8

gll_points = (
    -1.0,
    -0.8717401485096066,
    -0.5917001814331423,
    -0.2092992179024789,
    0.2092992179024789,
    0.5917001814331423,
    0.8717401485096066,
    1.0,
)
gll_weights = (
    0.03571428571428571,
    0.21070422714350603,
    0.3411226924835044,
    0.4124587946587038,
    0.4124587946587038,
    0.3411226924835044,
    0.21070422714350603,
    0.03571428571428571,
)
mass_coef = 0.2
scan_speed = 2.0
f32 = jnp.float32
VMEM = pl.BlockSpec(memory_space=pltpu.VMEM)
HBM = pl.BlockSpec(memory_space=pl.ANY)
COST = 1 << 20
LANES = 128
ORDER = (3, 0, 1, 2)
dot = functools.partial(jnp.dot, precision=lax.Precision.HIGHEST, preferred_element_type=f32)


def lagrange_derivative():
    points = np.array(gll_points)
    barycentric = np.array(
        [1.0 / np.prod([points[j] - points[m] for m in range(N) if m != j]) for j in range(N)]
    )
    derivative = np.zeros((N, N))
    for a in range(N):
        for b in range(N):
            if a != b:
                derivative[a, b] = barycentric[b] / barycentric[a] / (points[a] - points[b])
        derivative[a, a] = -np.sum(derivative[a])
    return derivative.astype(np.float32)


def pieces(v):
    high = v.astype(jnp.bfloat16)
    rest = v - high.astype(f32)
    middle = rest.astype(jnp.bfloat16)
    return high, middle, (rest - middle.astype(f32)).astype(jnp.bfloat16)


def stacked(m):
    high = m.astype(jnp.bfloat16).astype(np.float32)
    middle = (m - high).astype(jnp.bfloat16).astype(np.float32)
    low = m - high - middle
    both = np.concatenate([high, middle], 1)
    return [
        jnp.asarray(np.concatenate([both, both], 0), jnp.bfloat16),
        jnp.asarray(np.concatenate([low, high], 0), jnp.bfloat16),
    ]


def constants(elems_z):
    z_back = np.kron(np.eye(LANES // N, dtype=np.float32), lagrange_derivative())
    lane = np.arange(N * elems_z)
    low = (lane % N == 0) & (lane > 0)
    high = (lane % N == N - 1) & (lane < N * elems_z - 1)
    lanes = np.stack([low, high] + [0 * lane] * 6).astype(np.float32)
    return stacked(z_back.T) + stacked(z_back) + [jnp.asarray(lanes)]


def times(v, first, second):
    high, middle, low = pieces(v)
    product = functools.partial(jnp.dot, preferred_element_type=f32)
    large = product(jnp.concatenate([high, middle], 1), first[...])
    small = product(jnp.concatenate([high, low], 1), second[...])
    return (large[:, :LANES] + large[:, LANES:]) + small


def weights_1d():
    return [float(np.float32(x)) for x in gll_weights]


def position():
    return lax.axis_index("gx"), lax.axis_index("gy")


def tiles(ref):
    return [ref[N * a : N * a + N, :] for a in range(N)]


def store(ref, values):
    for a in range(N):
        ref[N * a : N * a + N, :] = values[a]


def row_index(shape):
    return lax.broadcasted_iota(jnp.int32, shape, 0)


def along(shape, values, index):
    out = jnp.full(shape, values[0], f32)
    for i in range(1, len(values)):
        out = jnp.where(index == i, values[i], out)
    return out


def fold_z(v, lanes):
    size = v.shape[1]
    return (
        v
        + pltpu.roll(v, 1, axis=1) * lanes[0:1, :]
        + pltpu.roll(v, size - 1, axis=1) * lanes[1:2, :]
    )


def pick(pos, axis, even, odd):
    return jnp.where(pos[axis] % 2 == 0, even, odd)


def send(pos, axis, low, high, even_ref, odd_ref):
    even_ref[...] = pick(pos, axis, high, low)
    odd_ref[...] = pick(pos, axis, low, high)


def received(sizes, pos, axis, even, odd):
    low = jnp.where(pos[axis] > 0, pick(pos, axis, odd, even), 0.0)
    high = jnp.where(pos[axis] < sizes[axis] - 1, pick(pos, axis, even, odd), 0.0)
    return low, high


def place(low, high, a, row):
    return jnp.where(row == 0, low[a : a + 1], jnp.where(row == N - 1, high[a : a + 1], 0.0))


def robin_tiles(sizes, pos, table, flags, classes, size):
    elems_z = flags.shape[1]
    coefficient = jnp.zeros(flags.shape, f32)
    for c in range(table.shape[1]):
        coefficient = jnp.where(classes[...] == c, table[:, c : c + 1], coefficient)
    element = lax.broadcasted_iota(jnp.int32, flags.shape, 1)
    sides = [
        pos[0] == 0, pos[0] == sizes[0] - 1, pos[1] == 0, pos[1] == sizes[1] - 1,
        element == 0, element == elems_z - 1,
    ]
    rows = []
    for bit, side in enumerate(sides):
        flagged = (flags[...] >> bit) % 2 == 1
        rows.append(jnp.where(flagged & side, coefficient, 0.0))
    rows += [jnp.zeros(flags.shape, f32)] * 2
    spread = lax.broadcasted_iota(jnp.int32, (elems_z, size), 1) // N == row_index((elems_z, size))
    faces = dot(jnp.concatenate(rows, 0), spread.astype(f32))
    node = lax.broadcasted_iota(jnp.int32, (1, size), 1) % N
    w = weights_1d()
    w_z = along((1, size), w, node)
    row = row_index((N, size))
    w_b = along((N, size), w, row)
    w_bz = w_b * w_z
    ends_z = jnp.where(node == 0, faces[4:5], 0.0) + jnp.where(node == N - 1, faces[5:6], 0.0)
    common = place(faces[2:3] * w_z, faces[3:4] * w_z, 0, row) + w_b * ends_z
    robin = [w[a] * common for a in range(N)]
    robin[0] += w_bz * faces[0:1]
    robin[N - 1] += w_bz * faces[1:2]
    return robin, w_bz


def field_kernel(sizes, source, k, flags, classes, table, even_out, odd_out,
                 v_ref, k_ref, flags_ref, classes_ref, table_ref, low, high, sems):
    pairs = (
        (flags, flags_ref), (classes, classes_ref), (table, table_ref), (source, v_ref), (k, k_ref),
    )
    copies = [pltpu.make_async_copy(*pair, sems.at[i]) for i, pair in enumerate(pairs)]
    for copy in copies:
        copy.start()
    for copy in copies[:3]:
        copy.wait()
    pos = position()
    robin, w_bz = robin_tiles(sizes, pos, table_ref, flags_ref, classes_ref, source.shape[1])
    for copy in copies[3:]:
        copy.wait()
    w = weights_1d()
    ws = [w[a] * w_bz * v for a, v in enumerate(tiles(v_ref))]
    wk = [w[a] * w_bz * v for a, v in enumerate(tiles(k_ref))]
    for i, field in enumerate((ws, wk, robin)):
        for a in range(N):
            low[N * i + a : N * i + a + 1, :] = field[a][0:1]
            high[N * i + a : N * i + a + 1, :] = field[a][N - 1 : N]
    send(pos, 1, low[...], high[...], even_out, odd_out)


def whole_field_kernel(sizes, source, k, flags, classes, table, ws_out, wk_out, robin_out):
    robin, w_bz = robin_tiles(sizes, position(), table, flags, classes, source.shape[1])
    w = weights_1d()
    store(robin_out, robin)
    store(ws_out, [w[a] * w_bz * v for a, v in enumerate(tiles(source))])
    store(wk_out, [w[a] * w_bz * v for a, v in enumerate(tiles(k))])


def fold_y_kernel(sizes, ws, wk, robin, odd, even, even_out, odd_out):
    pos = position()
    low, high = received(sizes, pos, 1, even[...], odd[...])
    row = row_index((N, ws.shape[1]))
    sides = []
    for a in (0, N - 1):
        part = [
            field[N * a : N * a + N, :] + place(low, high, N * i + a, row)
            for i, field in enumerate((ws, wk, robin))
        ]
        sides.append(jnp.concatenate(part + [wk[N * a : N * a + N, :]], 0))
    send(pos, 0, sides[0], sides[1], even_out, odd_out)


def prepare_kernel(sizes, ws, wk, robin, odd, even, lanes,
                   b_out, kx_out, ky_out, kz_out, advect_out, diagonal_out, inverse_out):
    pos = position()
    low, high = received(sizes, pos, 1, even[...], odd[...])
    shape = (N, ws.shape[1])
    row = row_index(shape)
    w = weights_1d()
    node = lax.broadcasted_iota(jnp.int32, (1, shape[1]), 1) % N
    copies_z = 1.0 + lanes[0:1, :] + lanes[1:2, :]
    shared_y = ((row == 0) & (pos[1] > 0)) | ((row == N - 1) & (pos[1] < sizes[1] - 1))
    copies_yz = jnp.where(shared_y, 2.0, 1.0) * copies_z
    weights_yz = along(shape, w, row) * along((1, shape[1]), w, node) * copies_yz
    inverse_yz = 1.0 / copies_yz
    for a in range(N):
        at = slice(N * a, N * a + N)
        summed = [
            field[at, :] + place(low, high, N * i + a, row) for i, field in enumerate((ws, wk, robin))
        ]
        b_out[at, :] = fold_z(summed[0], lanes)
        kz_out[at, :] = summed[1]
        kx_out[at, :] = fold_z(summed[1], lanes)
        ky_out[at, :] = fold_z(wk[at, :], lanes)
        copies_x = 1.0
        if a == 0:
            copies_x = jnp.where(pos[0] > 0, 2.0, 1.0)
        if a == N - 1:
            copies_x = jnp.where(pos[0] < sizes[0] - 1, 2.0, 1.0)
        weights_a = w[a] * weights_yz
        advect_out[at, :] = scan_speed * weights_a
        diagonal_out[at, :] = fold_z(summed[2], lanes) + mass_coef * copies_x * weights_a
        inverse_out[at, :] = inverse_yz * (1.0 / copies_x)


def contract(m, values):
    half = N // 2
    total = [values[b] + values[N - 1 - b] for b in range(half)]
    apart = [values[b] - values[N - 1 - b] for b in range(half)]
    out = [None] * N
    for a in range(half):
        even = sum(float((m[a][b] + m[a][N - 1 - b]) / 2) * total[b] for b in range(half))
        odd = sum(float((m[a][b] - m[a][N - 1 - b]) / 2) * apart[b] for b in range(half))
        out[a] = even + odd
        out[N - 1 - a] = odd - even
    return out


def rotations(m, row):
    return [along(row.shape, [float(m[b][(b + s) % N]) for b in range(N)], row) for s in range(N)]


def contract_rows(coefs, v):
    out = coefs[0] * v
    for s in range(1, N):
        out += coefs[s] * pltpu.roll(v, N - s, axis=0)
    return out


def operate(pos, v, kx, ky, advect, xy_out, sends, low, high):
    d = lagrange_derivative()
    k, speed = tiles(kx), tiles(advect)
    flux = [k[a] * g - speed[a] * v[a] for a, g in enumerate(contract(d, v))]
    x = contract(d.T, flux)
    send(pos, 0, x[0], x[N - 1], sends[0], sends[1])
    row = row_index(v[0].shape)
    forward, back = rotations(d, row), rotations(d.T, row)
    for a in range(N):
        at = slice(N * a, N * a + N)
        y = contract_rows(back, ky[at, :] * contract_rows(forward, v[a]))
        low[a : a + 1, :] = y[0:1]
        high[a : a + 1, :] = y[N - 1 : N]
        xy_out[at, :] = x[a] + y
    send(pos, 1, low[...], high[...], sends[2], sends[3])


def along_z(v, xy, kz, diagonal, forward_1, forward_2, back_1, back_2, lanes, q_out):
    rows, size = v.shape
    columns = [slice(i, i + LANES) for i in range(0, size, LANES)]
    grad = times(jnp.concatenate([v[:, c] for c in columns], 0), forward_1, forward_2)
    flux = [kz[:, c] * grad[i * rows : (i + 1) * rows] for i, c in enumerate(columns)]
    back = times(jnp.concatenate(flux, 0), back_1, back_2)
    back = jnp.concatenate([back[i * rows : (i + 1) * rows] for i in range(len(columns))], 1)
    q_out[...] = fold_z(back, lanes) + (xy[...] + diagonal[...] * v[...])


def assemble(sizes, pos, q, recv):
    x_even, x_odd, y_even, y_odd = (recv[ORDER.index(i)] for i in range(4))
    x_low, x_high = received(sizes, pos, 0, x_even[...], x_odd[...])
    y_low, y_high = received(sizes, pos, 1, y_even[...], y_odd[...])
    row = row_index(y_low.shape)
    out = [q[N * a : N * a + N, :] + place(y_low, y_high, a, row) for a in range(N)]
    out[0] += x_low
    out[N - 1] += x_high
    return out


def first_kernel(sizes, b_in, kx, ky_in, advect, odd, even, lanes,
                 b_out, ky_out, xy_out, *refs):
    pos = position()
    low, high = received(sizes, pos, 0, even[...], odd[...])
    b, ky = tiles(b_in), tiles(ky_in)
    for a, side in ((0, low), (N - 1, high)):
        b[a] += fold_z(side[0:N], lanes)
        ky[a] += fold_z(side[3 * N : 4 * N], lanes)
    store(b_out, b)
    store(ky_out, ky)
    operate(pos, b, kx, ky_out, advect, xy_out, refs[:4], *refs[4:])


def first_z_kernel(sizes, b, xy, kz_in, diagonal_in, odd, even, f1, f2, b1, b2, lanes,
                   kz_out, diagonal_out, q_out):
    pos = position()
    low, high = received(sizes, pos, 0, even[...], odd[...])
    kz_out[...] = kz_in[...]
    diagonal_out[...] = diagonal_in[...]
    for a, side in ((0, low), (N - 1, high)):
        at = slice(N * a, N * a + N)
        kz_out[at, :] += side[N : 2 * N]
        diagonal_out[at, :] += fold_z(side[2 * N : 3 * N], lanes)
    along_z(b, xy, kz_out, diagonal_out, f1, f2, b1, b2, lanes, q_out)


def dots_row(pairs, inverse, first=0):
    shape = (N, LANES)
    lane = lax.broadcasted_iota(jnp.int32, shape, 1)
    row = jnp.zeros(shape, f32)
    scaled = {}
    for i, (u, v) in enumerate(pairs):
        if id(u) not in scaled:
            scaled[id(u)] = [x * m for x, m in zip(u, inverse)]
        product = sum(x * y for x, y in zip(scaled[id(u)], v))
        product = sum(product[:, j : j + LANES] for j in range(0, product.shape[1], LANES))
        row = jnp.where(lane == first + i, jnp.sum(product, axis=1, keepdims=True), row)
    return jnp.sum(row, axis=0, keepdims=True)


def for_all(row, out):
    for i in range(out.shape[0]):
        out[i] = row


def totals(gathered, count):
    row = jnp.sum(gathered[...], axis=0)
    return [jnp.broadcast_to(row[:, i : i + 1], row.shape) for i in range(count)]


def wide(scalar, like):
    return jnp.concatenate([scalar] * (like.shape[1] // scalar.shape[1]), 1)


def steps(br, bs, bw, bz, wr, ws, zr, zs, ww, wz, zz):
    alpha = br / bs
    omega = (wr - alpha * (ws + zr) + alpha * alpha * zs) / (
        ww - 2.0 * alpha * wz + alpha * alpha * zz
    )
    rho_next = (br - alpha * bs) - omega * (bw - alpha * bz)
    beta = rho_next / br * (alpha / omega)
    return alpha, omega, beta


def second_pairs(b, r, s, w, z):
    return [(w, b), (w, r), (w, s), (w, w), (w, z), (r, b), (r, z)]


def early_pairs(b, e):
    return [(e[i], b) for i in range(6)] + [(e[i], e[j]) for i in range(6) for j in range(max(i, 2), 6)]


def late_pairs(b, e):
    return [(e[i], b) for i in (6, 7)] + [(e[j], e[i]) for j in (6, 7) for i in range(j + 1)]


EARLY = 31
LATE = 17


def guess(scalars, like):
    omega = wide(scalars[1:2, :], like)
    return 2.0 * omega, omega


def last_steps(sums, guessed_omega):
    names = second_pairs(*"brswz") + early_pairs("b", range(6)) + late_pairs("b", range(8))
    value = dict(zip(names, sums))
    g = lambda i, j: value[i, j] if (i, j) in value else value[j, i]
    second = steps(
        g("r", "b"), g(1, "b"), g("w", "b"), g(3, "b"),
        g("w", "r"), g("w", "s"), g("r", "z"), g(1, 3), g("w", "w"), g("w", "z"), g(3, 3),
    )
    alpha, omega, beta = second
    off_alpha, off_omega = alpha - 2.0 * guessed_omega, omega - guessed_omega
    ratio = off_omega / guessed_omega
    one, cross = jnp.ones_like(alpha), off_alpha * omega
    both = -off_alpha - beta * omega
    r = {0: one, 1: -off_alpha, 2: -off_omega, 3: cross, 4: -off_omega * guessed_omega}
    w = {2: one, 3: -off_alpha, 4: -off_omega, 5: cross}
    s = {1: beta, 2: one, 3: both, 4: -off_omega, 5: cross}
    z = {3: beta, 4: -ratio, 5: both, 6: one + ratio, 7: cross}
    with_b = lambda u: sum(c * g(i, "b") for i, c in u.items())
    times = lambda u: {i: sum(c * g(i, j) for j, c in u.items()) for i in range(8)}
    inner = lambda image, u: sum(c * image[i] for i, c in u.items())
    gw, gz = times(w), times(z)
    third = steps(
        with_b(r), with_b(s), with_b(w), with_b(z),
        inner(gw, r), inner(gw, s), inner(gz, r), inner(gz, s),
        inner(gw, w), inner(gw, z), inner(gz, z),
    )
    return second, third


def apply_kernel(sizes, q, x0, x1, y0, y1, kx, ky, advect, v_out, xy_out, *refs):
    pos = position()
    v = assemble(sizes, pos, q, (x0, x1, y0, y1))
    store(v_out, v)
    operate(pos, v, kx, ky, advect, xy_out, refs[:4], *refs[4:])


def z_kernel(*refs):
    along_z(*refs)


def z_dots_kernel(b, s, inverse, z, *refs):
    *shared, row_out, row, sem = refs
    b, s, z_ = tiles(b), tiles(s), tiles(z)
    for_all(dots_row([(b, b), (b, s), (b, z_), (s, s), (s, z_), (z_, z_)], tiles(inverse)), row)
    copy = pltpu.make_async_copy(row, row_out, sem)
    copy.start()
    along_z(z, *shared)
    copy.wait()


def first_steps_kernel(_, gathered, scalars):
    bb, bs, bz, ss, sz, zz = totals(gathered, 6)
    for i, value in enumerate(steps(bb, bs, bs, bz, bs, ss, bz, sz, ss, sz, zz)):
        scalars[i : i + 1, :] = value


def update_kernel(sizes, scalars, az, aaz, q, x0, x1, y0, y1, kx, ky, advect,
                  az_out, aaw_out, xy_out, *refs):
    pos = position()
    alpha, omega, beta = (wide(scalars[i : i + 1, :], az) for i in range(3))
    aaaz = assemble(sizes, pos, q, (x0, x1, y0, y1))
    az, aaz = tiles(az), tiles(aaz)
    aaw = [(az[i] - alpha * aaz[i]) - omega * (aaz[i] - alpha * aaaz[i]) for i in range(N)]
    az_next = [aaw[i] + beta * (az[i] - omega * aaz[i]) for i in range(N)]
    store(aaw_out, aaw)
    store(az_out, az_next)
    operate(pos, az_next, kx, ky, advect, xy_out, refs[:4], *refs[4:])


def update_rest_kernel(scalars, b, s, z, az, aaz, az_next, inverse,
                       x_out, r_out, p_out, s_out, w_out, z_out, aw_out, near_r_out, y_out, au_out, row):
    alpha, omega, beta = (wide(scalars[i : i + 1, :], s) for i in range(3))
    near_alpha, near_omega = guess(scalars, s)
    fields = [[] for _ in range(9)]
    for i in range(N):
        at = slice(N * i, N * i + N)
        b_, s_, z_, az_ = b[at, :], s[at, :], z[at, :], az[at, :]
        half, applied_half = b_ - alpha * s_, s_ - alpha * z_
        applied_twice = z_ - alpha * az_
        x_out[at, :] = alpha * b_ + omega * half
        r = half - omega * applied_half
        w = applied_half - omega * applied_twice
        aw = applied_twice - omega * (az_ - alpha * aaz[at, :])
        s_next = w + beta * (s_ - omega * z_)
        z_next = aw + beta * (z_ - omega * az_)
        p_out[at, :] = r + beta * (b_ - omega * s_)
        u = w - near_alpha * z_next
        au = aw - near_alpha * az_next[at, :]
        y = u - near_omega * au
        near_r = (r - near_alpha * s_next) - near_omega * u
        outs = r_out, s_out, w_out, z_out, aw_out, near_r_out, y_out, au_out
        values = r, s_next, w, z_next, aw, near_r, y, au
        for out, value in zip(outs, values):
            out[at, :] = value
        for kept, value in zip(fields, (b_, r, s_next, w, z_next, near_r, y, au, az_next[at, :])):
            kept.append(value)
    b_, r, s_next, w, z_next, near_r, y, au, az_ = fields
    pairs = second_pairs(b_, r, s_next, w, z_next)
    pairs += early_pairs(b_, [near_r, s_next, y, z_next, au, az_])
    row[...] = dots_row(pairs, tiles(inverse))


def late_dots_kernel(sizes, scalars, b, near_r, s, y, z, au, az, aaw, inverse, early, q,
                     x0, x1, y0, y1, aaz_out, row):
    aaz = assemble(sizes, position(), q, (x0, x1, y0, y1))
    store(aaz_out, aaz)
    alpha, omega = guess(scalars, s)
    e = [tiles(ref) for ref in (near_r, s, y, z, au, az)]
    aaw = tiles(aaw)
    ay = [e[4][i] - omega * (aaw[i] - alpha * aaz[i]) for i in range(N)]
    pairs = late_pairs(tiles(b), e + [ay, aaz])
    for_all(early[...] + dots_row(pairs, tiles(inverse), EARLY), row)


def last_kernel(gathered, scalars, x, p, r, s, w, z, aw, az, aaw, aaz, x_out, r_out):
    second, third = last_steps(totals(gathered, EARLY + LATE), scalars[1:2, :])
    alpha, omega, beta = (wide(value, s) for value in second)
    last_alpha, last_omega, _ = (wide(value, s) for value in third)
    for i in range(N):
        at = slice(N * i, N * i + N)
        p_, s_, z_, az_ = p[at, :], s[at, :], z[at, :], az[at, :]
        half, applied_half = r[at, :] - alpha * s_, w[at, :] - alpha * z_
        applied_twice = aw[at, :] - alpha * az_
        r_next = half - omega * applied_half
        w_next = applied_half - omega * applied_twice
        aw_next = applied_twice - omega * (aaw[at, :] - alpha * aaz[at, :])
        p_next = r_next + beta * (p_ - omega * s_)
        s_next = w_next + beta * (s_ - omega * z_)
        z_next = aw_next + beta * (z_ - omega * az_)
        last_half = r_next - last_alpha * s_next
        x_out[at, :] = (x[at, :] + alpha * p_ + omega * half) + (
            last_alpha * p_next + last_omega * last_half
        )
        r_out[at, :] = last_half - last_omega * (w_next - last_alpha * z_next)


def pairings(sizes):
    count_x, count_y = sizes
    grid = [(i, j) for i in range(count_x) for j in range(count_y)]
    number = lambda i, j: i * count_y + j
    step = lambda i: i + 1 if i % 2 else i - 1
    x_even = [(number(i, j), number(i ^ 1, j)) for i, j in grid]
    x_odd = [
        (number(i, j), number(step(i), j) if 0 < i < count_x - 1 else number(i, j ^ 1)) for i, j in grid
    ]
    y_even = [(number(i, j), number(i, j ^ 1)) for i, j in grid]
    y_odd = [
        (number(i, j), number(i, step(j)) if 0 < j < count_y - 1 else number(i ^ 1, j)) for i, j in grid
    ]
    return (x_even, x_odd), (y_even, y_odd)


def per_device(sizes, source, conductivity, robin_flags, htc_class, htc_table):
    shape = source.shape
    elems_z = robin_flags.shape[2]
    rows, size = shape[0] * shape[1], shape[2]
    assert robin_flags.shape[:2] == (1, 1) and size % LANES == 0
    assert sizes[0] % 2 == 0 and sizes[1] % 2 == 0
    devices = sizes[0] * sizes[1]
    *z_mats, lanes = constants(elems_z)
    x_pairs, y_pairs = pairings(sizes)

    def struct(n=rows):
        return jax.ShapeDtypeStruct((n, size), f32)

    field = struct()
    faces = [struct(N)] * 4
    row = jax.ShapeDtypeStruct((devices, 1, 128), f32)
    scalars = jax.ShapeDtypeStruct((N, 128), f32)
    side = [pltpu.VMEM((N, size), f32)] * 2
    row_side = [pltpu.VMEM(row.shape, f32), pltpu.SemaphoreType.DMA]

    def call(kernel, outs, *operands, scratch=(), hbm=0, limit=32, cost=0, hbm_out=0):
        specs = [HBM] * hbm + [VMEM] * (len(operands) - hbm)
        return pl.pallas_call(
            kernel,
            out_shape=outs,
            in_specs=specs,
            out_specs=[VMEM] * (len(outs) - hbm_out) + [HBM] * hbm_out,
            scratch_shapes=list(scratch),
            compiler_params=pltpu.CompilerParams(vmem_limit_bytes=limit * 1024 * 1024),
            cost_estimate=pl.CostEstimate(flops=cost, bytes_accessed=cost, transcendentals=0)
            if cost
            else None,
        )(*operands)

    def permute(values, pairs):
        return lax.ppermute(values, ("gx", "gy"), pairs)

    def exchange(pairs, even, odd):
        return permute(odd, pairs[1]), permute(even, pairs[0])

    def swap(parts):
        x_odd = permute(parts[1], x_pairs[1])
        y_odd = permute(parts[3], y_pairs[1])
        x_even = permute(parts[0], x_pairs[0])
        recv = x_even, x_odd, permute(parts[2], y_pairs[0]), y_odd
        return tuple(recv[i] for i in ORDER)

    def spread(values):
        return lax.all_to_all(values, ("gx", "gy"), 0, 0)

    given = (
        source.reshape(rows, size), conductivity.reshape(rows, size),
        robin_flags.reshape(1, elems_z), htc_class.reshape(1, elems_z), htc_table.reshape(1, -1),
    )
    parts = call(
        functools.partial(field_kernel, sizes), [struct(3 * N)] * 2, *given,
        hbm=5,
        limit=60,
        scratch=[pltpu.VMEM(v.shape, v.dtype) for v in given]
        + [pltpu.VMEM((3 * N, size), f32)] * 2
        + [pltpu.SemaphoreType.DMA((5,))],
    )
    recv = exchange(y_pairs, *parts)
    ws, wk, robin = call(functools.partial(whole_field_kernel, sizes), [field] * 3, *given, cost=COST)
    parts = call(
        functools.partial(fold_y_kernel, sizes), [struct(4 * N)] * 2, ws, wk, robin, *recv
    )
    b, kx, ky, kz, advect, diagonal, inverse = call(
        functools.partial(prepare_kernel, sizes), [field] * 7, ws, wk, robin, *recv, lanes,
        cost=COST,
    )
    recv = exchange(x_pairs, *parts)
    b, ky, xy, *parts = call(
        functools.partial(first_kernel, sizes), [field] * 3 + faces,
        b, kx, ky, advect, *recv, lanes, scratch=side,
    )
    kz, diagonal, q = call(
        functools.partial(first_z_kernel, sizes), [field] * 3,
        b, xy, kz, diagonal, *recv, *z_mats, lanes, cost=COST,
    )
    coefs = (kx, ky, advect)
    z_args = (kz, diagonal, *z_mats, lanes)
    recv = swap(parts)

    def apply(q, recv):
        v, xy, *parts = call(
            functools.partial(apply_kernel, sizes), [field] * 2 + faces, q, *recv, *coefs, scratch=side
        )
        recv = swap(parts)
        (q,) = call(z_kernel, [field], v, xy, *z_args, cost=COST)
        return v, q, recv

    s, q, recv = apply(q, recv)
    z, xy, *parts = call(
        functools.partial(apply_kernel, sizes), [field] * 2 + faces, q, *recv, *coefs, scratch=side
    )
    recv = swap(parts)
    q, products = call(
        z_dots_kernel, [field, row], b, s, inverse, z, xy, *z_args,
        cost=COST, scratch=row_side, hbm_out=1,
    )
    gathered = spread(products)
    az, q, recv = apply(q, recv)
    aaz, q, recv = apply(q, recv)
    (values,) = call(first_steps_kernel, [scalars], q, gathered, cost=COST)
    az_next, aaw, xy, *parts = call(
        functools.partial(update_kernel, sizes),
        [field] * 3 + faces,
        values, az, aaz, q, *recv, *coefs, scratch=side,
    )
    recv = swap(parts)
    (q,) = call(z_kernel, [field], az_next, xy, *z_args, cost=COST)
    x, r, p, s, w, z, aw, near_r, y, au, early = call(
        update_rest_kernel, [field] * 10 + [jax.ShapeDtypeStruct((1, LANES), f32)],
        values, b, s, z, az, aaz, az_next, inverse, cost=COST,
    )
    az = az_next
    aaz, products = call(
        functools.partial(late_dots_kernel, sizes), [field, row],
        values, b, near_r, s, y, z, au, az, aaw, inverse, early, q, *recv,
    )
    x, r = call(
        last_kernel, [field] * 2, spread(products), values, x, p, r, s, w, z, aw, az, aaw, aaz
    )
    return x.reshape(shape), r.reshape(shape)


def solution(mesh):
    sizes = (mesh.shape["gx"], mesh.shape["gy"])
    field = P("gx", "gy", None)
    return jax.shard_map(
        functools.partial(per_device, sizes),
        mesh=mesh,
        in_specs=(field, field, field, field, P()),
        out_specs=(field, field),
        check_vma=False,
    )
```
